32 devices in a mesh: seq: 8 (over y, x, core), head: 4 (over z).
Axes of the slice: x: 2, y: 2, z: 4, core: 2. Of those that a mesh axis runs over, the one named last changes fastest.
Arguments:
- query_rows: bfloat16 [4096, 2048], P(('seq', 'head')), may hold values from -48 to 48
- key_rows: bfloat16 [4096, 1024], P(('seq', 'head')), may hold values from -16 to 16
- saved_value_rows: bfloat16 [4096, 1024], P(('seq', 'head')), may hold values from -6 to 6
- out_grad: bfloat16 [4096, 2048], P(('seq', 'head')), may hold values from -6 to 6
Outputs:
- query_grad: bfloat16 [4096, 2048], P(('seq', 'head'))
- key_grad: bfloat16 [4096, 1024], P(('seq', 'head'))
- value_grad: bfloat16 [4096, 1024], P(('seq', 'head'))
The draws below stay inside these ranges and needn't reach their ends.
All inputs are finite; a program needn't handle non-finite values.
Results may differ from the reference program's by a relative error of at most 0.013.
Values may be sent and summed in bfloat16 or wider, within the bound.
No kernel may reach another device: no remote copies, remote signals or barrier semaphores. Data moves between devices by JAX's collectives and lax.ppermute only.
A program may use at most 64 MiB of HBM per device.

```python
import jax
import jax.numpy as jnp
from jax import lax

HQ = 16
KEY_VALUE_HEADS = 8
HEAD_SIZE = 128
W = 1024
SHARD_POSITIONS = 512
SEQUENCE_TOKENS = 4096
N_SEQ = 8


def draw_query_rows(key, part):
    drawn_result = jnp.clip(jax.random.normal(jax.random.fold_in(key, 202), (SEQUENCE_TOKENS, HQ, HEAD_SIZE), jnp.float32), -6.0, 6.0)
    return drawn_result.reshape(SEQUENCE_TOKENS, HQ * HEAD_SIZE).astype(jnp.bfloat16)


def draw_key_rows(key, part):
    drawn_result = jnp.clip(jax.random.normal(jax.random.fold_in(key, 302), (SEQUENCE_TOKENS, KEY_VALUE_HEADS, HEAD_SIZE), jnp.float32), -6.0, 6.0)
    return drawn_result.reshape(SEQUENCE_TOKENS, KEY_VALUE_HEADS * HEAD_SIZE).astype(jnp.bfloat16)


def steps_of(own_key, shape, cuts, least, largest):
    def one(dim, blocks):
        steps = jax.random.uniform(jax.random.fold_in(jax.random.fold_in(own_key, 6), dim), (blocks,), jnp.float32, least / len(cuts), largest / len(cuts))
        return jnp.repeat(jnp.exp(steps), shape[dim] // blocks).reshape((-1,) + (1,) * (len(shape) - dim - 1))

    loudness = one(*cuts[0])
    for cut in cuts[1:]:
        loudness = loudness * one(*cut)
    return loudness


def scatter_about(stream_key, shape, deviation, limit, pieces=(), held_as=jnp.bfloat16):
    result = deviation * jax.random.normal(stream_key, shape, jnp.float32)
    if pieces:
        result = result * steps_of(stream_key, shape, pieces, -0.22, 0.18)
    return jnp.clip(result, -limit, limit).astype(held_as)


def setup_inputs(seed: int = 0) -> dict:
    streams_of = jax.random.split(jax.random.key(seed), 5)
    return {
        "query_rows": draw_query_rows(jax.random.fold_in(streams_of[4], 71), 0),
        "key_rows": draw_key_rows(jax.random.fold_in(streams_of[4], 71), 0),
        "saved_value_rows": scatter_about(streams_of[2], (SEQUENCE_TOKENS, KEY_VALUE_HEADS * HEAD_SIZE), 1.0, 6.0, ((0, 32),)),
        "out_grad": scatter_about(streams_of[3], (SEQUENCE_TOKENS, HQ * HEAD_SIZE), 1.0, 6.0, ((0, 32),)),
    }


score_scale = 168.0 ** -0.5
masked_value = -1.0e30


def reference(query_rows, key_rows, saved_value_rows, out_grad):
    empty_rows = jnp.zeros((2 * SHARD_POSITIONS, KEY_VALUE_HEADS * HEAD_SIZE), jnp.bfloat16)
    padded_keys = jnp.concatenate([empty_rows, key_rows], 0)
    padded_values = jnp.concatenate([empty_rows, saved_value_rows], 0)

    def block_step(carry, block):
        key_acc, value_acc = carry
        start_offset = (block * SHARD_POSITIONS).astype(jnp.int32)
        query_block = lax.dynamic_slice_in_dim(query_rows, start_offset, SHARD_POSITIONS, 0).reshape(SHARD_POSITIONS, HQ, HEAD_SIZE).astype(jnp.float32)
        grad_block = lax.dynamic_slice_in_dim(out_grad, start_offset, SHARD_POSITIONS, 0).reshape(SHARD_POSITIONS, HQ, HEAD_SIZE).astype(jnp.float32)
        key_tile_block = lax.dynamic_slice_in_dim(padded_keys, start_offset, 3 * SHARD_POSITIONS, 0).reshape(3 * SHARD_POSITIONS, KEY_VALUE_HEADS, HEAD_SIZE)
        value_tile_block = lax.dynamic_slice_in_dim(padded_values, start_offset, 3 * SHARD_POSITIONS, 0).reshape(3 * SHARD_POSITIONS, KEY_VALUE_HEADS, HEAD_SIZE)
        key_heads = jnp.repeat(key_tile_block, 2, axis=1).astype(jnp.float32)
        value_heads = jnp.repeat(value_tile_block, 2, axis=1).astype(jnp.float32)
        query_pos = start_offset + jnp.arange(SHARD_POSITIONS, dtype=jnp.int32)
        key_pos = start_offset - 2 * SHARD_POSITIONS + jnp.arange(3 * SHARD_POSITIONS, dtype=jnp.int32)
        distance = query_pos[:, None] - key_pos[None, :]
        visible = (distance >= 0) & (distance < W) & (key_pos[None, :] >= 0)
        scores = jnp.einsum("qhd,khd->hqk", query_block, key_heads) * score_scale
        scores = jnp.where(visible[None], scores, masked_value)
        row_max = jnp.max(scores, axis=2, keepdims=True)
        weights = jnp.exp(scores - row_max)
        attention = weights / jnp.sum(weights, axis=2, keepdims=True)
        attention_low = attention.astype(jnp.bfloat16)
        prob_grad = jnp.einsum("qhd,khd->hqk", grad_block, value_heads)
        row_delta = jnp.sum(attention * prob_grad, axis=2, keepdims=True)
        score_grad = (score_scale * attention * (prob_grad - row_delta)).astype(jnp.bfloat16)
        query_part = jnp.einsum("hqk,khd->qhd", score_grad.astype(jnp.float32), key_heads)
        query_part = query_part.astype(jnp.bfloat16).reshape(SHARD_POSITIONS, HQ * HEAD_SIZE)
        key_portion = jnp.einsum("hqk,qhd->khd", score_grad.astype(jnp.float32), query_block)
        key_portion = key_portion.reshape(3 * SHARD_POSITIONS, KEY_VALUE_HEADS, 2, HEAD_SIZE).sum(axis=2).reshape(3 * SHARD_POSITIONS, KEY_VALUE_HEADS * HEAD_SIZE)
        value_portion = jnp.einsum("hqk,qhd->khd", attention_low.astype(jnp.float32), grad_block)
        value_portion = value_portion.reshape(3 * SHARD_POSITIONS, KEY_VALUE_HEADS, 2, HEAD_SIZE).sum(axis=2).reshape(3 * SHARD_POSITIONS, KEY_VALUE_HEADS * HEAD_SIZE)
        key_old = lax.dynamic_slice_in_dim(key_acc, start_offset, 3 * SHARD_POSITIONS, 0)
        value_old = lax.dynamic_slice_in_dim(value_acc, start_offset, 3 * SHARD_POSITIONS, 0)
        key_acc = lax.dynamic_update_slice_in_dim(key_acc, key_old + key_portion, start_offset, 0)
        value_acc = lax.dynamic_update_slice_in_dim(value_acc, value_old + value_portion, start_offset, 0)
        return (key_acc, value_acc), query_part

    start_accumulator = jnp.zeros((SEQUENCE_TOKENS + 2 * SHARD_POSITIONS, KEY_VALUE_HEADS * HEAD_SIZE), jnp.float32)
    (key_acc, value_acc), query_parts = lax.scan(block_step, (start_accumulator, start_accumulator), jnp.arange(N_SEQ, dtype=jnp.int32))
    query_grad = query_parts.reshape(SEQUENCE_TOKENS, HQ * HEAD_SIZE)
    key_grad = key_acc[2 * SHARD_POSITIONS:].astype(jnp.bfloat16)
    value_grad = value_acc[2 * SHARD_POSITIONS:].astype(jnp.bfloat16)
    return (query_grad, key_grad, value_grad)
```

```python
import functools

import jax
import jax.numpy as jnp
from jax import lax
from jax.experimental import pallas as pl
from jax.experimental.pallas import tpu as pltpu
from jax.sharding import Mesh
from jax.sharding import PartitionSpec as P

HEAD_SIZE = 128
BLOCK = 128
LOG2_E = 1.4426950408889634

score_scale = 168.0 ** (-0.5)
masked_value = -1e30
contract_last = (((1,), (1,)), ((), ()))
VMEM_SPEC = pl.BlockSpec(memory_space=pltpu.VMEM)
SMEM_SPEC = pl.BlockSpec(memory_space=pltpu.SMEM)
GROUP = ("core", "head")


def pack_kernel(groups, a_ref, b_ref, out_ref):
    width = a_ref.shape[1] // groups
    for g in range(groups):
        out_ref[g, :, :width] = a_ref[:, g * width : (g + 1) * width]
        out_ref[g, :, width:] = b_ref[:, g * width : (g + 1) * width]


def packed(a, b, groups):
    rows, columns = a.shape
    width = columns // groups
    out = pl.pallas_call(
        functools.partial(pack_kernel, groups),
        out_shape=jax.ShapeDtypeStruct((groups, rows, 2 * width), a.dtype),
        in_specs=[VMEM_SPEC] * 2,
        out_specs=VMEM_SPEC,
        compiler_params=pltpu.CompilerParams(vmem_limit_bytes=16 * 2**20),
        cost_estimate=pl.CostEstimate(flops=0, bytes_accessed=8 * rows * columns, transcendentals=0),
    )(a, b)
    return out.reshape(groups * rows, 2 * width)


def unpack_one_kernel(groups, in_ref, out_ref):
    width = in_ref.shape[2]
    for g in range(groups):
        out_ref[:, g * width : (g + 1) * width] = in_ref[g]


def unpacked_one(a, groups):
    rows = a.shape[0] // groups
    width = a.shape[1]
    return pl.pallas_call(
        functools.partial(unpack_one_kernel, groups),
        out_shape=jax.ShapeDtypeStruct((rows, groups * width), a.dtype),
        in_specs=[VMEM_SPEC],
        out_specs=VMEM_SPEC,
        compiler_params=pltpu.CompilerParams(vmem_limit_bytes=16 * 2**20),
        cost_estimate=pl.CostEstimate(flops=0, bytes_accessed=4 * a.size, transcendentals=0),
    )(a.reshape(groups, rows, width))


def unpack_two_kernel(groups, in_ref, first_ref, second_ref):
    width = in_ref.shape[2] // 2
    for g in range(groups):
        first_ref[:, g * width : (g + 1) * width] = in_ref[g, :, :width]
        second_ref[:, g * width : (g + 1) * width] = in_ref[g, :, width:]


def unpacked_two(a, groups):
    rows = a.shape[0] // groups
    width = a.shape[1] // 2
    shape = jax.ShapeDtypeStruct((rows, groups * width), a.dtype)
    return pl.pallas_call(
        functools.partial(unpack_two_kernel, groups),
        out_shape=(shape, shape),
        in_specs=[VMEM_SPEC],
        out_specs=(VMEM_SPEC, VMEM_SPEC),
        compiler_params=pltpu.CompilerParams(vmem_limit_bytes=16 * 2**20),
        cost_estimate=pl.CostEstimate(flops=0, bytes_accessed=4 * a.size, transcendentals=0),
    )(a.reshape(groups, rows, 2 * width))


def attention_kernel(
    first_ref, qd_ref, own_ref, prev_ref, dq_ref, own_grad_ref, prev_grad_ref,
    own_kt_ref, prev_kt_ref, dk_prev_ref, dv_prev_ref,
):
    d = HEAD_SIZE
    positions = qd_ref.shape[0]
    steps = positions // BLOCK
    bias = jnp.where(first_ref[0] == 1, masked_value, 0.0).astype(jnp.float32)
    own_kt_ref[...] = own_ref[:, :d].T
    prev_kt_ref[...] = prev_ref[:, :d].T
    key_row = lax.broadcasted_iota(jnp.int32, (BLOCK, 2 * BLOCK), 0)
    query_row = lax.broadcasted_iota(jnp.int32, (BLOCK, 2 * BLOCK), 1) % BLOCK
    own_seen = key_row <= query_row
    for i in range(steps):
        low, high = i * BLOCK, (i + 1) * BLOCK
        q = jnp.concatenate([qd_ref[low:high, :d], qd_ref[low:high, d : 2 * d]], 0)
        g = jnp.concatenate([qd_ref[low:high, 2 * d : 3 * d], qd_ref[low:high, 3 * d :]], 0)
        dot_t = lambda a, b: lax.dot_general(a, b, contract_last, preferred_element_type=jnp.float32)
        s_own = dot_t(own_ref[:high, :d], q)
        s_prev = dot_t(prev_ref[low:, :d], q) + bias
        p_own = dot_t(own_ref[:high, d:], g)
        p_prev = dot_t(prev_ref[low:, d:], g)
        s_diag = jnp.where(own_seen, s_own[low:], s_prev[:BLOCK])
        p_diag = jnp.where(own_seen, p_own[low:], p_prev[:BLOCK])
        s = [s_own[:low]] * (i > 0) + [s_diag] + [s_prev[BLOCK:]] * (i < steps - 1)
        dp = [p_own[:low]] * (i > 0) + [p_diag] + [p_prev[BLOCK:]] * (i < steps - 1)
        s = jnp.concatenate(s, 0)
        dp = jnp.concatenate(dp, 0)
        top = jnp.max(s, axis=0, keepdims=True)
        w = jnp.exp2((s - top) * (score_scale * LOG2_E))
        inverse = 1.0 / jnp.sum(w, axis=0, keepdims=True)
        delta = jnp.sum(w * dp, axis=0, keepdims=True) * inverse
        attention = w * inverse
        ds = (attention * (dp - delta)).astype(jnp.bfloat16)
        low_attention = attention.astype(jnp.bfloat16)
        zero = jnp.zeros((BLOCK, 2 * BLOCK), jnp.bfloat16)
        ds_diag, at_diag = ds[low:high], low_attention[low:high]
        ds_own = jnp.concatenate([ds[:low]] * (i > 0) + [jnp.where(own_seen, ds_diag, zero)], 0)
        ds_prev = jnp.concatenate([jnp.where(own_seen, zero, ds_diag)] + [ds[high:]] * (i < steps - 1), 0)
        at_own = jnp.concatenate([low_attention[:low]] * (i > 0) + [jnp.where(own_seen, at_diag, zero)], 0)
        at_prev = jnp.concatenate(
            [jnp.where(own_seen, zero, at_diag)] + [low_attention[high:]] * (i < steps - 1), 0
        )
        dot = lambda a, b: jnp.dot(a, b, preferred_element_type=jnp.float32)
        dq_t = dot(own_kt_ref[:, :high], ds_own) + dot(prev_kt_ref[:, low:], ds_prev)
        dq_t = dq_t * score_scale
        dq_ref[low:high, :d] = dq_t[:, :BLOCK].T.astype(jnp.bfloat16)
        dq_ref[low:high, d:] = dq_t[:, BLOCK:].T.astype(jnp.bfloat16)
        dk_own, dk_prev = dot(ds_own, q), dot(ds_prev, q)
        dv_own, dv_prev = dot(at_own, g), dot(at_prev, g)
        if i > 0:
            own_grad_ref[:low, :d] += dk_own[:low]
            own_grad_ref[:low, d:] += dv_own[:low]
            dk_prev_ref[low:] += dk_prev
            dv_prev_ref[low:] += dv_prev
        else:
            dk_prev_ref[...] = dk_prev
            dv_prev_ref[...] = dv_prev
        own_grad_ref[low:high, :d] = dk_own[low:]
        own_grad_ref[low:high, d:] = dv_own[low:]
    own_grad_ref[:, :d] = own_grad_ref[:, :d] * score_scale
    prev_grad_ref[:, :d] = (dk_prev_ref[...] * score_scale).astype(jnp.bfloat16)
    prev_grad_ref[:, d:] = dv_prev_ref[...].astype(jnp.bfloat16)


def attention_backward(first, qd, own, prev):
    positions = qd.shape[0]
    d = HEAD_SIZE
    return pl.pallas_call(
        attention_kernel,
        out_shape=(
            jax.ShapeDtypeStruct((positions, 2 * d), jnp.bfloat16),
            jax.ShapeDtypeStruct((positions, 2 * d), jnp.float32),
            jax.ShapeDtypeStruct((positions, 2 * d), jnp.bfloat16),
        ),
        in_specs=[SMEM_SPEC] + [VMEM_SPEC] * 3,
        out_specs=(VMEM_SPEC,) * 3,
        scratch_shapes=[
            pltpu.VMEM((d, positions), jnp.bfloat16),
            pltpu.VMEM((d, positions), jnp.bfloat16),
            pltpu.VMEM((positions, d), jnp.float32),
            pltpu.VMEM((positions, d), jnp.float32),
        ],
        compiler_params=pltpu.CompilerParams(vmem_limit_bytes=48 * 2**20),
        cost_estimate=pl.CostEstimate(
            flops=20 * positions * positions * d, bytes_accessed=12 * positions * d, transcendentals=2 * positions**2
        ),
    )(first, qd, own, prev)


def add_kernel(own_ref, back_ref, out_ref):
    out_ref[...] = (own_ref[...] + back_ref[...].astype(jnp.float32)).astype(jnp.bfloat16)


def added(own, back):
    return pl.pallas_call(
        add_kernel,
        out_shape=jax.ShapeDtypeStruct(back.shape, back.dtype),
        in_specs=[VMEM_SPEC] * 2,
        out_specs=VMEM_SPEC,
        compiler_params=pltpu.CompilerParams(vmem_limit_bytes=16 * 2**20),
    )(own, back)


def exchanged(value):
    return lax.all_to_all(value, GROUP, split_axis=0, concat_axis=0, tiled=True)


def on_device(groups, query_rows, key_rows, saved_value_rows, out_grad):
    chips = lax.axis_size("chip")
    first = (lax.axis_index("chip") == 0).astype(jnp.int32).reshape(1)
    own = exchanged(packed(key_rows, saved_value_rows, groups))
    prev = lax.ppermute(own, "chip", [(c, c + 1) for c in range(chips - 1)])
    qd = exchanged(packed(query_rows, out_grad, groups))
    dq, own_grad, prev_grad = attention_backward(first, qd, own, prev)
    back = lax.ppermute(prev_grad, "chip", [(c + 1, c) for c in range(chips - 1)])
    query_grad = unpacked_one(exchanged(dq), groups)
    key_grad, value_grad = unpacked_two(exchanged(added(own_grad, back)), groups)
    return query_grad, key_grad, value_grad


def solution(mesh):
    heads = mesh.shape["head"]
    devices = mesh.devices.reshape(-1, 2, heads)
    fine_mesh = Mesh(devices, ("chip", "core", "head"))
    rows = P(("chip", "core", "head"), None)
    return jax.shard_map(
        functools.partial(on_device, 2 * heads),
        mesh=fine_mesh,
        in_specs=(rows,) * 4,
        out_specs=(rows,) * 3,
        check_vma=False,
    )
```

```python
import functools

import jax
import jax.numpy as jnp
from jax import lax
from jax.experimental import pallas as pl
from jax.experimental.pallas import tpu as pltpu
from jax.sharding import Mesh
from jax.sharding import PartitionSpec as P

HEAD_SIZE = 128
BLOCK = 128
LOG2_E = 1.4426950408889634

score_scale = 168.0 ** (-0.5)
masked_value = -1e30
contract_last = (((1,), (1,)), ((), ()))
VMEM_SPEC = pl.BlockSpec(memory_space=pltpu.VMEM)
SMEM_SPEC = pl.BlockSpec(memory_space=pltpu.SMEM)


def call(kernel, out_shape, operands, scratch=(), flops=0, transcendentals=0, vmem=16):
    outs = out_shape if isinstance(out_shape, tuple) else (out_shape,)
    moved = sum(a.size * a.dtype.itemsize for a in operands + outs)
    return pl.pallas_call(
        kernel,
        out_shape=out_shape,
        in_specs=[SMEM_SPEC] + [VMEM_SPEC] * (len(operands) - 1),
        out_specs=jax.tree.map(lambda _: VMEM_SPEC, out_shape),
        scratch_shapes=list(scratch),
        compiler_params=pltpu.CompilerParams(vmem_limit_bytes=vmem * 2**20),
        cost_estimate=pl.CostEstimate(flops=flops, bytes_accessed=moved, transcendentals=transcendentals),
    )(*operands)


def shape_of(dtype, *shape):
    return jax.ShapeDtypeStruct(shape, dtype)


def at(start, size):
    return pl.ds(pl.multiple_of(start, size), size)


def pack_kv_kernel(heads, place_ref, k_ref, v_ref, out_ref):
    core = place_ref[1]
    d = HEAD_SIZE
    for z in range(heads):
        mine, other = at((2 * z + core) * d, d), at((2 * z + 1 - core) * d, d)
        out_ref[z, :, :d] = k_ref[:, mine]
        out_ref[z, :, d : 2 * d] = v_ref[:, mine]
        out_ref[z, :, 2 * d : 3 * d] = k_ref[:, other]
        out_ref[z, :, 3 * d :] = v_ref[:, other]


def pack_qd_kernel(heads, place_ref, q_ref, g_ref, *out_refs):
    core, head = place_ref[1], place_ref[2]
    width = 2 * HEAD_SIZE
    for n, out_ref in enumerate(out_refs):
        step, flip = n // 2, n % 2
        z = lax.rem(head + step, heads)
        c = 1 - core if flip else core
        columns = at((2 * z + c) * width, width)
        out_ref[:, :width] = q_ref[:, columns]
        out_ref[:, width:] = g_ref[:, columns]


def unpack_dq_kernel(heads, place_ref, *refs):
    core, head = place_ref[1], place_ref[2]
    width = 2 * HEAD_SIZE
    in_refs, out_ref = refs[:-1], refs[-1]
    for n, in_ref in enumerate(in_refs):
        step, flip = n // 2, n % 2
        z = lax.rem(head + heads - step, heads)
        c = 1 - core if flip else core
        out_ref[:, at((2 * z + c) * width, width)] = in_ref[...]


def unpack_kv_kernel(heads, place_ref, in_ref, k_ref, v_ref):
    core = place_ref[1]
    d = HEAD_SIZE
    for z in range(heads):
        mine, other = at((2 * z + core) * d, d), at((2 * z + 1 - core) * d, d)
        k_ref[:, mine] = in_ref[z, :, :d]
        v_ref[:, mine] = in_ref[z, :, d : 2 * d]
        k_ref[:, other] = in_ref[z, :, 2 * d : 3 * d]
        v_ref[:, other] = in_ref[z, :, 3 * d :]


def add_kernel(place_ref, own_ref, near_ref, sibling_ref, far_ref, out_ref):
    width = 2 * HEAD_SIZE
    wide = lambda ref: ref[...].astype(jnp.float32)
    out_ref[:, :width] = (own_ref[...] + wide(near_ref)).astype(jnp.bfloat16)
    out_ref[:, width:] = (wide(sibling_ref) + wide(far_ref)).astype(jnp.bfloat16)


def attention_kernel(heads, place_ref, mine_ref, sibling_ref, near_ref, far_ref, *refs):
    d = HEAD_SIZE
    count = 2 * heads
    block_refs, refs = refs[:count], refs[count:]
    dq_refs, refs = refs[:count], refs[count:]
    own_mine_ref, own_other_ref, prev_mine_ref, prev_other_ref = refs[:4]
    qd_ref, own_ref, prev_ref, dq_ref, own_kt_ref, prev_kt_ref, own_grad_ref, prev_grad_ref = refs[4:]
    first, core, head = place_ref[0], place_ref[1], place_ref[2]
    half = heads * BLOCK
    mine, other = at(core * half, half), at((1 - core) * half, half)
    own_ref[mine] = mine_ref[:, : 2 * d]
    own_ref[other] = sibling_ref[...]
    prev_ref[mine] = near_ref[...]
    prev_ref[other] = far_ref[...]

    def rows_of(n, step):
        c = 1 - core if n % 2 else core
        return at((c * heads + lax.rem(head + step, heads)) * BLOCK, BLOCK)

    for n in range(count):
        qd_ref[rows_of(n, heads - n // 2)] = block_refs[n][...]

    bias = jnp.where(first == 1, masked_value, 0.0).astype(jnp.float32)
    own_kt_ref[...] = own_ref[:, :d].T
    prev_kt_ref[...] = prev_ref[:, :d].T
    key_row = lax.broadcasted_iota(jnp.int32, (BLOCK, 2 * BLOCK), 0)
    query_row = lax.broadcasted_iota(jnp.int32, (BLOCK, 2 * BLOCK), 1) % BLOCK
    own_seen = key_row <= query_row
    zero = jnp.zeros((BLOCK, 2 * BLOCK), jnp.bfloat16)
    dot_t = lambda a, b: lax.dot_general(a, b, contract_last, preferred_element_type=jnp.float32)
    dot = lambda a, b: jnp.dot(a, b, preferred_element_type=jnp.float32)
    for i in range(count):
        low, high = i * BLOCK, (i + 1) * BLOCK
        below, above = i > 0, i < count - 1
        q = jnp.concatenate([qd_ref[low:high, :d], qd_ref[low:high, d : 2 * d]], 0)
        g = jnp.concatenate([qd_ref[low:high, 2 * d : 3 * d], qd_ref[low:high, 3 * d :]], 0)
        s_own = dot_t(own_ref[:high, :d], q)
        s_prev = dot_t(prev_ref[low:, :d], q) + bias
        p_own = dot_t(own_ref[:high, d:], g)
        p_prev = dot_t(prev_ref[low:, d:], g)
        s_diag = jnp.where(own_seen, s_own[low:], s_prev[:BLOCK])
        p_diag = jnp.where(own_seen, p_own[low:], p_prev[:BLOCK])
        s = jnp.concatenate([s_own[:low]] * below + [s_diag] + [s_prev[BLOCK:]] * above, 0)
        dp = jnp.concatenate([p_own[:low]] * below + [p_diag] + [p_prev[BLOCK:]] * above, 0)
        top = jnp.max(s, axis=0, keepdims=True)
        w = jnp.exp2((s - top) * (score_scale * LOG2_E))
        inverse = 1.0 / jnp.sum(w, axis=0, keepdims=True)
        delta = jnp.sum(w * dp, axis=0, keepdims=True) * inverse
        attention = w * inverse
        ds = (attention * (dp - delta)).astype(jnp.bfloat16)
        low_attention = attention.astype(jnp.bfloat16)
        split = lambda x: (
            jnp.concatenate([x[:low]] * below + [jnp.where(own_seen, x[low:high], zero)], 0),
            jnp.concatenate([jnp.where(own_seen, zero, x[low:high])] + [x[high:]] * above, 0),
        )
        ds_own, ds_prev = split(ds)
        at_own, at_prev = split(low_attention)
        dq_t = dot(own_kt_ref[:, :high], ds_own) + dot(prev_kt_ref[:, low:], ds_prev)
        dq_t = dq_t * score_scale
        dq_ref[low:high, :d] = dq_t[:, :BLOCK].T.astype(jnp.bfloat16)
        dq_ref[low:high, d:] = dq_t[:, BLOCK:].T.astype(jnp.bfloat16)
        dk_own, dk_prev = dot(ds_own, q), dot(ds_prev, q)
        dv_own, dv_prev = dot(at_own, g), dot(at_prev, g)
        if below:
            own_grad_ref[:low, :d] += dk_own[:low]
            own_grad_ref[:low, d:] += dv_own[:low]
            prev_grad_ref[low:, :d] += dk_prev
            prev_grad_ref[low:, d:] += dv_prev
        else:
            prev_grad_ref[:, :d] = dk_prev
            prev_grad_ref[:, d:] = dv_prev
        own_grad_ref[low:high, :d] = dk_own[low:]
        own_grad_ref[low:high, d:] = dv_own[low:]
    for n in range(count):
        dq_refs[n][...] = dq_ref[rows_of(n, n // 2)]
    for ref, grad_ref, rows in (
        (own_mine_ref, own_grad_ref, mine),
        (own_other_ref, own_grad_ref, other),
        (prev_mine_ref, prev_grad_ref, mine),
        (prev_other_ref, prev_grad_ref, other),
    ):
        ref[:, :d] = (grad_ref[rows, :d] * score_scale).astype(ref.dtype)
        ref[:, d:] = grad_ref[rows, d:].astype(ref.dtype)


def attention_backward(heads, place, mine, sibling, near, far, blocks):
    half, d = heads * BLOCK, HEAD_SIZE
    whole = 2 * half
    low, wide = jnp.bfloat16, jnp.float32
    outs = (shape_of(low, BLOCK, 2 * d),) * (2 * heads) + (
        shape_of(wide, half, 2 * d),
        shape_of(low, half, 2 * d),
        shape_of(low, half, 2 * d),
        shape_of(low, half, 2 * d),
    )
    scratch = (
        pltpu.VMEM((whole, 4 * d), low),
        pltpu.VMEM((whole, 2 * d), low),
        pltpu.VMEM((whole, 2 * d), low),
        pltpu.VMEM((whole, 2 * d), low),
        pltpu.VMEM((d, whole), low),
        pltpu.VMEM((d, whole), low),
        pltpu.VMEM((whole, 2 * d), wide),
        pltpu.VMEM((whole, 2 * d), wide),
    )
    outs = call(
        functools.partial(attention_kernel, heads),
        outs,
        (place, mine, sibling, near, far) + tuple(blocks),
        scratch,
        20 * whole * whole * d,
        2 * whole * whole,
        48,
    )
    return outs[: 2 * heads], outs[2 * heads :]


def moved(value, chips, heads, chip_step, flip, head_step):
    index = lambda chip, core, head: (chip * 2 + core) * heads + head
    pairs = [
        (index(chip, core, head), index(chip + chip_step, core ^ flip, (head + head_step) % heads))
        for chip in range(chips)
        for core in range(2)
        for head in range(heads)
        if 0 <= chip + chip_step < chips
    ]
    return lax.ppermute(value, ("chip", "core", "head"), pairs)


def swapped_heads(value, rows):
    out = lax.all_to_all(value.reshape(-1, value.shape[-1]), "head", split_axis=0, concat_axis=0, tiled=True)
    return out


def on_device(query_rows, key_rows, saved_value_rows, out_grad):
    chips, heads = lax.axis_size("chip"), lax.axis_size("head")
    send = functools.partial(moved, chips=chips, heads=heads)
    rows, d, low = key_rows.shape[0], HEAD_SIZE, jnp.bfloat16
    place = jnp.stack(
        [(lax.axis_index("chip") == 0).astype(jnp.int32), lax.axis_index("core"), lax.axis_index("head")]
    ).astype(jnp.int32)
    kv = call(
        functools.partial(pack_kv_kernel, heads),
        shape_of(low, heads, rows, 4 * d),
        (place, key_rows, saved_value_rows),
    )
    kv = swapped_heads(kv, rows)
    other = kv[:, 2 * d :]
    sibling = send(other, chip_step=0, flip=1, head_step=0)
    near = send(kv[:, : 2 * d], chip_step=1, flip=0, head_step=0)
    far = send(other, chip_step=1, flip=1, head_step=0)
    blocks = call(
        functools.partial(pack_qd_kernel, heads),
        (shape_of(low, rows, 4 * d),) * (2 * heads),
        (place, query_rows, out_grad),
    )
    blocks = [blocks[0]] + [
        send(blocks[n], chip_step=0, flip=n % 2, head_step=n // 2) for n in range(1, 2 * heads)
    ]
    dqs, (own_mine, own_other, prev_mine, prev_other) = attention_backward(
        heads, place, kv, sibling, near, far, blocks
    )
    near_back = send(prev_mine, chip_step=-1, flip=0, head_step=0)
    far_back = send(prev_other, chip_step=-1, flip=1, head_step=0)
    sibling_back = send(own_other, chip_step=0, flip=1, head_step=0)
    dqs = [dqs[0]] + [send(dqs[n], chip_step=0, flip=n % 2, head_step=n // 2) for n in range(1, 2 * heads)]
    query_grad = call(
        functools.partial(unpack_dq_kernel, heads),
        shape_of(low, *query_rows.shape),
        (place,) + tuple(dqs),
    )
    total = call(
        add_kernel,
        shape_of(low, heads * rows, 4 * d),
        (place, own_mine, near_back, sibling_back, far_back),
    )
    total = swapped_heads(total, rows).reshape(heads, rows, 4 * d)
    key_grad, value_grad = call(
        functools.partial(unpack_kv_kernel, heads),
        (shape_of(low, *key_rows.shape),) * 2,
        (place, total),
    )
    return query_grad, key_grad, value_grad


def solution(mesh):
    heads = mesh.shape["head"]
    devices = mesh.devices.reshape(-1, 2, heads)
    fine_mesh = Mesh(devices, ("chip", "core", "head"))
    rows = P(("chip", "core", "head"), None)
    return jax.shard_map(
        on_device,
        mesh=fine_mesh,
        in_specs=(rows,) * 4,
        out_specs=(rows,) * 3,
        check_vma=False,
    )
```

```python
import functools

import jax
import jax.numpy as jnp
from jax import lax
from jax.experimental import pallas as pl
from jax.experimental.pallas import tpu as pltpu
from jax.sharding import Mesh
from jax.sharding import PartitionSpec as P

HEAD_SIZE = 128
BLOCK = 128
LOG2_E = 1.4426950408889634

score_scale = 168.0 ** (-0.5)
masked_value = -1e30
contract_last = (((1,), (1,)), ((), ()))
VMEM_SPEC = pl.BlockSpec(memory_space=pltpu.VMEM)
SMEM_SPEC = pl.BlockSpec(memory_space=pltpu.SMEM)


def call(kernel, out_shape, operands, scratch=(), flops=0, transcendentals=0, vmem=16, spec=VMEM_SPEC):
    outs = out_shape if isinstance(out_shape, tuple) else (out_shape,)
    moved = sum(a.size * a.dtype.itemsize for a in operands + outs)
    return pl.pallas_call(
        kernel,
        out_shape=out_shape,
        in_specs=[SMEM_SPEC] + [spec] * (len(operands) - 1),
        out_specs=jax.tree.map(lambda _: spec, out_shape),
        scratch_shapes=list(scratch),
        compiler_params=pltpu.CompilerParams(vmem_limit_bytes=vmem * 2**20),
        cost_estimate=pl.CostEstimate(flops=flops, bytes_accessed=moved, transcendentals=transcendentals),
    )(*operands)


def copy_call(kernel, copies, out_shape, operands):
    spec = pl.BlockSpec(memory_space=pltpu.HBM)
    return call(kernel, out_shape, operands, (pltpu.SemaphoreType.DMA((copies,)),), spec=spec)


def shape_of(dtype, *shape):
    return jax.ShapeDtypeStruct(shape, dtype)


def at(start, size):
    return pl.ds(pl.multiple_of(start, size), size)


def copied(sems, pairs):
    copies = [pltpu.make_async_copy(src, dst, sems.at[n]) for n, (src, dst) in enumerate(pairs)]
    for copy in copies:
        copy.start()
    for copy in copies:
        copy.wait()


def pack_kv_kernel(heads, place_ref, k_ref, v_ref, out_ref, sems):
    core = place_ref[1]
    d = HEAD_SIZE
    pairs = []
    for z in range(heads):
        for n, g in enumerate((2 * z + core, 2 * z + 1 - core)):
            columns = at(g * d, d)
            pairs.append((k_ref.at[:, columns], out_ref.at[z, :, pl.ds(2 * n * d, d)]))
            pairs.append((v_ref.at[:, columns], out_ref.at[z, :, pl.ds((2 * n + 1) * d, d)]))
    copied(sems, pairs)


def pack_qd_kernel(heads, place_ref, q_ref, g_ref, mine_ref, other_ref, sems):
    core = place_ref[1]
    width = 2 * HEAD_SIZE
    pairs = []
    for ref, c in ((other_ref, 1 - core), (mine_ref, core)):
        for z in range(heads):
            columns = at((2 * z + c) * width, width)
            pairs.append((q_ref.at[:, columns], ref.at[z, :, pl.ds(0, width)]))
            pairs.append((g_ref.at[:, columns], ref.at[z, :, pl.ds(width, width)]))
    copied(sems, pairs)


def merge_rows_kernel(heads, place_ref, mine_ref, other_ref, out_ref):
    core = place_ref[1]
    for z in range(heads):
        out_ref[z, at(core * BLOCK, BLOCK)] = mine_ref[z]
        out_ref[z, at((1 - core) * BLOCK, BLOCK)] = other_ref[z]


def merge_columns_kernel(heads, place_ref, mine_ref, other_ref, out_ref):
    core = place_ref[1]
    width = 2 * HEAD_SIZE
    for z in range(heads):
        out_ref[z, :, at(core * width, width)] = mine_ref[z]
        out_ref[z, :, at((1 - core) * width, width)] = other_ref[z]


def unpack_dq_kernel(heads, place_ref, in_ref, out_ref, sems):
    width = 4 * HEAD_SIZE
    copied(sems, [(in_ref.at[z], out_ref.at[:, pl.ds(z * width, width)]) for z in range(heads)])


def unpack_kv_kernel(heads, place_ref, in_ref, k_ref, v_ref, sems):
    core = place_ref[1]
    d = HEAD_SIZE
    pairs = []
    for z in range(heads):
        for n, g in enumerate((2 * z + core, 2 * z + 1 - core)):
            columns = at(g * d, d)
            pairs.append((in_ref.at[z, :, pl.ds(2 * n * d, d)], k_ref.at[:, columns]))
            pairs.append((in_ref.at[z, :, pl.ds((2 * n + 1) * d, d)], v_ref.at[:, columns]))
    copied(sems, pairs)


def add_kernel(place_ref, own_ref, near_ref, sibling_ref, far_ref, out_ref):
    width = 2 * HEAD_SIZE
    wide = lambda ref: ref[...].astype(jnp.float32)
    out_ref[:, :width] = (own_ref[...] + wide(near_ref)).astype(jnp.bfloat16)
    out_ref[:, width:] = (wide(sibling_ref) + wide(far_ref)).astype(jnp.bfloat16)


def attention_kernel(heads, place_ref, mine_ref, sibling_ref, near_ref, far_ref, blocks_ref, *refs):
    d = HEAD_SIZE
    count = 2 * heads
    dq_mine_ref, dq_other_ref, own_mine_ref, own_other_ref, prev_mine_ref, prev_other_ref = refs[:6]
    qd_ref, own_ref, prev_ref, dq_ref, own_kt_ref, prev_kt_ref, own_grad_ref, prev_grad_ref = refs[6:]
    first, core = place_ref[0], place_ref[1]
    half = heads * BLOCK
    mine, other = at(core * half, half), at((1 - core) * half, half)
    own_ref[mine] = mine_ref[:, : 2 * d]
    own_ref[other] = sibling_ref[...]
    prev_ref[mine] = near_ref[...]
    prev_ref[other] = far_ref[...]
    for c in range(2):
        for z in range(heads):
            start = (c * heads + z) * BLOCK
            qd_ref[start : start + BLOCK] = blocks_ref[z, c * BLOCK : (c + 1) * BLOCK]
    bias = jnp.where(first == 1, masked_value, 0.0).astype(jnp.float32)
    own_kt_ref[...] = own_ref[:, :d].T
    prev_kt_ref[...] = prev_ref[:, :d].T
    key_row = lax.broadcasted_iota(jnp.int32, (BLOCK, 2 * BLOCK), 0)
    query_row = lax.broadcasted_iota(jnp.int32, (BLOCK, 2 * BLOCK), 1) % BLOCK
    own_seen = key_row <= query_row
    zero = jnp.zeros((BLOCK, 2 * BLOCK), jnp.bfloat16)
    dot_t = lambda a, b: lax.dot_general(a, b, contract_last, preferred_element_type=jnp.float32)
    dot = lambda a, b: jnp.dot(a, b, preferred_element_type=jnp.float32)
    for i in range(count):
        low, high = i * BLOCK, (i + 1) * BLOCK
        below, above = i > 0, i < count - 1
        q = jnp.concatenate([qd_ref[low:high, :d], qd_ref[low:high, d : 2 * d]], 0)
        g = jnp.concatenate([qd_ref[low:high, 2 * d : 3 * d], qd_ref[low:high, 3 * d :]], 0)
        s_own = dot_t(own_ref[:high, :d], q)
        s_prev = dot_t(prev_ref[low:, :d], q) + bias
        p_own = dot_t(own_ref[:high, d:], g)
        p_prev = dot_t(prev_ref[low:, d:], g)
        s_diag = jnp.where(own_seen, s_own[low:], s_prev[:BLOCK])
        p_diag = jnp.where(own_seen, p_own[low:], p_prev[:BLOCK])
        s = jnp.concatenate([s_own[:low]] * below + [s_diag] + [s_prev[BLOCK:]] * above, 0)
        dp = jnp.concatenate([p_own[:low]] * below + [p_diag] + [p_prev[BLOCK:]] * above, 0)
        top = jnp.max(s, axis=0, keepdims=True)
        w = jnp.exp2((s - top) * (score_scale * LOG2_E))
        inverse = 1.0 / jnp.sum(w, axis=0, keepdims=True)
        delta = jnp.sum(w * dp, axis=0, keepdims=True) * inverse
        attention = w * inverse
        ds = (attention * (dp - delta)).astype(jnp.bfloat16)
        low_attention = attention.astype(jnp.bfloat16)
        split = lambda x: (
            jnp.concatenate([x[:low]] * below + [jnp.where(own_seen, x[low:high], zero)], 0),
            jnp.concatenate([jnp.where(own_seen, zero, x[low:high])] + [x[high:]] * above, 0),
        )
        ds_own, ds_prev = split(ds)
        at_own, at_prev = split(low_attention)
        dq_t = dot(own_kt_ref[:, :high], ds_own) + dot(prev_kt_ref[:, low:], ds_prev)
        dq_t = dq_t * score_scale
        dq_ref[low:high, :d] = dq_t[:, :BLOCK].T.astype(jnp.bfloat16)
        dq_ref[low:high, d:] = dq_t[:, BLOCK:].T.astype(jnp.bfloat16)
        dk_own, dk_prev = dot(ds_own, q), dot(ds_prev, q)
        dv_own, dv_prev = dot(at_own, g), dot(at_prev, g)
        if below:
            own_grad_ref[:low, :d] += dk_own[:low]
            own_grad_ref[:low, d:] += dv_own[:low]
            prev_grad_ref[low:, :d] += dk_prev
            prev_grad_ref[low:, d:] += dv_prev
        else:
            prev_grad_ref[:, :d] = dk_prev
            prev_grad_ref[:, d:] = dv_prev
        own_grad_ref[low:high, :d] = dk_own[low:]
        own_grad_ref[low:high, d:] = dv_own[low:]
    dq_mine_ref[...] = dq_ref[mine]
    dq_other_ref[...] = dq_ref[other]
    for ref, grad_ref, rows in (
        (own_mine_ref, own_grad_ref, mine),
        (own_other_ref, own_grad_ref, other),
        (prev_mine_ref, prev_grad_ref, mine),
        (prev_other_ref, prev_grad_ref, other),
    ):
        ref[:, :d] = (grad_ref[rows, :d] * score_scale).astype(ref.dtype)
        ref[:, d:] = grad_ref[rows, d:].astype(ref.dtype)


def attention_backward(heads, place, mine, sibling, near, far, blocks):
    half, d = heads * BLOCK, HEAD_SIZE
    whole = 2 * half
    low, wide = jnp.bfloat16, jnp.float32
    part = shape_of(low, half, 2 * d)
    outs = (part, part, shape_of(wide, half, 2 * d), part, part, part)
    scratch = (
        pltpu.VMEM((whole, 4 * d), low),
        pltpu.VMEM((whole, 2 * d), low),
        pltpu.VMEM((whole, 2 * d), low),
        pltpu.VMEM((whole, 2 * d), low),
        pltpu.VMEM((d, whole), low),
        pltpu.VMEM((d, whole), low),
        pltpu.VMEM((whole, 2 * d), wide),
        pltpu.VMEM((whole, 2 * d), wide),
    )
    return call(
        functools.partial(attention_kernel, heads),
        outs,
        (place, mine, sibling, near, far, blocks),
        scratch,
        20 * whole * whole * d,
        2 * whole * whole,
        48,
    )


def moved(value, chips, heads, chip_step, flip, head_step):
    index = lambda chip, core, head: (chip * 2 + core) * heads + head
    pairs = [
        (index(chip, core, head), index(chip + chip_step, core ^ flip, (head + head_step) % heads))
        for chip in range(chips)
        for core in range(2)
        for head in range(heads)
        if 0 <= chip + chip_step < chips
    ]
    return lax.ppermute(value, ("chip", "core", "head"), pairs)


def swapped_heads(value):
    return lax.all_to_all(value, "head", split_axis=0, concat_axis=0, tiled=True)


def on_device(query_rows, key_rows, saved_value_rows, out_grad):
    chips, heads = lax.axis_size("chip"), lax.axis_size("head")
    send = functools.partial(moved, chips=chips, heads=heads, head_step=0)
    rows, d, low = key_rows.shape[0], HEAD_SIZE, jnp.bfloat16
    bind = lambda kernel: functools.partial(kernel, heads)
    place = jnp.stack(
        [(lax.axis_index("chip") == 0).astype(jnp.int32), lax.axis_index("core"), lax.axis_index("head")]
    ).astype(jnp.int32)
    kv = copy_call(
        bind(pack_kv_kernel), 4 * heads, shape_of(low, heads, rows, 4 * d), (place, key_rows, saved_value_rows)
    )
    qd_mine, qd_other = copy_call(
        bind(pack_qd_kernel), 4 * heads, (shape_of(low, heads, rows, 4 * d),) * 2, (place, query_rows, out_grad)
    )
    kv = swapped_heads(kv).reshape(heads * rows, 4 * d)
    qd_other = send(qd_other, chip_step=0, flip=1)
    qd = call(bind(merge_rows_kernel), shape_of(low, heads, 2 * rows, 4 * d), (place, qd_mine, qd_other))
    other = kv[:, 2 * d :]
    near = send(kv[:, : 2 * d], chip_step=1, flip=0)
    far = send(other, chip_step=1, flip=1)
    sibling = send(other, chip_step=0, flip=1)
    blocks = swapped_heads(qd)
    dq_mine, dq_other, own_mine, own_other, prev_mine, prev_other = attention_backward(
        heads, place, kv, sibling, near, far, blocks
    )
    near_back = send(prev_mine, chip_step=-1, flip=0)
    far_back = send(prev_other, chip_step=-1, flip=1)
    sibling_back = send(own_other, chip_step=0, flip=1)
    dq_other = send(dq_other, chip_step=0, flip=1)
    split = lambda x: x.reshape(heads, rows, -1)
    dq = call(
        bind(merge_columns_kernel), shape_of(low, heads, rows, 4 * d), (place, split(dq_mine), split(dq_other))
    )
    query_grad = copy_call(
        bind(unpack_dq_kernel), heads, shape_of(low, *query_rows.shape), (place, swapped_heads(dq))
    )
    total = call(
        add_kernel,
        shape_of(low, heads * rows, 4 * d),
        (place, own_mine, near_back, sibling_back, far_back),
    )
    total = swapped_heads(split(total))
    key_grad, value_grad = copy_call(
        bind(unpack_kv_kernel), 4 * heads, (shape_of(low, *key_rows.shape),) * 2, (place, total)
    )
    return query_grad, key_grad, value_grad


def solution(mesh):
    heads = mesh.shape["head"]
    devices = mesh.devices.reshape(-1, 2, heads)
    fine_mesh = Mesh(devices, ("chip", "core", "head"))
    rows = P(("chip", "core", "head"), None)
    return jax.shard_map(
        on_device,
        mesh=fine_mesh,
        in_specs=(rows,) * 4,
        out_specs=(rows,) * 3,
        check_vma=False,
    )
```

```python
import functools

import jax
import jax.numpy as jnp
from jax import lax
from jax.experimental import pallas as pl
from jax.experimental.pallas import tpu as pltpu
from jax.sharding import Mesh
from jax.sharding import PartitionSpec as P

HEAD_SIZE = 128
BLOCK = 128
LOG2_E = 1.4426950408889634

score_scale = 168.0 ** (-0.5)
masked_value = -1e30
contract_last = (((1,), (1,)), ((), ()))
VMEM_SPEC = pl.BlockSpec(memory_space=pltpu.VMEM)
SMEM_SPEC = pl.BlockSpec(memory_space=pltpu.SMEM)


def call(kernel, out_shape, operands, scratch=(), flops=0, transcendentals=0, vmem=16, spec=VMEM_SPEC):
    outs = out_shape if isinstance(out_shape, tuple) else (out_shape,)
    moved = sum(a.size * a.dtype.itemsize for a in operands + outs)
    return pl.pallas_call(
        kernel,
        out_shape=out_shape,
        in_specs=[SMEM_SPEC] + [spec] * (len(operands) - 1),
        out_specs=jax.tree.map(lambda _: spec, out_shape),
        scratch_shapes=list(scratch),
        compiler_params=pltpu.CompilerParams(vmem_limit_bytes=vmem * 2**20),
        cost_estimate=pl.CostEstimate(flops=flops, bytes_accessed=moved, transcendentals=transcendentals),
    )(*operands)


def copy_call(kernel, copies, out_shape, operands):
    spec = pl.BlockSpec(memory_space=pltpu.HBM)
    return call(kernel, out_shape, operands, (pltpu.SemaphoreType.DMA((copies,)),), spec=spec)


def shape_of(dtype, *shape):
    return jax.ShapeDtypeStruct(shape, dtype)


def at(start, size):
    return pl.ds(pl.multiple_of(start, size), size)


def copied(sems, pairs):
    copies = [pltpu.make_async_copy(src, dst, sems.at[n]) for n, (src, dst) in enumerate(pairs)]
    for copy in copies:
        copy.start()
    for copy in copies:
        copy.wait()


def onward(place_ref, heads, k):
    return lax.rem(place_ref[2] + k, heads)


def source(place_ref, heads, k):
    return lax.rem(place_ref[2] + heads - k, heads)


def pack_kv_kernel(heads, place_ref, k_ref, v_ref, *refs):
    out_refs, sems = refs[:-1], refs[-1]
    core = place_ref[1]
    d = HEAD_SIZE
    pairs = []
    for k, out_ref in enumerate(out_refs):
        z = onward(place_ref, heads, k)
        for n, g in enumerate((2 * z + core, 2 * z + 1 - core)):
            columns = at(g * d, d)
            pairs.append((k_ref.at[:, columns], out_ref.at[:, pl.ds(2 * n * d, d)]))
            pairs.append((v_ref.at[:, columns], out_ref.at[:, pl.ds((2 * n + 1) * d, d)]))
    copied(sems, pairs)


def pack_qd_kernel(heads, place_ref, q_ref, g_ref, mine_ref, other_ref, sems):
    core = place_ref[1]
    width = 2 * HEAD_SIZE
    pairs = []
    for ref, c in ((other_ref, 1 - core), (mine_ref, core)):
        for k in range(heads):
            columns = at((2 * onward(place_ref, heads, k) + c) * width, width)
            pairs.append((q_ref.at[:, columns], ref.at[k, :, pl.ds(0, width)]))
            pairs.append((g_ref.at[:, columns], ref.at[k, :, pl.ds(width, width)]))
    copied(sems, pairs)


def gather_kv_kernel(heads, place_ref, *refs):
    in_refs, (mine_ref, other_ref) = refs[:heads], refs[heads:]
    width = 2 * HEAD_SIZE
    for k, in_ref in enumerate(in_refs):
        rows = at(source(place_ref, heads, k) * BLOCK, BLOCK)
        mine_ref[rows] = in_ref[:, :width]
        other_ref[rows] = in_ref[:, width:]


def join_kernel(place_ref, mine_ref, sibling_ref, out_ref):
    core = place_ref[1]
    half = mine_ref.shape[0]
    out_ref[at(core * half, half)] = mine_ref[...]
    out_ref[at((1 - core) * half, half)] = sibling_ref[...]


def merge_rows_kernel(heads, place_ref, mine_ref, other_ref, after_ref, *out_refs):
    core = place_ref[1]
    for k, out_ref in enumerate(out_refs):
        out_ref[at(core * BLOCK, BLOCK)] = mine_ref[k]
        out_ref[at((1 - core) * BLOCK, BLOCK)] = other_ref[k]


def merge_columns_kernel(heads, place_ref, mine_ref, other_ref, *out_refs):
    core = place_ref[1]
    width = 2 * HEAD_SIZE
    for k, out_ref in enumerate(out_refs):
        rows = slice(k * BLOCK, (k + 1) * BLOCK)
        out_ref[:, at(core * width, width)] = mine_ref[rows]
        out_ref[:, at((1 - core) * width, width)] = other_ref[rows]


def unpack_dq_kernel(heads, place_ref, *refs):
    in_refs, out_ref, sems = refs[:-2], refs[-2], refs[-1]
    width = 4 * HEAD_SIZE
    pairs = []
    for k, in_ref in enumerate(in_refs):
        pairs.append((in_ref, out_ref.at[:, at(source(place_ref, heads, k) * width, width)]))
    copied(sems, pairs)


def unpack_kv_kernel(heads, place_ref, *refs):
    in_refs, k_ref, v_ref, sems = refs[:-3], refs[-3], refs[-2], refs[-1]
    core = place_ref[1]
    d = HEAD_SIZE
    pairs = []
    for k, in_ref in enumerate(in_refs):
        z = source(place_ref, heads, k)
        for n, g in enumerate((2 * z + core, 2 * z + 1 - core)):
            columns = at(g * d, d)
            pairs.append((in_ref.at[:, pl.ds(2 * n * d, d)], k_ref.at[:, columns]))
            pairs.append((in_ref.at[:, pl.ds((2 * n + 1) * d, d)], v_ref.at[:, columns]))
    copied(sems, pairs)


def add_kernel(heads, place_ref, own_ref, near_ref, sibling_ref, far_ref, *out_refs):
    width = 2 * HEAD_SIZE
    for k, out_ref in enumerate(out_refs):
        rows = at(onward(place_ref, heads, k) * BLOCK, BLOCK)
        wide = lambda ref: ref[rows].astype(jnp.float32)
        out_ref[:, :width] = (own_ref[rows] + wide(near_ref)).astype(jnp.bfloat16)
        out_ref[:, width:] = (wide(sibling_ref) + wide(far_ref)).astype(jnp.bfloat16)


def attention_kernel(heads, place_ref, own_ref, prev_ref, *refs):
    d = HEAD_SIZE
    count = 2 * heads
    block_refs, refs = refs[:heads], refs[heads:]
    dq_mine_ref, dq_other_ref, own_mine_ref, own_other_ref, prev_mine_ref, prev_other_ref = refs[:6]
    qd_ref, dq_ref, own_kt_ref, prev_kt_ref, own_grad_ref, prev_grad_ref = refs[6:]
    first, core = place_ref[0], place_ref[1]
    half = heads * BLOCK
    mine, other = at(core * half, half), at((1 - core) * half, half)
    for k, block_ref in enumerate(block_refs):
        for c in range(2):
            rows = at((c * heads + source(place_ref, heads, k)) * BLOCK, BLOCK)
            qd_ref[rows] = block_ref[c * BLOCK : (c + 1) * BLOCK]
    bias = jnp.where(first == 1, masked_value, 0.0).astype(jnp.float32)
    own_kt_ref[...] = own_ref[:, :d].T
    prev_kt_ref[...] = prev_ref[:, :d].T
    key_row = lax.broadcasted_iota(jnp.int32, (BLOCK, 2 * BLOCK), 0)
    query_row = lax.broadcasted_iota(jnp.int32, (BLOCK, 2 * BLOCK), 1) % BLOCK
    own_seen = key_row <= query_row
    zero = jnp.zeros((BLOCK, 2 * BLOCK), jnp.bfloat16)
    dot_t = lambda a, b: lax.dot_general(a, b, contract_last, preferred_element_type=jnp.float32)
    dot = lambda a, b: jnp.dot(a, b, preferred_element_type=jnp.float32)
    for i in range(count):
        low, high = i * BLOCK, (i + 1) * BLOCK
        below, above = i > 0, i < count - 1
        q = jnp.concatenate([qd_ref[low:high, :d], qd_ref[low:high, d : 2 * d]], 0)
        g = jnp.concatenate([qd_ref[low:high, 2 * d : 3 * d], qd_ref[low:high, 3 * d :]], 0)
        s_own = dot_t(own_ref[:high, :d], q)
        s_prev = dot_t(prev_ref[low:, :d], q) + bias
        p_own = dot_t(own_ref[:high, d:], g)
        p_prev = dot_t(prev_ref[low:, d:], g)
        s_diag = jnp.where(own_seen, s_own[low:], s_prev[:BLOCK])
        p_diag = jnp.where(own_seen, p_own[low:], p_prev[:BLOCK])
        s = jnp.concatenate([s_own[:low]] * below + [s_diag] + [s_prev[BLOCK:]] * above, 0)
        dp = jnp.concatenate([p_own[:low]] * below + [p_diag] + [p_prev[BLOCK:]] * above, 0)
        top = jnp.max(s, axis=0, keepdims=True)
        w = jnp.exp2((s - top) * (score_scale * LOG2_E))
        inverse = 1.0 / jnp.sum(w, axis=0, keepdims=True)
        delta = jnp.sum(w * dp, axis=0, keepdims=True) * inverse
        attention = w * inverse
        ds = (attention * (dp - delta)).astype(jnp.bfloat16)
        low_attention = attention.astype(jnp.bfloat16)
        split = lambda x: (
            jnp.concatenate([x[:low]] * below + [jnp.where(own_seen, x[low:high], zero)], 0),
            jnp.concatenate([jnp.where(own_seen, zero, x[low:high])] + [x[high:]] * above, 0),
        )
        ds_own, ds_prev = split(ds)
        at_own, at_prev = split(low_attention)
        dq_t = dot(own_kt_ref[:, :high], ds_own) + dot(prev_kt_ref[:, low:], ds_prev)
        dq_t = dq_t * score_scale
        dq_ref[low:high, :d] = dq_t[:, :BLOCK].T.astype(jnp.bfloat16)
        dq_ref[low:high, d:] = dq_t[:, BLOCK:].T.astype(jnp.bfloat16)
        dk_own, dk_prev = dot(ds_own, q), dot(ds_prev, q)
        dv_own, dv_prev = dot(at_own, g), dot(at_prev, g)
        if below:
            own_grad_ref[:low, :d] += dk_own[:low]
            own_grad_ref[:low, d:] += dv_own[:low]
            prev_grad_ref[low:, :d] += dk_prev
            prev_grad_ref[low:, d:] += dv_prev
        else:
            prev_grad_ref[:, :d] = dk_prev
            prev_grad_ref[:, d:] = dv_prev
        own_grad_ref[low:high, :d] = dk_own[low:]
        own_grad_ref[low:high, d:] = dv_own[low:]
    for ref, c in ((dq_mine_ref, core), (dq_other_ref, 1 - core)):
        for k in range(heads):
            rows = at((c * heads + onward(place_ref, heads, k)) * BLOCK, BLOCK)
            ref[k * BLOCK : (k + 1) * BLOCK] = dq_ref[rows]
    for ref, grad_ref, rows in (
        (own_mine_ref, own_grad_ref, mine),
        (own_other_ref, own_grad_ref, other),
        (prev_mine_ref, prev_grad_ref, mine),
        (prev_other_ref, prev_grad_ref, other),
    ):
        ref[:, :d] = (grad_ref[rows, :d] * score_scale).astype(ref.dtype)
        ref[:, d:] = grad_ref[rows, d:].astype(ref.dtype)


def attention_backward(heads, place, own, prev, blocks):
    half, d = heads * BLOCK, HEAD_SIZE
    whole = 2 * half
    low, wide = jnp.bfloat16, jnp.float32
    part = shape_of(low, half, 2 * d)
    outs = (part, part, shape_of(wide, half, 2 * d), part, part, part)
    scratch = (
        pltpu.VMEM((whole, 4 * d), low),
        pltpu.VMEM((whole, 2 * d), low),
        pltpu.VMEM((d, whole), low),
        pltpu.VMEM((d, whole), low),
        pltpu.VMEM((whole, 2 * d), wide),
        pltpu.VMEM((whole, 2 * d), wide),
    )
    return call(
        functools.partial(attention_kernel, heads),
        outs,
        (place, own, prev) + tuple(blocks),
        scratch,
        20 * whole * whole * d,
        2 * whole * whole,
        32,
    )


def moved(value, chips, heads, chip_step, flip, head_step):
    index = lambda chip, core, head: (chip * 2 + core) * heads + head
    pairs = [
        (index(chip, core, head), index(chip + chip_step, core ^ flip, (head + head_step) % heads))
        for chip in range(chips)
        for core in range(2)
        for head in range(heads)
        if 0 <= chip + chip_step < chips
    ]
    return lax.ppermute(value, ("chip", "core", "head"), pairs)


def on_device(query_rows, key_rows, saved_value_rows, out_grad):
    chips, heads = lax.axis_size("chip"), lax.axis_size("head")
    send = functools.partial(moved, chips=chips, heads=heads)
    rows, d, low = key_rows.shape[0], HEAD_SIZE, jnp.bfloat16
    bind = lambda kernel: functools.partial(kernel, heads)
    place = jnp.stack(
        [(lax.axis_index("chip") == 0).astype(jnp.int32), lax.axis_index("core"), lax.axis_index("head")]
    ).astype(jnp.int32)

    def spread(parts):
        order = sorted(range(1, heads), key=lambda k: -min(k, heads - k))
        out = {k: send(parts[k], chip_step=0, flip=0, head_step=k) for k in order}
        return (parts[0],) + tuple(out[k] for k in range(1, heads))

    across = functools.partial(send, head_step=0)
    slab = shape_of(low, rows, 4 * d)
    kvs = spread(copy_call(bind(pack_kv_kernel), 4 * heads, (slab,) * heads, (place, key_rows, saved_value_rows)))
    qd_mine, qd_other = copy_call(
        bind(pack_qd_kernel), 4 * heads, (shape_of(low, heads, rows, 4 * d),) * 2, (place, query_rows, out_grad)
    )
    qd_other = across(qd_other, chip_step=0, flip=1)
    mine, other = call(bind(gather_kv_kernel), (shape_of(low, heads * rows, 2 * d),) * 2, (place,) + kvs)
    sibling = across(other, chip_step=0, flip=1)
    blocks = spread(
        call(
            bind(merge_rows_kernel),
            (shape_of(low, 2 * rows, 4 * d),) * heads,
            (place, qd_mine, qd_other, mine[:8]),
        )
    )
    own = call(join_kernel, shape_of(low, 2 * heads * rows, 2 * d), (place, mine, sibling))
    prev = across(own, chip_step=1, flip=0)
    dq_mine, dq_other, own_mine, own_other, prev_mine, prev_other = attention_backward(
        heads, place, own, prev, blocks
    )
    near_back = across(prev_mine, chip_step=-1, flip=0)
    far_back = across(prev_other, chip_step=-1, flip=1)
    sibling_back = across(own_other, chip_step=0, flip=1)
    dq_other = across(dq_other, chip_step=0, flip=1)
    dqs = spread(call(bind(merge_columns_kernel), (slab,) * heads, (place, dq_mine, dq_other)))
    query_grad = copy_call(bind(unpack_dq_kernel), heads, shape_of(low, *query_rows.shape), (place,) + dqs)
    totals = spread(
        call(bind(add_kernel), (slab,) * heads, (place, own_mine, near_back, sibling_back, far_back))
    )
    key_grad, value_grad = copy_call(
        bind(unpack_kv_kernel), 4 * heads, (shape_of(low, *key_rows.shape),) * 2, (place,) + totals
    )
    return query_grad, key_grad, value_grad


def solution(mesh):
    heads = mesh.shape["head"]
    devices = mesh.devices.reshape(-1, 2, heads)
    fine_mesh = Mesh(devices, ("chip", "core", "head"))
    rows = P(("chip", "core", "head"), None)
    return jax.shard_map(
        on_device,
        mesh=fine_mesh,
        in_specs=(rows,) * 4,
        out_specs=(rows,) * 3,
        check_vma=False,
    )
```

```python
import functools

import jax
import jax.numpy as jnp
from jax import lax
from jax.experimental import pallas as pl
from jax.experimental.pallas import tpu as pltpu
from jax.sharding import Mesh
from jax.sharding import PartitionSpec as P

HEAD_SIZE = 128
BLOCK = 128
LOG2_E = 1.4426950408889634

score_scale = 168.0 ** (-0.5)
masked_value = -1e30
contract_last = (((1,), (1,)), ((), ()))
VMEM_SPEC = pl.BlockSpec(memory_space=pltpu.VMEM)
ANY_SPEC = pl.BlockSpec(memory_space=pl.ANY)
SMEM_SPEC = pl.BlockSpec(memory_space=pltpu.SMEM)


def call(kernel, out_shape, operands, scratch=(), flops=0, transcendentals=0, vmem=16, spec=VMEM_SPEC, out_spec=VMEM_SPEC):
    return pl.pallas_call(
        kernel,
        out_shape=out_shape,
        in_specs=[SMEM_SPEC] + [spec] * (len(operands) - 1),
        out_specs=jax.tree.map(lambda _: out_spec, out_shape),
        scratch_shapes=list(scratch),
        compiler_params=pltpu.CompilerParams(vmem_limit_bytes=vmem * 2**20),
        cost_estimate=pl.CostEstimate(flops=flops, bytes_accessed=1, transcendentals=transcendentals),
    )(*operands)


def copy_call(kernel, copies, out_shape, operands):
    return call(kernel, out_shape, operands, (pltpu.SemaphoreType.DMA((copies,)),), spec=ANY_SPEC, out_spec=ANY_SPEC)


def shape_of(dtype, *shape):
    return jax.ShapeDtypeStruct(shape, dtype)


def at(start, size):
    return pl.ds(pl.multiple_of(start, size), size)


def copied(sems, pairs):
    copies = [pltpu.make_async_copy(src, dst, sems.at[n]) for n, (src, dst) in enumerate(pairs)]
    for copy in copies:
        copy.start()
    for copy in copies:
        copy.wait()


def onward(place_ref, heads, k):
    return lax.rem(place_ref[2] + k, heads)


def source(place_ref, heads, k):
    return lax.rem(place_ref[2] + heads - k, heads)


def pack_kv_kernel(heads, place_ref, k_ref, v_ref, *refs):
    out_refs, sems = refs[:-1], refs[-1]
    core = place_ref[1]
    d = HEAD_SIZE
    pairs = []
    for k, out_ref in enumerate(out_refs):
        z = onward(place_ref, heads, k)
        for n, g in enumerate((2 * z + core, 2 * z + 1 - core)):
            columns = at(g * d, d)
            pairs.append((k_ref.at[:, columns], out_ref.at[:, pl.ds(2 * n * d, d)]))
            pairs.append((v_ref.at[:, columns], out_ref.at[:, pl.ds((2 * n + 1) * d, d)]))
    copied(sems, pairs)


def pack_qd_kernel(heads, place_ref, q_ref, g_ref, mine_ref, other_ref, sems):
    core = place_ref[1]
    width = 2 * HEAD_SIZE
    pairs = []
    for ref, c in ((other_ref, 1 - core), (mine_ref, core)):
        for k in range(heads):
            columns = at((2 * onward(place_ref, heads, k) + c) * width, width)
            pairs.append((q_ref.at[:, columns], ref.at[k, :, pl.ds(0, width)]))
            pairs.append((g_ref.at[:, columns], ref.at[k, :, pl.ds(width, width)]))
    copied(sems, pairs)


def gather_kv_kernel(heads, place_ref, *refs):
    in_refs, (mine_ref, other_ref) = refs[:heads], refs[heads:]
    width = 2 * HEAD_SIZE
    for k, in_ref in enumerate(in_refs):
        rows = at(source(place_ref, heads, k) * BLOCK, BLOCK)
        mine_ref[rows] = in_ref[:, :width]
        other_ref[rows] = in_ref[:, width:]


def join_kernel(place_ref, mine_ref, sibling_ref, out_ref):
    core = place_ref[1]
    half = mine_ref.shape[0]
    out_ref[at(core * half, half)] = mine_ref[...]
    out_ref[at((1 - core) * half, half)] = sibling_ref[...]


def merge_rows_kernel(heads, place_ref, mine_ref, other_ref, after_ref, *out_refs):
    core = place_ref[1]
    for k, out_ref in enumerate(out_refs):
        out_ref[at(core * BLOCK, BLOCK)] = mine_ref[k]
        out_ref[at((1 - core) * BLOCK, BLOCK)] = other_ref[k]


def merge_columns_kernel(heads, place_ref, mine_ref, other_ref, *out_refs):
    core = place_ref[1]
    width = 2 * HEAD_SIZE
    for k, out_ref in enumerate(out_refs):
        rows = slice(k * BLOCK, (k + 1) * BLOCK)
        out_ref[:, at(core * width, width)] = mine_ref[rows]
        out_ref[:, at((1 - core) * width, width)] = other_ref[rows]


def unpack_dq_kernel(heads, place_ref, *refs):
    in_refs, out_ref, sems = refs[:-2], refs[-2], refs[-1]
    width = 4 * HEAD_SIZE
    pairs = []
    for k, in_ref in enumerate(in_refs):
        pairs.append((in_ref, out_ref.at[:, at(source(place_ref, heads, k) * width, width)]))
    copied(sems, pairs)


def unpack_kv_kernel(heads, place_ref, *refs):
    in_refs, k_ref, v_ref, sems = refs[:-3], refs[-3], refs[-2], refs[-1]
    core = place_ref[1]
    d = HEAD_SIZE
    pairs = []
    for k, in_ref in enumerate(in_refs):
        z = source(place_ref, heads, k)
        for n, g in enumerate((2 * z + core, 2 * z + 1 - core)):
            columns = at(g * d, d)
            pairs.append((in_ref.at[:, pl.ds(2 * n * d, d)], k_ref.at[:, columns]))
            pairs.append((in_ref.at[:, pl.ds((2 * n + 1) * d, d)], v_ref.at[:, columns]))
    copied(sems, pairs)


def add_kernel(heads, place_ref, own_ref, near_ref, sibling_ref, far_ref, *out_refs):
    width = 2 * HEAD_SIZE
    for k, out_ref in enumerate(out_refs):
        rows = at(onward(place_ref, heads, k) * BLOCK, BLOCK)
        wide = lambda ref: ref[rows].astype(jnp.float32)
        out_ref[:, :width] = (own_ref[rows] + wide(near_ref)).astype(jnp.bfloat16)
        out_ref[:, width:] = (wide(sibling_ref) + wide(far_ref)).astype(jnp.bfloat16)


def attention_kernel(heads, place_ref, own_ref, near_ref, far_ref, *refs):
    d = HEAD_SIZE
    count = 2 * heads
    block_refs, refs = refs[:heads], refs[heads:]
    dq_mine_ref, dq_other_ref, own_mine_ref, own_other_ref, prev_mine_ref, prev_other_ref = refs[:6]
    qd_ref, prev_ref, dq_ref, own_kt_ref, prev_kt_ref, own_grad_ref, prev_grad_ref = refs[6:]
    first, core = place_ref[0], place_ref[1]
    half = heads * BLOCK
    mine, other = at(core * half, half), at((1 - core) * half, half)
    prev_ref[mine] = near_ref[...]
    prev_ref[other] = far_ref[...]
    for k, block_ref in enumerate(block_refs):
        for c in range(2):
            rows = at((c * heads + source(place_ref, heads, k)) * BLOCK, BLOCK)
            qd_ref[rows] = block_ref[c * BLOCK : (c + 1) * BLOCK]
    bias = jnp.where(first == 1, masked_value, 0.0).astype(jnp.float32)
    own_kt_ref[...] = own_ref[:, :d].T
    prev_kt_ref[...] = prev_ref[:, :d].T
    key_row = lax.broadcasted_iota(jnp.int32, (BLOCK, 2 * BLOCK), 0)
    query_row = lax.broadcasted_iota(jnp.int32, (BLOCK, 2 * BLOCK), 1) % BLOCK
    own_seen = key_row <= query_row
    zero = jnp.zeros((BLOCK, 2 * BLOCK), jnp.bfloat16)
    dot_t = lambda a, b: lax.dot_general(a, b, contract_last, preferred_element_type=jnp.float32)
    dot = lambda a, b: jnp.dot(a, b, preferred_element_type=jnp.float32)
    for i in range(count):
        low, high = i * BLOCK, (i + 1) * BLOCK
        below, above = i > 0, i < count - 1
        q = jnp.concatenate([qd_ref[low:high, :d], qd_ref[low:high, d : 2 * d]], 0)
        g = jnp.concatenate([qd_ref[low:high, 2 * d : 3 * d], qd_ref[low:high, 3 * d :]], 0)
        s_own = dot_t(own_ref[:high, :d], q)
        s_prev = dot_t(prev_ref[low:, :d], q) + bias
        p_own = dot_t(own_ref[:high, d:], g)
        p_prev = dot_t(prev_ref[low:, d:], g)
        s_diag = jnp.where(own_seen, s_own[low:], s_prev[:BLOCK])
        p_diag = jnp.where(own_seen, p_own[low:], p_prev[:BLOCK])
        s = jnp.concatenate([s_own[:low]] * below + [s_diag] + [s_prev[BLOCK:]] * above, 0)
        dp = jnp.concatenate([p_own[:low]] * below + [p_diag] + [p_prev[BLOCK:]] * above, 0)
        top = jnp.max(s, axis=0, keepdims=True)
        w = jnp.exp2((s - top) * (score_scale * LOG2_E))
        inverse = 1.0 / jnp.sum(w, axis=0, keepdims=True)
        delta = jnp.sum(w * dp, axis=0, keepdims=True) * inverse
        attention = w * inverse
        ds = (attention * (dp - delta)).astype(jnp.bfloat16)
        low_attention = attention.astype(jnp.bfloat16)
        split = lambda x: (
            jnp.concatenate([x[:low]] * below + [jnp.where(own_seen, x[low:high], zero)], 0),
            jnp.concatenate([jnp.where(own_seen, zero, x[low:high])] + [x[high:]] * above, 0),
        )
        ds_own, ds_prev = split(ds)
        at_own, at_prev = split(low_attention)
        dq_t = dot(own_kt_ref[:, :high], ds_own) + dot(prev_kt_ref[:, low:], ds_prev)
        dq_t = dq_t * score_scale
        dq_ref[low:high, :d] = dq_t[:, :BLOCK].T.astype(jnp.bfloat16)
        dq_ref[low:high, d:] = dq_t[:, BLOCK:].T.astype(jnp.bfloat16)
        dk_own, dk_prev = dot(ds_own, q), dot(ds_prev, q)
        dv_own, dv_prev = dot(at_own, g), dot(at_prev, g)
        if below:
            own_grad_ref[:low, :d] += dk_own[:low]
            own_grad_ref[:low, d:] += dv_own[:low]
            prev_grad_ref[low:, :d] += dk_prev
            prev_grad_ref[low:, d:] += dv_prev
        else:
            prev_grad_ref[:, :d] = dk_prev
            prev_grad_ref[:, d:] = dv_prev
        own_grad_ref[low:high, :d] = dk_own[low:]
        own_grad_ref[low:high, d:] = dv_own[low:]
    for ref, c in ((dq_mine_ref, core), (dq_other_ref, 1 - core)):
        for k in range(heads):
            rows = at((c * heads + onward(place_ref, heads, k)) * BLOCK, BLOCK)
            ref[k * BLOCK : (k + 1) * BLOCK] = dq_ref[rows]
    for ref, grad_ref, rows in (
        (own_mine_ref, own_grad_ref, mine),
        (own_other_ref, own_grad_ref, other),
        (prev_mine_ref, prev_grad_ref, mine),
        (prev_other_ref, prev_grad_ref, other),
    ):
        ref[:, :d] = (grad_ref[rows, :d] * score_scale).astype(ref.dtype)
        ref[:, d:] = grad_ref[rows, d:].astype(ref.dtype)


def attention_backward(heads, place, own, near, far, blocks):
    half, d = heads * BLOCK, HEAD_SIZE
    whole = 2 * half
    low, wide = jnp.bfloat16, jnp.float32
    part = shape_of(low, half, 2 * d)
    outs = (part, part, shape_of(wide, half, 2 * d), part, part, part)
    scratch = (
        pltpu.VMEM((whole, 4 * d), low),
        pltpu.VMEM((whole, 2 * d), low),
        pltpu.VMEM((whole, 2 * d), low),
        pltpu.VMEM((d, whole), low),
        pltpu.VMEM((d, whole), low),
        pltpu.VMEM((whole, 2 * d), wide),
        pltpu.VMEM((whole, 2 * d), wide),
    )
    return call(
        functools.partial(attention_kernel, heads),
        outs,
        (place, own, near, far) + tuple(blocks),
        scratch,
        20 * whole * whole * d,
        2 * whole * whole,
        32,
    )


def moved(value, chips, heads, chip_step, flip, head_step):
    index = lambda chip, core, head: (chip * 2 + core) * heads + head
    pairs = [
        (index(chip, core, head), index(chip + chip_step, core ^ flip, (head + head_step) % heads))
        for chip in range(chips)
        for core in range(2)
        for head in range(heads)
        if 0 <= chip + chip_step < chips
    ]
    return lax.ppermute(value, ("chip", "core", "head"), pairs)


def on_device(query_rows, key_rows, saved_value_rows, out_grad):
    chips, heads = lax.axis_size("chip"), lax.axis_size("head")
    send = functools.partial(moved, chips=chips, heads=heads)
    rows, d, low = key_rows.shape[0], HEAD_SIZE, jnp.bfloat16
    bind = lambda kernel: functools.partial(kernel, heads)
    place = jnp.stack(
        [(lax.axis_index("chip") == 0).astype(jnp.int32), lax.axis_index("core"), lax.axis_index("head")]
    ).astype(jnp.int32)

    def spread(parts):
        order = sorted(range(1, heads), key=lambda k: -min(k, heads - k))
        out = {k: send(parts[k], chip_step=0, flip=0, head_step=k) for k in order}
        return (parts[0],) + tuple(out[k] for k in range(1, heads))

    across = functools.partial(send, head_step=0)
    slab = shape_of(low, rows, 4 * d)
    kvs = copy_call(bind(pack_kv_kernel), 4 * heads, (slab,) * heads, (place, key_rows, saved_value_rows))
    qd_mine, qd_other = copy_call(
        bind(pack_qd_kernel),
        4 * heads,
        (shape_of(low, heads, rows, 4 * d),) * 2,
        (place, query_rows, out_grad),
    )
    kvs = spread(kvs)
    qd_other = across(qd_other, chip_step=0, flip=1)
    mine, other = call(bind(gather_kv_kernel), (shape_of(low, heads * rows, 2 * d),) * 2, (place,) + kvs)
    near = across(mine, chip_step=1, flip=0)
    far = across(other, chip_step=1, flip=1)
    blocks = call(
        bind(merge_rows_kernel),
        (shape_of(low, 2 * rows, 4 * d),) * heads,
        (place, qd_mine, qd_other, kvs[-1][:8]),
    )
    blocks = spread(blocks)
    sibling = across(other, chip_step=0, flip=1)
    own = call(join_kernel, shape_of(low, 2 * heads * rows, 2 * d), (place, mine, sibling))
    dq_mine, dq_other, own_mine, own_other, prev_mine, prev_other = attention_backward(
        heads, place, own, near, far, blocks
    )
    near_back = across(prev_mine, chip_step=-1, flip=0)
    far_back = across(prev_other, chip_step=-1, flip=1)
    sibling_back = across(own_other, chip_step=0, flip=1)
    dq_other = across(dq_other, chip_step=0, flip=1)
    dqs = spread(call(bind(merge_columns_kernel), (slab,) * heads, (place, dq_mine, dq_other)))
    query_grad = copy_call(bind(unpack_dq_kernel), heads, shape_of(low, *query_rows.shape), (place,) + dqs)
    totals = spread(
        call(bind(add_kernel), (slab,) * heads, (place, own_mine, near_back, sibling_back, far_back))
    )
    key_grad, value_grad = copy_call(
        bind(unpack_kv_kernel), 4 * heads, (shape_of(low, *key_rows.shape),) * 2, (place,) + totals
    )
    return query_grad, key_grad, value_grad


def solution(mesh):
    heads = mesh.shape["head"]
    devices = mesh.devices.reshape(-1, 2, heads)
    fine_mesh = Mesh(devices, ("chip", "core", "head"))
    rows = P(("chip", "core", "head"), None)
    return jax.shard_map(
        on_device,
        mesh=fine_mesh,
        in_specs=(rows,) * 4,
        out_specs=(rows,) * 3,
        check_vma=False,
    )
```

```python
import functools

import jax
import jax.numpy as jnp
from jax import lax
from jax.experimental import pallas as pl
from jax.experimental.pallas import tpu as pltpu
from jax.sharding import Mesh
from jax.sharding import PartitionSpec as P

HEAD_SIZE = 128
BLOCK = 128
LOG2_E = 1.4426950408889634

score_scale = 168.0 ** (-0.5)
masked_value = -1e30
contract_last = (((1,), (1,)), ((), ()))
VMEM_SPEC = pl.BlockSpec(memory_space=pltpu.VMEM)
ANY_SPEC = pl.BlockSpec(memory_space=pl.ANY)
SMEM_SPEC = pl.BlockSpec(memory_space=pltpu.SMEM)


def call(kernel, out_shape, operands, scratch=(), flops=0, transcendentals=0, vmem=16, spec=VMEM_SPEC, out_spec=VMEM_SPEC):
    outs = out_shape if isinstance(out_shape, tuple) else (out_shape,)
    moved = sum(a.size * a.dtype.itemsize for a in operands + outs)
    return pl.pallas_call(
        kernel,
        out_shape=out_shape,
        in_specs=[SMEM_SPEC] + [spec] * (len(operands) - 1),
        out_specs=jax.tree.map(lambda _: out_spec, out_shape),
        scratch_shapes=list(scratch),
        compiler_params=pltpu.CompilerParams(vmem_limit_bytes=vmem * 2**20),
        cost_estimate=pl.CostEstimate(flops=flops, bytes_accessed=moved, transcendentals=transcendentals),
    )(*operands)


def copy_call(kernel, copies, out_shape, operands):
    return call(kernel, out_shape, operands, (pltpu.SemaphoreType.DMA((copies,)),), spec=ANY_SPEC, out_spec=ANY_SPEC)


def shape_of(dtype, *shape):
    return jax.ShapeDtypeStruct(shape, dtype)


def at(start, size):
    return pl.ds(pl.multiple_of(start, size), size)


def copied(sems, pairs):
    copies = [pltpu.make_async_copy(src, dst, sems.at[n]) for n, (src, dst) in enumerate(pairs)]
    for copy in copies:
        copy.start()
    for copy in copies:
        copy.wait()


def onward(place_ref, heads, k):
    return lax.rem(place_ref[2] + k, heads)


def source(place_ref, heads, k):
    return lax.rem(place_ref[2] + heads - k, heads)


def pack_kv_kernel(heads, place_ref, k_ref, v_ref, *refs):
    out_refs, sems = refs[:-1], refs[-1]
    core = place_ref[1]
    d = HEAD_SIZE
    pairs = []
    for k, out_ref in enumerate(out_refs):
        z = onward(place_ref, heads, k)
        for n, g in enumerate((2 * z + core, 2 * z + 1 - core)):
            columns = at(g * d, d)
            pairs.append((k_ref.at[:, columns], out_ref.at[:, pl.ds(2 * n * d, d)]))
            pairs.append((v_ref.at[:, columns], out_ref.at[:, pl.ds((2 * n + 1) * d, d)]))
    copied(sems, pairs)


def pack_qd_kernel(heads, place_ref, q_ref, g_ref, mine_ref, other_ref, sems):
    core = place_ref[1]
    width = 2 * HEAD_SIZE
    pairs = []
    for ref, c in ((other_ref, 1 - core), (mine_ref, core)):
        for k in range(heads):
            columns = at((2 * onward(place_ref, heads, k) + c) * width, width)
            pairs.append((q_ref.at[:, columns], ref.at[k, :, pl.ds(0, width)]))
            pairs.append((g_ref.at[:, columns], ref.at[k, :, pl.ds(width, width)]))
    copied(sems, pairs)


def gather_kv_kernel(heads, place_ref, *refs):
    in_refs, (mine_ref, other_ref) = refs[:heads], refs[heads:]
    width = 2 * HEAD_SIZE
    for k, in_ref in enumerate(in_refs):
        rows = at(source(place_ref, heads, k) * BLOCK, BLOCK)
        mine_ref[rows] = in_ref[:, :width]
        other_ref[rows] = in_ref[:, width:]


def join_kernel(place_ref, mine_ref, sibling_ref, out_ref):
    core = place_ref[1]
    half = mine_ref.shape[0]
    out_ref[at(core * half, half)] = mine_ref[...]
    out_ref[at((1 - core) * half, half)] = sibling_ref[...]


def merge_rows_kernel(heads, place_ref, mine_ref, other_ref, *out_refs):
    core = place_ref[1]
    for k, out_ref in enumerate(out_refs):
        out_ref[at(core * BLOCK, BLOCK)] = mine_ref[k]
        out_ref[at((1 - core) * BLOCK, BLOCK)] = other_ref[k]


def merge_columns_kernel(heads, place_ref, mine_ref, other_ref, *out_refs):
    core = place_ref[1]
    width = 2 * HEAD_SIZE
    for k, out_ref in enumerate(out_refs):
        rows = slice(k * BLOCK, (k + 1) * BLOCK)
        out_ref[:, at(core * width, width)] = mine_ref[rows]
        out_ref[:, at((1 - core) * width, width)] = other_ref[rows]


def unpack_dq_kernel(heads, place_ref, *refs):
    in_refs, out_ref, sems = refs[:-2], refs[-2], refs[-1]
    width = 4 * HEAD_SIZE
    pairs = []
    for k, in_ref in enumerate(in_refs):
        pairs.append((in_ref, out_ref.at[:, at(source(place_ref, heads, k) * width, width)]))
    copied(sems, pairs)


def unpack_kv_kernel(heads, place_ref, *refs):
    in_refs, k_ref, v_ref, sems = refs[:-3], refs[-3], refs[-2], refs[-1]
    core = place_ref[1]
    d = HEAD_SIZE
    pairs = []
    for k, in_ref in enumerate(in_refs):
        z = source(place_ref, heads, k)
        for n, g in enumerate((2 * z + core, 2 * z + 1 - core)):
            columns = at(g * d, d)
            pairs.append((in_ref.at[:, pl.ds(2 * n * d, d)], k_ref.at[:, columns]))
            pairs.append((in_ref.at[:, pl.ds((2 * n + 1) * d, d)], v_ref.at[:, columns]))
    copied(sems, pairs)


def add_kernel(heads, place_ref, own_ref, near_ref, sibling_ref, far_ref, *out_refs):
    width = 2 * HEAD_SIZE
    for k, out_ref in enumerate(out_refs):
        rows = at(onward(place_ref, heads, k) * BLOCK, BLOCK)
        wide = lambda ref: ref[rows].astype(jnp.float32)
        out_ref[:, :width] = (own_ref[rows] + wide(near_ref)).astype(jnp.bfloat16)
        out_ref[:, width:] = (wide(sibling_ref) + wide(far_ref)).astype(jnp.bfloat16)


def attention_block(i, count, q, g, own_ref, prev_ref, own_kt_ref, prev_kt_ref, own_grad_ref, prev_grad_ref, bias):
    d = HEAD_SIZE
    low, high = i * BLOCK, (i + 1) * BLOCK
    below, above = i > 0, i < count - 1
    key_row = lax.broadcasted_iota(jnp.int32, (BLOCK, 2 * BLOCK), 0)
    query_row = lax.broadcasted_iota(jnp.int32, (BLOCK, 2 * BLOCK), 1) % BLOCK
    own_seen = key_row <= query_row
    zero = jnp.zeros((BLOCK, 2 * BLOCK), jnp.bfloat16)
    dot_t = lambda a, b: lax.dot_general(a, b, contract_last, preferred_element_type=jnp.float32)
    dot = lambda a, b: jnp.dot(a, b, preferred_element_type=jnp.float32)
    s_own = dot_t(own_ref[:high, :d], q)
    s_prev = dot_t(prev_ref[low:, :d], q) + bias
    p_own = dot_t(own_ref[:high, d:], g)
    p_prev = dot_t(prev_ref[low:, d:], g)
    s_diag = jnp.where(own_seen, s_own[low:], s_prev[:BLOCK])
    p_diag = jnp.where(own_seen, p_own[low:], p_prev[:BLOCK])
    s = jnp.concatenate([s_own[:low]] * below + [s_diag] + [s_prev[BLOCK:]] * above, 0)
    dp = jnp.concatenate([p_own[:low]] * below + [p_diag] + [p_prev[BLOCK:]] * above, 0)
    top = jnp.max(s, axis=0, keepdims=True)
    w = jnp.exp2((s - top) * (score_scale * LOG2_E))
    inverse = 1.0 / jnp.sum(w, axis=0, keepdims=True)
    delta = jnp.sum(w * dp, axis=0, keepdims=True) * inverse
    attention = w * inverse
    ds = (attention * (dp - delta)).astype(jnp.bfloat16)
    low_attention = attention.astype(jnp.bfloat16)
    split = lambda x: (
        jnp.concatenate([x[:low]] * below + [jnp.where(own_seen, x[low:high], zero)], 0),
        jnp.concatenate([jnp.where(own_seen, zero, x[low:high])] + [x[high:]] * above, 0),
    )
    ds_own, ds_prev = split(ds)
    at_own, at_prev = split(low_attention)
    own_grad_ref[:high, d:] += dot(at_own, g)
    prev_grad_ref[low:, d:] += dot(at_prev, g)
    own_grad_ref[:high, :d] += dot(ds_own, q)
    prev_grad_ref[low:, :d] += dot(ds_prev, q)
    dq_t = dot(own_kt_ref[:, :high], ds_own) + dot(prev_kt_ref[:, low:], ds_prev)
    return dq_t * score_scale


def attention_kernel(heads, steps, last, place_ref, own_ref, near_ref, far_ref, *refs):
    d = HEAD_SIZE
    count = 2 * heads
    half = heads * BLOCK
    block_refs, refs = refs[: len(steps)], refs[len(steps) :]
    if last:
        own_so_far_ref, prev_so_far_ref, mine_so_far_ref, other_so_far_ref = refs[:4]
        dq_mine_ref, dq_other_ref, own_mine_ref, own_other_ref, prev_mine_ref, prev_other_ref = refs[4:10]
        qd_ref, prev_ref, own_kt_ref, prev_kt_ref, own_grad_ref, prev_grad_ref = refs[10:]
        own_grad_ref[...] = own_so_far_ref[...]
        prev_grad_ref[...] = prev_so_far_ref[...]
        dq_mine_ref[...] = mine_so_far_ref[...]
        dq_other_ref[...] = other_so_far_ref[...]
    else:
        dq_mine_ref, dq_other_ref, own_grad_ref, prev_grad_ref = refs[:4]
        qd_ref, prev_ref, own_kt_ref, prev_kt_ref = refs[4:]
        own_grad_ref[...] = jnp.zeros_like(own_grad_ref)
        prev_grad_ref[...] = jnp.zeros_like(prev_grad_ref)
        dq_mine_ref[...] = jnp.zeros_like(dq_mine_ref)
        dq_other_ref[...] = jnp.zeros_like(dq_other_ref)
    first, core, head = place_ref[0], place_ref[1], place_ref[2]
    mine, other = at(core * half, half), at((1 - core) * half, half)
    prev_ref[mine] = near_ref[...]
    prev_ref[other] = far_ref[...]
    for n, block_ref in enumerate(block_refs):
        qd_ref[n] = block_ref[: 2 * BLOCK]
    bias = jnp.where(first == 1, masked_value, 0.0).astype(jnp.float32)
    own_kt_ref[...] = own_ref[:, :d].T
    prev_kt_ref[...] = prev_ref[:, :d].T

    @pl.loop(0, len(steps))
    def _(n):
        step = steps[0] + n
        z_here = lax.rem(head + heads - step, heads)
        place_out = at(lax.rem(heads - step, heads) * BLOCK, BLOCK)
        for z in range(heads):

            @pl.when(z_here == z)
            def _():
                for c in range(2):
                    rows = slice(c * BLOCK, (c + 1) * BLOCK)
                    q = jnp.concatenate([qd_ref[n, rows, :d], qd_ref[n, rows, d : 2 * d]], 0)
                    g = jnp.concatenate([qd_ref[n, rows, 2 * d : 3 * d], qd_ref[n, rows, 3 * d :]], 0)
                    dq_t = attention_block(
                        c * heads + z, count, q, g, own_ref, prev_ref, own_kt_ref, prev_kt_ref,
                        own_grad_ref, prev_grad_ref, bias,
                    )
                    dq = jnp.concatenate([dq_t[:, :BLOCK].T, dq_t[:, BLOCK:].T], 1).astype(jnp.bfloat16)

                    @pl.when(core == c)
                    def _():
                        dq_mine_ref[place_out] = dq

                    @pl.when(core != c)
                    def _():
                        dq_other_ref[place_out] = dq

    if last:
        for ref, grad_ref, rows in (
            (prev_mine_ref, prev_grad_ref, mine),
            (prev_other_ref, prev_grad_ref, other),
            (own_other_ref, own_grad_ref, other),
            (own_mine_ref, own_grad_ref, mine),
        ):
            ref[:, :d] = (grad_ref[rows, :d] * score_scale).astype(ref.dtype)
            ref[:, d:] = grad_ref[rows, d:].astype(ref.dtype)


def attention_backward(heads, steps, place, own, near, far, blocks, so_far=()):
    half, d = heads * BLOCK, HEAD_SIZE
    whole = 2 * half
    low, wide = jnp.bfloat16, jnp.float32
    part = shape_of(low, half, 2 * d)
    scratch = (
        pltpu.VMEM((len(steps), 2 * BLOCK, 4 * d), low),
        pltpu.VMEM((whole, 2 * d), low),
        pltpu.VMEM((d, whole), low),
        pltpu.VMEM((d, whole), low),
    )
    sums = shape_of(wide, whole, 2 * d)
    if so_far:
        outs = (part, part, shape_of(wide, half, 2 * d), part, part, part)
        scratch += (pltpu.VMEM((whole, 2 * d), wide), pltpu.VMEM((whole, 2 * d), wide))
    else:
        outs = (part, part, sums, sums)
    return call(
        functools.partial(attention_kernel, heads, steps, bool(so_far)),
        outs,
        (place, own, near, far) + tuple(blocks) + tuple(so_far),
        scratch,
        10 * whole * whole * d,
        whole * whole,
        32,
    )


def moved(value, chips, heads, chip_step, flip, head_step):
    index = lambda chip, core, head: (chip * 2 + core) * heads + head
    pairs = [
        (index(chip, core, head), index(chip + chip_step, core ^ flip, (head + head_step) % heads))
        for chip in range(chips)
        for core in range(2)
        for head in range(heads)
        if 0 <= chip + chip_step < chips
    ]
    return lax.ppermute(value, ("chip", "core", "head"), pairs)


def on_device(query_rows, key_rows, saved_value_rows, out_grad):
    chips, heads = lax.axis_size("chip"), lax.axis_size("head")
    send = functools.partial(moved, chips=chips, heads=heads)
    rows, d, low = key_rows.shape[0], HEAD_SIZE, jnp.bfloat16
    bind = lambda kernel: functools.partial(kernel, heads)
    place = jnp.stack(
        [(lax.axis_index("chip") == 0).astype(jnp.int32), lax.axis_index("core"), lax.axis_index("head")]
    ).astype(jnp.int32)

    def spread(parts):
        order = sorted(range(1, heads), key=lambda k: -min(k, heads - k))
        out = {k: send(parts[k], chip_step=0, flip=0, head_step=k) for k in order}
        return (parts[0],) + tuple(out[k] for k in range(1, heads))

    across = functools.partial(send, head_step=0)
    slab = shape_of(low, rows, 4 * d)
    kvs = copy_call(bind(pack_kv_kernel), 4 * heads, (slab,) * heads, (place, key_rows, saved_value_rows))
    qd_mine, qd_other = copy_call(
        bind(pack_qd_kernel),
        4 * heads,
        (shape_of(low, heads, rows, 4 * d),) * 2,
        (place, query_rows, out_grad),
    )
    kvs = spread(kvs)
    qd_other = across(qd_other, chip_step=0, flip=1)
    mine, other = call(bind(gather_kv_kernel), (shape_of(low, heads * rows, 2 * d),) * 2, (place,) + kvs)
    near = across(mine, chip_step=1, flip=0)
    far = across(other, chip_step=1, flip=1)
    blocks = call(
        bind(merge_rows_kernel),
        (shape_of(low, 2 * rows + 16, 4 * d),) * heads,
        (place, qd_mine, qd_other),
    )
    blocks = spread(blocks)
    sibling = across(other, chip_step=0, flip=1)
    own = call(join_kernel, shape_of(low, 2 * heads * rows, 2 * d), (place, mine, sibling))
    early, late = tuple(range(heads // 2)), tuple(range(heads // 2, heads))
    dq_mine, dq_other, own_sums, prev_sums = attention_backward(
        heads, early, place, own, near, far, [blocks[k] for k in early]
    )
    dq_mine, dq_other, own_mine, own_other, prev_mine, prev_other = attention_backward(
        heads, late, place, own, near, far, [blocks[k] for k in late], (own_sums, prev_sums, dq_mine, dq_other)
    )
    near_back = across(prev_mine, chip_step=-1, flip=0)
    far_back = across(prev_other, chip_step=-1, flip=1)
    sibling_back = across(own_other, chip_step=0, flip=1)
    dq_other = across(dq_other, chip_step=0, flip=1)
    dqs = spread(call(bind(merge_columns_kernel), (slab,) * heads, (place, dq_mine, dq_other)))
    query_grad = copy_call(bind(unpack_dq_kernel), heads, shape_of(low, *query_rows.shape), (place,) + dqs)
    totals = spread(
        call(bind(add_kernel), (slab,) * heads, (place, own_mine, near_back, sibling_back, far_back))
    )
    key_grad, value_grad = copy_call(
        bind(unpack_kv_kernel), 4 * heads, (shape_of(low, *key_rows.shape),) * 2, (place,) + totals
    )
    return query_grad, key_grad, value_grad


def solution(mesh):
    heads = mesh.shape["head"]
    devices = mesh.devices.reshape(-1, 2, heads)
    fine_mesh = Mesh(devices, ("chip", "core", "head"))
    rows = P(("chip", "core", "head"), None)
    return jax.shard_map(
        on_device,
        mesh=fine_mesh,
        in_specs=(rows,) * 4,
        out_specs=(rows,) * 3,
        check_vma=False,
    )
```

```python
import functools

import jax
import jax.numpy as jnp
from jax import lax
from jax.experimental import pallas as pl
from jax.experimental.pallas import tpu as pltpu
from jax.sharding import Mesh
from jax.sharding import PartitionSpec as P

HEAD_SIZE = 128
BLOCK = 128
LOG2_E = 1.4426950408889634

score_scale = 168.0 ** (-0.5)
masked_value = -1e30
contract_last = (((1,), (1,)), ((), ()))
VMEM_SPEC = pl.BlockSpec(memory_space=pltpu.VMEM)
ANY_SPEC = pl.BlockSpec(memory_space=pl.ANY)
SMEM_SPEC = pl.BlockSpec(memory_space=pltpu.SMEM)


def call(kernel, out_shape, operands, scratch=(), flops=0, transcendentals=0, vmem=16, spec=VMEM_SPEC, out_spec=VMEM_SPEC):
    outs = out_shape if isinstance(out_shape, tuple) else (out_shape,)
    moved = sum(a.size * a.dtype.itemsize for a in operands + outs)
    return pl.pallas_call(
        kernel,
        out_shape=out_shape,
        in_specs=[SMEM_SPEC] + [spec] * (len(operands) - 1),
        out_specs=jax.tree.map(lambda _: out_spec, out_shape),
        scratch_shapes=list(scratch),
        compiler_params=pltpu.CompilerParams(vmem_limit_bytes=vmem * 2**20),
        cost_estimate=pl.CostEstimate(flops=flops, bytes_accessed=moved, transcendentals=transcendentals),
    )(*operands)


def copy_call(kernel, copies, out_shape, operands):
    return call(kernel, out_shape, operands, (pltpu.SemaphoreType.DMA((copies,)),), spec=ANY_SPEC, out_spec=ANY_SPEC)


def shape_of(dtype, *shape):
    return jax.ShapeDtypeStruct(shape, dtype)


def at(start, size):
    return pl.ds(pl.multiple_of(start, size), size)


def copied(sems, pairs):
    copies = [pltpu.make_async_copy(src, dst, sems.at[n]) for n, (src, dst) in enumerate(pairs)]
    for copy in copies:
        copy.start()
    for copy in copies:
        copy.wait()


def onward(place_ref, heads, k):
    return lax.rem(place_ref[2] + k, heads)


def source(place_ref, heads, k):
    return lax.rem(place_ref[2] + heads - k, heads)


def pack_kv_kernel(heads, place_ref, k_ref, v_ref, *refs):
    out_refs, sems = refs[:-1], refs[-1]
    core = place_ref[1]
    d = HEAD_SIZE
    pairs = []
    for k, out_ref in enumerate(out_refs):
        z = onward(place_ref, heads, k)
        for n, g in enumerate((2 * z + core, 2 * z + 1 - core)):
            columns = at(g * d, d)
            pairs.append((k_ref.at[:, columns], out_ref.at[:, pl.ds(2 * n * d, d)]))
            pairs.append((v_ref.at[:, columns], out_ref.at[:, pl.ds((2 * n + 1) * d, d)]))
    copied(sems, pairs)


def pack_qd_kernel(heads, place_ref, q_ref, g_ref, mine_ref, other_ref, sems):
    core = place_ref[1]
    width = 2 * HEAD_SIZE
    pairs = []
    for ref, c in ((other_ref, 1 - core), (mine_ref, core)):
        for k in range(heads):
            columns = at((2 * onward(place_ref, heads, k) + c) * width, width)
            pairs.append((q_ref.at[:, columns], ref.at[k, :, pl.ds(0, width)]))
            pairs.append((g_ref.at[:, columns], ref.at[k, :, pl.ds(width, width)]))
    copied(sems, pairs)


def gather_kv_kernel(heads, place_ref, *refs):
    in_refs, (mine_ref, other_ref) = refs[:heads], refs[heads:]
    width = 2 * HEAD_SIZE
    for k, in_ref in enumerate(in_refs):
        rows = at(source(place_ref, heads, k) * BLOCK, BLOCK)
        mine_ref[rows] = in_ref[:, :width]
        other_ref[rows] = in_ref[:, width:]


def join_kernel(place_ref, mine_ref, sibling_ref, out_ref, kt_ref):
    core = place_ref[1]
    half = mine_ref.shape[0]
    out_ref[at(core * half, half)] = mine_ref[...]
    out_ref[at((1 - core) * half, half)] = sibling_ref[...]
    kt_ref[...] = out_ref[:, :HEAD_SIZE].T


def merge_rows_kernel(heads, place_ref, mine_ref, other_ref, after_ref, *out_refs):
    core = place_ref[1]
    for k, out_ref in enumerate(out_refs):
        out_ref[at(core * BLOCK, BLOCK)] = mine_ref[k]
        out_ref[at((1 - core) * BLOCK, BLOCK)] = other_ref[k]


def sort_dq_kernel(heads, place_ref, *refs):
    in_refs, (mine_ref, other_ref) = refs[:heads], refs[heads:]
    core = place_ref[1]
    for k, in_ref in enumerate(in_refs):
        mine_ref[k * BLOCK : (k + 1) * BLOCK] = in_ref[at(core * BLOCK, BLOCK)]
        other_ref[k * BLOCK : (k + 1) * BLOCK] = in_ref[at((1 - core) * BLOCK, BLOCK)]


def unpack_dq_kernel(heads, place_ref, mine_ref, sibling_ref, out_ref, sems):
    core = place_ref[1]
    width = 2 * HEAD_SIZE
    pairs = []
    for k in range(heads):
        z = source(place_ref, heads, k)
        for ref, c in ((mine_ref, core), (sibling_ref, 1 - core)):
            rows = pl.ds(k * BLOCK, BLOCK)
            pairs.append((ref.at[rows], out_ref.at[:, at((2 * z + c) * width, width)]))
    copied(sems, pairs)


def unpack_kv_kernel(heads, place_ref, *refs):
    in_refs, (k_ref, v_ref) = refs[:heads], refs[heads:]
    core, head = place_ref[1], place_ref[2]
    d = HEAD_SIZE
    for h in range(heads):
        for c in range(2):

            @pl.when((head == h) & (core == c))
            def _():
                for k, in_ref in enumerate(in_refs):
                    z = (h - k) % heads
                    for n, g in enumerate((2 * z + c, 2 * z + 1 - c)):
                        k_ref[:, g * d : (g + 1) * d] = in_ref[:, 2 * n * d : (2 * n + 1) * d]
                        v_ref[:, g * d : (g + 1) * d] = in_ref[:, (2 * n + 1) * d : (2 * n + 2) * d]


def add_kernel(heads, place_ref, own_ref, near_ref, sibling_ref, far_ref, *out_refs):
    width = 2 * HEAD_SIZE
    for k, out_ref in enumerate(out_refs):
        rows = at(onward(place_ref, heads, k) * BLOCK, BLOCK)
        wide = lambda ref: ref[rows].astype(jnp.float32)
        out_ref[:, :width] = (own_ref[rows] + wide(near_ref)).astype(jnp.bfloat16)
        out_ref[:, width:] = (wide(sibling_ref) + wide(far_ref)).astype(jnp.bfloat16)


def attention_block(i, count, q, g, own_ref, prev_ref, own_kt_ref, prev_kt_ref, own_grad_ref, prev_grad_ref, bias):
    d = HEAD_SIZE
    low, high = i * BLOCK, (i + 1) * BLOCK
    below, above = i > 0, i < count - 1
    key_row = lax.broadcasted_iota(jnp.int32, (BLOCK, 2 * BLOCK), 0)
    query_row = lax.broadcasted_iota(jnp.int32, (BLOCK, 2 * BLOCK), 1) % BLOCK
    own_seen = key_row <= query_row
    zero = jnp.zeros((BLOCK, 2 * BLOCK), jnp.bfloat16)
    dot_t = lambda a, b: lax.dot_general(a, b, contract_last, preferred_element_type=jnp.float32)
    dot = lambda a, b: jnp.dot(a, b, preferred_element_type=jnp.float32)
    s_own = dot_t(own_ref[:high, :d], q)
    s_prev = dot_t(prev_ref[low:, :d], q) + bias
    p_own = dot_t(own_ref[:high, d:], g)
    p_prev = dot_t(prev_ref[low:, d:], g)
    s_diag = jnp.where(own_seen, s_own[low:], s_prev[:BLOCK])
    p_diag = jnp.where(own_seen, p_own[low:], p_prev[:BLOCK])
    s = jnp.concatenate([s_own[:low]] * below + [s_diag] + [s_prev[BLOCK:]] * above, 0)
    dp = jnp.concatenate([p_own[:low]] * below + [p_diag] + [p_prev[BLOCK:]] * above, 0)
    top = jnp.max(s, axis=0, keepdims=True)
    w = jnp.exp2((s - top) * (score_scale * LOG2_E))
    inverse = 1.0 / jnp.sum(w, axis=0, keepdims=True)
    delta = jnp.sum(w * dp, axis=0, keepdims=True) * inverse
    attention = w * inverse
    ds = (attention * (dp - delta)).astype(jnp.bfloat16)
    low_attention = attention.astype(jnp.bfloat16)
    split = lambda x: (
        jnp.concatenate([x[:low]] * below + [jnp.where(own_seen, x[low:high], zero)], 0),
        jnp.concatenate([jnp.where(own_seen, zero, x[low:high])] + [x[high:]] * above, 0),
    )
    ds_own, ds_prev = split(ds)
    at_own, at_prev = split(low_attention)
    own_grad_ref[:high, d:] += dot(at_own, g)
    prev_grad_ref[low:, d:] += dot(at_prev, g)
    own_grad_ref[:high, :d] += dot(ds_own, q)
    prev_grad_ref[low:, :d] += dot(ds_prev, q)
    dq_t = dot(own_kt_ref[:, :high], ds_own) + dot(prev_kt_ref[:, low:], ds_prev)
    return dq_t * score_scale


def attention_kernel(heads, steps, last, place_ref, own_ref, own_kt_ref, a_ref, b_ref, *refs):
    d = HEAD_SIZE
    count = 2 * heads
    half = heads * BLOCK
    block_refs, refs = refs[: len(steps)], refs[len(steps) :]
    if last:
        own_so_far_ref, prev_so_far_ref = refs[:2]
        own_mine_ref, own_other_ref, prev_mine_ref, prev_other_ref = refs[2:6]
        dq_refs, (qd_ref, dq_ref, own_grad_ref, prev_grad_ref) = refs[6:-4], refs[-4:]
        prev_ref, prev_kt_ref = a_ref, b_ref
        own_grad_ref[...] = own_so_far_ref[...]
        prev_grad_ref[...] = prev_so_far_ref[...]
    else:
        prev_ref, prev_kt_ref, own_grad_ref, prev_grad_ref = refs[:4]
        dq_refs, (qd_ref, dq_ref) = refs[4:-2], refs[-2:]
        own_grad_ref[...] = jnp.zeros_like(own_grad_ref)
        prev_grad_ref[...] = jnp.zeros_like(prev_grad_ref)
    first, core, head = place_ref[0], place_ref[1], place_ref[2]
    mine, other = at(core * half, half), at((1 - core) * half, half)
    if not last:
        prev_ref[mine] = a_ref[...]
        prev_ref[other] = b_ref[...]
        prev_kt_ref[...] = prev_ref[:, :d].T
    for n, block_ref in enumerate(block_refs):
        qd_ref[n] = block_ref[: 2 * BLOCK]
    bias = jnp.where(first == 1, masked_value, 0.0).astype(jnp.float32)

    @pl.loop(0, len(steps))
    def _(n):
        step = steps[0] + n
        z_here = lax.rem(head + heads - step, heads)
        for z in range(heads):

            @pl.when(z_here == z)
            def _():
                for c in range(2):
                    rows = slice(c * BLOCK, (c + 1) * BLOCK)
                    q = jnp.concatenate([qd_ref[n, rows, :d], qd_ref[n, rows, d : 2 * d]], 0)
                    g = jnp.concatenate([qd_ref[n, rows, 2 * d : 3 * d], qd_ref[n, rows, 3 * d :]], 0)
                    dq_t = attention_block(
                        c * heads + z, count, q, g, own_ref, prev_ref, own_kt_ref, prev_kt_ref,
                        own_grad_ref, prev_grad_ref, bias,
                    )
                    dq_ref[n, rows, :d] = dq_t[:, :BLOCK].T.astype(jnp.bfloat16)
                    dq_ref[n, rows, d:] = dq_t[:, BLOCK:].T.astype(jnp.bfloat16)

    for n, ref in enumerate(dq_refs):
        ref[...] = dq_ref[n]
    if last:
        for ref, grad_ref, rows in (
            (prev_mine_ref, prev_grad_ref, mine),
            (prev_other_ref, prev_grad_ref, other),
            (own_other_ref, own_grad_ref, other),
            (own_mine_ref, own_grad_ref, mine),
        ):
            ref[:, :d] = (grad_ref[rows, :d] * score_scale).astype(ref.dtype)
            ref[:, d:] = grad_ref[rows, d:].astype(ref.dtype)


def attention_backward(heads, steps, place, own, prev, blocks, so_far=()):
    half, d = heads * BLOCK, HEAD_SIZE
    whole = 2 * half
    low, wide = jnp.bfloat16, jnp.float32
    part = shape_of(low, half, 2 * d)
    sums = shape_of(wide, whole, 2 * d)
    scratch = (
        pltpu.VMEM((len(steps), 2 * BLOCK, 4 * d), low),
        pltpu.VMEM((len(steps), 2 * BLOCK, 2 * d), low),
    )
    if so_far:
        outs = (shape_of(wide, half, 2 * d), part, part, part)
        scratch += (pltpu.VMEM((whole, 2 * d), wide), pltpu.VMEM((whole, 2 * d), wide))
    else:
        outs = (shape_of(low, whole, 2 * d), shape_of(low, d, whole), sums, sums)
    outs = call(
        functools.partial(attention_kernel, heads, steps, bool(so_far)),
        outs + (shape_of(low, 2 * BLOCK, 2 * d),) * len(steps),
        (place,) + tuple(own) + tuple(prev) + tuple(blocks) + tuple(so_far),
        scratch,
        10 * whole * whole * d,
        whole * whole,
        32,
    )
    return outs[:4], outs[4:]


def moved(value, chips, heads, chip_step, flip, head_step):
    index = lambda chip, core, head: (chip * 2 + core) * heads + head
    pairs = [
        (index(chip, core, head), index(chip + chip_step, core ^ flip, (head + head_step) % heads))
        for chip in range(chips)
        for core in range(2)
        for head in range(heads)
        if 0 <= chip + chip_step < chips
    ]
    return lax.ppermute(value, ("chip", "core", "head"), pairs)


def on_device(query_rows, key_rows, saved_value_rows, out_grad):
    chips, heads = lax.axis_size("chip"), lax.axis_size("head")
    send = functools.partial(moved, chips=chips, heads=heads)
    rows, d, low = key_rows.shape[0], HEAD_SIZE, jnp.bfloat16
    bind = lambda kernel: functools.partial(kernel, heads)
    place = jnp.stack(
        [(lax.axis_index("chip") == 0).astype(jnp.int32), lax.axis_index("core"), lax.axis_index("head")]
    ).astype(jnp.int32)

    def spread(parts):
        order = sorted(range(1, heads), key=lambda k: -min(k, heads - k))
        out = {k: send(parts[k], chip_step=0, flip=0, head_step=k) for k in order}
        return (parts[0],) + tuple(out[k] for k in range(1, heads))

    across = functools.partial(send, head_step=0)
    slab = shape_of(low, rows, 4 * d)
    kvs = copy_call(bind(pack_kv_kernel), 4 * heads, (slab,) * heads, (place, key_rows, saved_value_rows))
    qd_mine, qd_other = copy_call(
        bind(pack_qd_kernel),
        4 * heads,
        (shape_of(low, heads, rows, 4 * d),) * 2,
        (place, query_rows, out_grad),
    )
    kvs = spread(kvs)
    qd_other = across(qd_other, chip_step=0, flip=1)
    mine, other = call(bind(gather_kv_kernel), (shape_of(low, heads * rows, 2 * d),) * 2, (place,) + kvs)
    near = across(mine, chip_step=1, flip=0)
    far = across(other, chip_step=1, flip=1)
    blocks = call(
        bind(merge_rows_kernel),
        (shape_of(low, 2 * rows + 16, 4 * d),) * heads,
        (place, qd_mine, qd_other, mine[:8]),
    )
    blocks = spread(blocks)
    sibling = across(other, chip_step=0, flip=1)
    own = call(
        join_kernel,
        (shape_of(low, 2 * heads * rows, 2 * d), shape_of(low, d, 2 * heads * rows)),
        (place, mine, sibling),
    )
    early, late = tuple(range(heads // 2)), tuple(range(heads // 2, heads))
    prev_and_sums, dq_early = attention_backward(heads, early, place, own, (near, far), [blocks[k] for k in early])
    grads, dq_late = attention_backward(
        heads, late, place, own, prev_and_sums[:2], [blocks[k] for k in late], prev_and_sums[2:]
    )
    own_mine, own_other, prev_mine, prev_other = grads
    near_back = across(prev_mine, chip_step=-1, flip=0)
    far_back = across(prev_other, chip_step=-1, flip=1)
    sibling_back = across(own_other, chip_step=0, flip=1)
    back = dict(zip(early + late, dq_early + dq_late))
    dqs = [
        send(back[heads - k], chip_step=0, flip=0, head_step=k) if k else back[0] for k in range(heads)
    ]
    totals = call(bind(add_kernel), (slab,) * heads, (place, own_mine, near_back, sibling_back, far_back))
    dq_mine, dq_other = call(
        bind(sort_dq_kernel), (shape_of(low, heads * rows, 2 * d),) * 2, (place,) + tuple(dqs)
    )
    dq_sibling = across(dq_other, chip_step=0, flip=1)
    query_grad = copy_call(
        bind(unpack_dq_kernel), 2 * heads, shape_of(low, *query_rows.shape), (place, dq_mine, dq_sibling)
    )
    totals = spread(totals)
    key_grad, value_grad = call(
        bind(unpack_kv_kernel), (shape_of(low, *key_rows.shape),) * 2, (place,) + totals
    )
    return query_grad, key_grad, value_grad


def solution(mesh):
    heads = mesh.shape["head"]
    devices = mesh.devices.reshape(-1, 2, heads)
    fine_mesh = Mesh(devices, ("chip", "core", "head"))
    rows = P(("chip", "core", "head"), None)
    return jax.shard_map(
        on_device,
        mesh=fine_mesh,
        in_specs=(rows,) * 4,
        out_specs=(rows,) * 3,
        check_vma=False,
    )
```

```python
import functools

import jax
import jax.numpy as jnp
from jax import lax
from jax.experimental import pallas as pl
from jax.experimental.pallas import tpu as pltpu
from jax.sharding import Mesh
from jax.sharding import PartitionSpec as P

HEAD_SIZE = 128
BLOCK = 128
LOG2_E = 1.4426950408889634

score_scale = 168.0 ** (-0.5)
masked_value = -1e30
contract_last = (((1,), (1,)), ((), ()))
VMEM_SPEC = pl.BlockSpec(memory_space=pltpu.VMEM)
ANY_SPEC = pl.BlockSpec(memory_space=pl.ANY)
SMEM_SPEC = pl.BlockSpec(memory_space=pltpu.SMEM)


def call(kernel, out_shape, operands, scratch=(), flops=0, transcendentals=0, vmem=16, spec=VMEM_SPEC, out_spec=VMEM_SPEC):
    outs = out_shape if isinstance(out_shape, tuple) else (out_shape,)
    moved = sum(a.size * a.dtype.itemsize for a in operands + outs)
    return pl.pallas_call(
        kernel,
        out_shape=out_shape,
        in_specs=[SMEM_SPEC] + [spec] * (len(operands) - 1),
        out_specs=jax.tree.map(lambda _: out_spec, out_shape),
        scratch_shapes=list(scratch),
        compiler_params=pltpu.CompilerParams(vmem_limit_bytes=vmem * 2**20),
        cost_estimate=pl.CostEstimate(flops=flops, bytes_accessed=moved, transcendentals=transcendentals),
    )(*operands)


def copy_call(kernel, copies, out_shape, operands):
    return call(kernel, out_shape, operands, (pltpu.SemaphoreType.DMA((copies,)),), spec=ANY_SPEC, out_spec=ANY_SPEC)


def shape_of(dtype, *shape):
    return jax.ShapeDtypeStruct(shape, dtype)


def at(start, size):
    return pl.ds(pl.multiple_of(start, size), size)


def copied(sems, pairs):
    copies = [pltpu.make_async_copy(src, dst, sems.at[n]) for n, (src, dst) in enumerate(pairs)]
    for copy in copies:
        copy.start()
    for copy in copies:
        copy.wait()


def onward(place_ref, heads, k):
    return lax.rem(place_ref[2] + k, heads)


def source(place_ref, heads, k):
    return lax.rem(place_ref[2] + heads - k, heads)


def pack_kv_kernel(heads, place_ref, k_ref, v_ref, *refs):
    out_refs, sems = refs[:-1], refs[-1]
    core = place_ref[1]
    d = HEAD_SIZE
    pairs = []
    for k, out_ref in enumerate(out_refs):
        z = onward(place_ref, heads, k)
        for n, g in enumerate((2 * z + core, 2 * z + 1 - core)):
            columns = at(g * d, d)
            pairs.append((k_ref.at[:, columns], out_ref.at[:, pl.ds(2 * n * d, d)]))
            pairs.append((v_ref.at[:, columns], out_ref.at[:, pl.ds((2 * n + 1) * d, d)]))
    copied(sems, pairs)


def pack_qd_kernel(heads, place_ref, q_ref, g_ref, mine_ref, other_ref, sems):
    core = place_ref[1]
    width = 2 * HEAD_SIZE
    pairs = []
    for ref, c in ((other_ref, 1 - core), (mine_ref, core)):
        for k in range(heads):
            columns = at((2 * k + c) * width, width)
            pairs.append((q_ref.at[:, columns], ref.at[k, :, pl.ds(0, width)]))
            pairs.append((g_ref.at[:, columns], ref.at[k, :, pl.ds(width, width)]))
    copied(sems, pairs)


def gather_kv_kernel(heads, place_ref, *refs):
    in_refs, (mine_ref, other_ref) = refs[:heads], refs[heads:]
    width = 2 * HEAD_SIZE
    for k, in_ref in enumerate(in_refs):
        rows = at(source(place_ref, heads, k) * BLOCK, BLOCK)
        mine_ref[rows] = in_ref[:, :width]
        other_ref[rows] = in_ref[:, width:]


def join_kernel(place_ref, mine_ref, sibling_ref, out_ref, kt_ref):
    core = place_ref[1]
    half = mine_ref.shape[0]
    out_ref[at(core * half, half)] = mine_ref[...]
    out_ref[at((1 - core) * half, half)] = sibling_ref[...]
    kt_ref[...] = out_ref[:, :HEAD_SIZE].T


def merge_rows_kernel(heads, place_ref, mine_ref, other_ref, out_ref):
    core = place_ref[1]
    for z in range(heads):
        out_ref[z, at(core * BLOCK, BLOCK)] = mine_ref[z]
        out_ref[z, at((1 - core) * BLOCK, BLOCK)] = other_ref[z]


def sort_dq_kernel(heads, place_ref, *refs):
    in_refs, (after_ref, mine_ref, other_ref) = refs[:heads], refs[heads:]
    core = place_ref[1]
    for k, in_ref in enumerate(in_refs):
        mine_ref[k * BLOCK : (k + 1) * BLOCK] = in_ref[at(core * BLOCK, BLOCK)]
        other_ref[k * BLOCK : (k + 1) * BLOCK] = in_ref[at((1 - core) * BLOCK, BLOCK)]


def unpack_dq_kernel(heads, place_ref, mine_ref, sibling_ref, out_ref, sems):
    core = place_ref[1]
    width = 2 * HEAD_SIZE
    pairs = []
    for k in range(heads):
        z = source(place_ref, heads, k)
        for ref, c in ((mine_ref, core), (sibling_ref, 1 - core)):
            rows = pl.ds(k * BLOCK, BLOCK)
            pairs.append((ref.at[rows], out_ref.at[:, at((2 * z + c) * width, width)]))
    copied(sems, pairs)


def unpack_kv_kernel(heads, place_ref, *refs):
    in_refs, (k_ref, v_ref) = refs[:heads], refs[heads:]
    core, head = place_ref[1], place_ref[2]
    d = HEAD_SIZE
    for h in range(heads):
        for c in range(2):

            @pl.when((head == h) & (core == c))
            def _():
                for k, in_ref in enumerate(in_refs):
                    z = (h - k) % heads
                    for n, g in enumerate((2 * z + c, 2 * z + 1 - c)):
                        k_ref[:, g * d : (g + 1) * d] = in_ref[:, 2 * n * d : (2 * n + 1) * d]
                        v_ref[:, g * d : (g + 1) * d] = in_ref[:, (2 * n + 1) * d : (2 * n + 2) * d]


def add_kernel(heads, place_ref, own_ref, near_ref, sibling_ref, far_ref, *out_refs):
    width = 2 * HEAD_SIZE
    for k, out_ref in enumerate(out_refs):
        rows = at(onward(place_ref, heads, k) * BLOCK, BLOCK)
        wide = lambda ref: ref[rows].astype(jnp.float32)
        out_ref[:, :width] = (own_ref[rows] + wide(near_ref)).astype(jnp.bfloat16)
        out_ref[:, width:] = (wide(sibling_ref) + wide(far_ref)).astype(jnp.bfloat16)


def attention_block(i, count, q, g, own_ref, prev_ref, own_kt_ref, prev_kt_ref, own_grad_ref, prev_grad_ref, bias):
    d = HEAD_SIZE
    low, high = i * BLOCK, (i + 1) * BLOCK
    below, above = i > 0, i < count - 1
    key_row = lax.broadcasted_iota(jnp.int32, (BLOCK, 2 * BLOCK), 0)
    query_row = lax.broadcasted_iota(jnp.int32, (BLOCK, 2 * BLOCK), 1) % BLOCK
    own_seen = key_row <= query_row
    zero = jnp.zeros((BLOCK, 2 * BLOCK), jnp.bfloat16)
    dot_t = lambda a, b: lax.dot_general(a, b, contract_last, preferred_element_type=jnp.float32)
    dot = lambda a, b: jnp.dot(a, b, preferred_element_type=jnp.float32)
    s_own = dot_t(own_ref[:high, :d], q)
    s_prev = dot_t(prev_ref[low:, :d], q) + bias
    p_own = dot_t(own_ref[:high, d:], g)
    p_prev = dot_t(prev_ref[low:, d:], g)
    s_diag = jnp.where(own_seen, s_own[low:], s_prev[:BLOCK])
    p_diag = jnp.where(own_seen, p_own[low:], p_prev[:BLOCK])
    s = jnp.concatenate([s_own[:low]] * below + [s_diag] + [s_prev[BLOCK:]] * above, 0)
    dp = jnp.concatenate([p_own[:low]] * below + [p_diag] + [p_prev[BLOCK:]] * above, 0)
    top = jnp.max(s, axis=0, keepdims=True)
    w = jnp.exp2((s - top) * (score_scale * LOG2_E))
    inverse = 1.0 / jnp.sum(w, axis=0, keepdims=True)
    delta = jnp.sum(w * dp, axis=0, keepdims=True) * inverse
    attention = w * inverse
    ds = (attention * (dp - delta)).astype(jnp.bfloat16)
    low_attention = attention.astype(jnp.bfloat16)
    split = lambda x: (
        jnp.concatenate([x[:low]] * below + [jnp.where(own_seen, x[low:high], zero)], 0),
        jnp.concatenate([jnp.where(own_seen, zero, x[low:high])] + [x[high:]] * above, 0),
    )
    ds_own, ds_prev = split(ds)
    at_own, at_prev = split(low_attention)
    for columns, x_own, x_prev, y in ((slice(d, 2 * d), at_own, at_prev, g), (slice(0, d), ds_own, ds_prev, q)):
        sum_own, sum_prev = dot(x_own, y), dot(x_prev, y)
        if below:
            own_grad_ref[:low, columns] += sum_own[:low]
            prev_grad_ref[low:, columns] += sum_prev
        else:
            prev_grad_ref[:, columns] = sum_prev
        own_grad_ref[low:high, columns] = sum_own[low:]
    dq_t = dot(own_kt_ref[:, :high], ds_own) + dot(prev_kt_ref[:, low:], ds_prev)
    return dq_t * score_scale


def attention_kernel(heads, place_ref, own_ref, own_kt_ref, near_ref, far_ref, blocks_ref, *refs):
    d = HEAD_SIZE
    count = 2 * heads
    half = heads * BLOCK
    own_mine_ref, own_other_ref, prev_mine_ref, prev_other_ref = refs[:4]
    dq_refs, refs = refs[4 : 4 + heads], refs[4 + heads :]
    prev_ref, prev_kt_ref, dq_ref, own_grad_ref, prev_grad_ref = refs
    first, core, head = place_ref[0], place_ref[1], place_ref[2]
    mine, other = at(core * half, half), at((1 - core) * half, half)
    prev_ref[mine] = near_ref[...]
    prev_ref[other] = far_ref[...]
    prev_kt_ref[...] = prev_ref[:, :d].T
    bias = jnp.where(first == 1, masked_value, 0.0).astype(jnp.float32)
    for i in range(count):
        c, z = i // heads, i % heads
        rows = slice(c * BLOCK, (c + 1) * BLOCK)
        q = jnp.concatenate([blocks_ref[z, rows, :d], blocks_ref[z, rows, d : 2 * d]], 0)
        g = jnp.concatenate([blocks_ref[z, rows, 2 * d : 3 * d], blocks_ref[z, rows, 3 * d :]], 0)
        dq_t = attention_block(
            i, count, q, g, own_ref, prev_ref, own_kt_ref, prev_kt_ref, own_grad_ref, prev_grad_ref, bias
        )
        dq_ref[z, rows, :d] = dq_t[:, :BLOCK].T.astype(jnp.bfloat16)
        dq_ref[z, rows, d:] = dq_t[:, BLOCK:].T.astype(jnp.bfloat16)
    for k, ref in enumerate(dq_refs):
        ref[...] = dq_ref[lax.rem(head + k, heads)]
    for ref, grad_ref, rows in (
        (prev_mine_ref, prev_grad_ref, mine),
        (prev_other_ref, prev_grad_ref, other),
        (own_other_ref, own_grad_ref, other),
        (own_mine_ref, own_grad_ref, mine),
    ):
        ref[:, :d] = (grad_ref[rows, :d] * score_scale).astype(ref.dtype)
        ref[:, d:] = grad_ref[rows, d:].astype(ref.dtype)


def attention_backward(heads, place, own, near, far, blocks):
    half, d = heads * BLOCK, HEAD_SIZE
    whole = 2 * half
    low, wide = jnp.bfloat16, jnp.float32
    part = shape_of(low, half, 2 * d)
    scratch = (
        pltpu.VMEM((whole, 2 * d), low),
        pltpu.VMEM((d, whole), low),
        pltpu.VMEM((heads, 2 * BLOCK, 2 * d), low),
        pltpu.VMEM((whole, 2 * d), wide),
        pltpu.VMEM((whole, 2 * d), wide),
    )
    outs = call(
        functools.partial(attention_kernel, heads),
        (shape_of(wide, half, 2 * d), part, part, part) + (shape_of(low, 2 * BLOCK, 2 * d),) * heads,
        (place,) + tuple(own) + (near, far, blocks),
        scratch,
        20 * whole * whole * d,
        2 * whole * whole,
        32,
    )
    return outs[:4], outs[4:]


def moved(value, chips, heads, chip_step, flip, head_step):
    index = lambda chip, core, head: (chip * 2 + core) * heads + head
    pairs = [
        (index(chip, core, head), index(chip + chip_step, core ^ flip, (head + head_step) % heads))
        for chip in range(chips)
        for core in range(2)
        for head in range(heads)
        if 0 <= chip + chip_step < chips
    ]
    return lax.ppermute(value, ("chip", "core", "head"), pairs)


def on_device(query_rows, key_rows, saved_value_rows, out_grad):
    chips, heads = lax.axis_size("chip"), lax.axis_size("head")
    send = functools.partial(moved, chips=chips, heads=heads)
    rows, d, low = key_rows.shape[0], HEAD_SIZE, jnp.bfloat16
    bind = lambda kernel: functools.partial(kernel, heads)
    place = jnp.stack(
        [(lax.axis_index("chip") == 0).astype(jnp.int32), lax.axis_index("core"), lax.axis_index("head")]
    ).astype(jnp.int32)

    def spread(parts):
        order = sorted(range(1, heads), key=lambda k: -min(k, heads - k))
        out = {k: send(parts[k], chip_step=0, flip=0, head_step=k) for k in order}
        return (parts[0],) + tuple(out[k] for k in range(1, heads))

    across = functools.partial(send, head_step=0)
    slab = shape_of(low, rows, 4 * d)
    kvs = copy_call(bind(pack_kv_kernel), 4 * heads, (slab,) * heads, (place, key_rows, saved_value_rows))
    qd_mine, qd_other = copy_call(
        bind(pack_qd_kernel),
        4 * heads,
        (shape_of(low, heads, rows, 4 * d),) * 2,
        (place, query_rows, out_grad),
    )
    kvs = spread(kvs)
    qd_other = across(qd_other, chip_step=0, flip=1)
    mine, other = call(bind(gather_kv_kernel), (shape_of(low, heads * rows, 2 * d),) * 2, (place,) + kvs)
    near = across(mine, chip_step=1, flip=0)
    far = across(other, chip_step=1, flip=1)
    blocks = call(bind(merge_rows_kernel), shape_of(low, heads, 2 * rows, 4 * d), (place, qd_mine, qd_other))
    blocks = lax.all_to_all(blocks, "head", split_axis=0, concat_axis=0, tiled=True)
    sibling = across(other, chip_step=0, flip=1)
    own = call(
        join_kernel,
        (shape_of(low, 2 * heads * rows, 2 * d), shape_of(low, d, 2 * heads * rows)),
        (place, mine, sibling),
    )
    grads, dqs = attention_backward(heads, place, own, near, far, blocks)
    own_mine, own_other, prev_mine, prev_other = grads
    near_back = across(prev_mine, chip_step=-1, flip=0)
    far_back = across(prev_other, chip_step=-1, flip=1)
    sibling_back = across(own_other, chip_step=0, flip=1)
    dqs = spread(dqs)
    totals = call(bind(add_kernel), (slab,) * heads, (place, own_mine, near_back, sibling_back, far_back))
    dq_mine, dq_other = call(
        bind(sort_dq_kernel), (shape_of(low, heads * rows, 2 * d),) * 2, (place,) + dqs + (near_back[:8],)
    )
    dq_sibling = across(dq_other, chip_step=0, flip=1)
    query_grad = copy_call(
        bind(unpack_dq_kernel), 2 * heads, shape_of(low, *query_rows.shape), (place, dq_mine, dq_sibling)
    )
    totals = spread(totals)
    key_grad, value_grad = call(
        bind(unpack_kv_kernel), (shape_of(low, *key_rows.shape),) * 2, (place,) + totals
    )
    return query_grad, key_grad, value_grad


def solution(mesh):
    heads = mesh.shape["head"]
    devices = mesh.devices.reshape(-1, 2, heads)
    fine_mesh = Mesh(devices, ("chip", "core", "head"))
    rows = P(("chip", "core", "head"), None)
    return jax.shard_map(
        on_device,
        mesh=fine_mesh,
        in_specs=(rows,) * 4,
        out_specs=(rows,) * 3,
        check_vma=False,
    )
```

```python
import functools

import jax
import jax.numpy as jnp
from jax import lax
from jax.experimental import pallas as pl
from jax.experimental.pallas import tpu as pltpu
from jax.sharding import Mesh
from jax.sharding import PartitionSpec as P

HEAD_SIZE = 128
BLOCK = 128
LOG2_E = 1.4426950408889634

score_scale = 168.0 ** (-0.5)
masked_value = -1e30
contract_last = (((1,), (1,)), ((), ()))
VMEM_SPEC = pl.BlockSpec(memory_space=pltpu.VMEM)
ANY_SPEC = pl.BlockSpec(memory_space=pl.ANY)
SMEM_SPEC = pl.BlockSpec(memory_space=pltpu.SMEM)


def call(kernel, out_shape, operands, scratch=(), flops=0, transcendentals=0, vmem=16, spec=VMEM_SPEC, out_spec=VMEM_SPEC):
    outs = out_shape if isinstance(out_shape, tuple) else (out_shape,)
    moved = sum(a.size * a.dtype.itemsize for a in operands + outs)
    return pl.pallas_call(
        kernel,
        out_shape=out_shape,
        in_specs=[SMEM_SPEC] + [spec] * (len(operands) - 1),
        out_specs=jax.tree.map(lambda _: out_spec, out_shape),
        scratch_shapes=list(scratch),
        compiler_params=pltpu.CompilerParams(vmem_limit_bytes=vmem * 2**20),
        cost_estimate=pl.CostEstimate(flops=flops, bytes_accessed=moved, transcendentals=transcendentals),
    )(*operands)


def copy_call(kernel, copies, out_shape, operands):
    return call(kernel, out_shape, operands, (pltpu.SemaphoreType.DMA((copies,)),), spec=ANY_SPEC, out_spec=ANY_SPEC)


def shape_of(dtype, *shape):
    return jax.ShapeDtypeStruct(shape, dtype)


def at(start, size):
    return pl.ds(pl.multiple_of(start, size), size)


def copied(sems, pairs):
    copies = [pltpu.make_async_copy(src, dst, sems.at[n]) for n, (src, dst) in enumerate(pairs)]
    for copy in copies:
        copy.start()
    for copy in copies:
        copy.wait()


def onward(place_ref, heads, k):
    return lax.rem(place_ref[2] + k, heads)


def source(place_ref, heads, k):
    return lax.rem(place_ref[2] + heads - k, heads)


def pack_kv_kernel(heads, place_ref, k_ref, v_ref, *refs):
    out_refs, sems = refs[:-1], refs[-1]
    core = place_ref[1]
    d = HEAD_SIZE
    pairs = []
    for k, out_ref in enumerate(out_refs):
        z = onward(place_ref, heads, k)
        for n, g in enumerate((2 * z + core, 2 * z + 1 - core)):
            columns = at(g * d, d)
            pairs.append((k_ref.at[:, columns], out_ref.at[:, pl.ds(2 * n * d, d)]))
            pairs.append((v_ref.at[:, columns], out_ref.at[:, pl.ds((2 * n + 1) * d, d)]))
    copied(sems, pairs)


def pack_qd_kernel(heads, place_ref, q_ref, g_ref, mine_ref, other_ref, sems):
    core = place_ref[1]
    width = 2 * HEAD_SIZE
    pairs = []
    for ref, c in ((other_ref, 1 - core), (mine_ref, core)):
        for k in range(heads):
            columns = at((2 * onward(place_ref, heads, k) + c) * width, width)
            pairs.append((q_ref.at[:, columns], ref.at[k, :, pl.ds(0, width)]))
            pairs.append((g_ref.at[:, columns], ref.at[k, :, pl.ds(width, width)]))
    copied(sems, pairs)


def gather_kv_kernel(heads, place_ref, *refs):
    in_refs, (mine_ref, other_ref) = refs[:heads], refs[heads:]
    width = 2 * HEAD_SIZE
    for k, in_ref in enumerate(in_refs):
        rows = at(source(place_ref, heads, k) * BLOCK, BLOCK)
        mine_ref[rows] = in_ref[:, :width]
        other_ref[rows] = in_ref[:, width:]


def join_kernel(place_ref, mine_ref, sibling_ref, out_ref, kt_ref):
    core = place_ref[1]
    half = mine_ref.shape[0]
    out_ref[at(core * half, half)] = mine_ref[...]
    out_ref[at((1 - core) * half, half)] = sibling_ref[...]
    kt_ref[...] = out_ref[:, :HEAD_SIZE].T


def merge_rows_kernel(heads, place_ref, mine_ref, other_ref, after_ref, *out_refs):
    core = place_ref[1]
    for k, out_ref in enumerate(out_refs):
        out_ref[at(core * BLOCK, BLOCK)] = mine_ref[k]
        out_ref[at((1 - core) * BLOCK, BLOCK)] = other_ref[k]


def sort_dq_kernel(heads, place_ref, *refs):
    in_refs, (mine_ref, other_ref) = refs[:heads], refs[heads:]
    core = place_ref[1]
    for k, in_ref in enumerate(in_refs):
        mine_ref[k * BLOCK : (k + 1) * BLOCK] = in_ref[at(core * BLOCK, BLOCK)]
        other_ref[k * BLOCK : (k + 1) * BLOCK] = in_ref[at((1 - core) * BLOCK, BLOCK)]


def unpack_dq_kernel(heads, place_ref, mine_ref, sibling_ref, out_ref, sems):
    core = place_ref[1]
    width = 2 * HEAD_SIZE
    pairs = []
    for k in range(heads):
        z = source(place_ref, heads, k)
        for ref, c in ((mine_ref, core), (sibling_ref, 1 - core)):
            rows = pl.ds(k * BLOCK, BLOCK)
            pairs.append((ref.at[rows], out_ref.at[:, at((2 * z + c) * width, width)]))
    copied(sems, pairs)


def sort_kv_kernel(heads, place_ref, *refs):
    halves, (mine_ref, other_ref) = (refs[:heads], refs[heads : 2 * heads]), refs[2 * heads :]
    core = place_ref[1]
    for c in range(2):

        @pl.when(core == c)
        def _():
            for k in range(heads):
                mine_ref[k * BLOCK : (k + 1) * BLOCK] = halves[c][k][...]
                other_ref[k * BLOCK : (k + 1) * BLOCK] = halves[1 - c][k][...]


def unpack_kv_kernel(heads, place_ref, mine_ref, sibling_ref, k_ref, v_ref):
    core = place_ref[1]
    d = HEAD_SIZE
    for k in range(heads):
        z = source(place_ref, heads, k)
        rows = slice(k * BLOCK, (k + 1) * BLOCK)
        for ref, c in ((mine_ref, core), (sibling_ref, 1 - core)):
            columns = at((2 * z + c) * d, d)
            k_ref[:, columns] = ref[rows, :d]
            v_ref[:, columns] = ref[rows, d:]


def add_kernel(heads, place_ref, own_ref, back_ref, after_ref, *out_refs):
    for k, out_ref in enumerate(out_refs):
        rows = at(onward(place_ref, heads, k) * BLOCK, BLOCK)
        out_ref[...] = (own_ref[rows] + back_ref[rows].astype(jnp.float32)).astype(jnp.bfloat16)


def attention_block(i, count, q, g, own_ref, prev_ref, own_kt_ref, prev_kt_ref, own_grad_ref, prev_grad_ref, bias):
    d = HEAD_SIZE
    low, high = i * BLOCK, (i + 1) * BLOCK
    below, above = i > 0, i < count - 1
    key_row = lax.broadcasted_iota(jnp.int32, (BLOCK, 2 * BLOCK), 0)
    query_row = lax.broadcasted_iota(jnp.int32, (BLOCK, 2 * BLOCK), 1) % BLOCK
    own_seen = key_row <= query_row
    zero = jnp.zeros((BLOCK, 2 * BLOCK), jnp.bfloat16)
    dot_t = lambda a, b: lax.dot_general(a, b, contract_last, preferred_element_type=jnp.float32)
    dot = lambda a, b: jnp.dot(a, b, preferred_element_type=jnp.float32)
    s_own = dot_t(own_ref[:high, :d], q)
    s_prev = dot_t(prev_ref[low:, :d], q) + bias
    p_own = dot_t(own_ref[:high, d:], g)
    p_prev = dot_t(prev_ref[low:, d:], g)
    s_diag = jnp.where(own_seen, s_own[low:], s_prev[:BLOCK])
    p_diag = jnp.where(own_seen, p_own[low:], p_prev[:BLOCK])
    s = jnp.concatenate([s_own[:low]] * below + [s_diag] + [s_prev[BLOCK:]] * above, 0)
    dp = jnp.concatenate([p_own[:low]] * below + [p_diag] + [p_prev[BLOCK:]] * above, 0)
    top = jnp.max(s, axis=0, keepdims=True)
    w = jnp.exp2((s - top) * (score_scale * LOG2_E))
    inverse = 1.0 / jnp.sum(w, axis=0, keepdims=True)
    delta = jnp.sum(w * dp, axis=0, keepdims=True) * inverse
    attention = w * inverse
    ds = (attention * (dp - delta)).astype(jnp.bfloat16)
    low_attention = attention.astype(jnp.bfloat16)
    split = lambda x: (
        jnp.concatenate([x[:low]] * below + [jnp.where(own_seen, x[low:high], zero)], 0),
        jnp.concatenate([jnp.where(own_seen, zero, x[low:high])] + [x[high:]] * above, 0),
    )
    ds_own, ds_prev = split(ds)
    at_own, at_prev = split(low_attention)
    own_grad_ref[:high, d:] += dot(at_own, g)
    prev_grad_ref[low:, d:] += dot(at_prev, g)
    own_grad_ref[:high, :d] += dot(ds_own, q)
    prev_grad_ref[low:, :d] += dot(ds_prev, q)
    dq_t = dot(own_kt_ref[:, :high], ds_own) + dot(prev_kt_ref[:, low:], ds_prev)
    return dq_t * score_scale


def attention_kernel(heads, steps, cores, phase, place_ref, own_ref, own_kt_ref, a_ref, b_ref, *refs):
    d = HEAD_SIZE
    count = 2 * heads
    half = heads * BLOCK
    first, core, head = place_ref[0], place_ref[1], place_ref[2]
    low_rows, high_rows = slice(0, half), slice(half, 2 * half)
    block_refs, refs = refs[: len(steps)], refs[len(steps) :]
    prev_ref, prev_kt_ref = a_ref, b_ref
    if phase == 0:
        prev_ref, prev_kt_ref, own_grad_ref, prev_grad_ref = refs[:4]
        dq_refs, (qd_ref, dq_ref) = refs[4:-2], refs[-2:]
        own_grad_ref[...] = jnp.zeros_like(own_grad_ref)
        prev_grad_ref[...] = jnp.zeros_like(prev_grad_ref)
        prev_ref[at(core * half, half)] = a_ref[...]
        prev_ref[at((1 - core) * half, half)] = b_ref[...]
        prev_kt_ref[...] = prev_ref[:, :d].T
    elif phase == 1:
        own_sums_ref, prev_sums_ref, own_grad_ref, prev_high_ref, back_ref, dq_out_ref = refs[:6]
        qd_ref, dq_ref, prev_grad_ref = refs[6:]
        own_grad_ref[...] = own_sums_ref[low_rows]
        prev_grad_ref[...] = prev_sums_ref[...]
    else:
        own_low_ref, own_sums_ref, prev_high_ref, dq_so_far_ref = refs[:4]
        dq_early_refs, refs = refs[4 : 4 + heads - len(steps)], refs[4 + heads - len(steps) :]
        own_a_ref, own_b_ref, back_ref = refs[:3]
        dq_refs, (qd_ref, dq_ref, own_grad_ref, prev_grad_ref) = refs[3:-4], refs[-4:]
        own_grad_ref[low_rows] = own_low_ref[...]
        own_grad_ref[high_rows] = own_sums_ref[high_rows]
        prev_grad_ref[high_rows] = prev_high_ref[...]
        dq_ref[:, :BLOCK] = dq_so_far_ref[...]
    for n, block_ref in enumerate(block_refs):
        qd_ref[n] = block_ref[: 2 * BLOCK]
    bias = jnp.where(first == 1, masked_value, 0.0).astype(jnp.float32)

    @pl.loop(0, len(steps))
    def _(n):
        z_here = lax.rem(head + heads - (steps[0] + n), heads)
        for z in range(heads):

            @pl.when(z_here == z)
            def _():
                for c in cores:
                    rows = slice(c * BLOCK, (c + 1) * BLOCK)
                    q = jnp.concatenate([qd_ref[n, rows, :d], qd_ref[n, rows, d : 2 * d]], 0)
                    g = jnp.concatenate([qd_ref[n, rows, 2 * d : 3 * d], qd_ref[n, rows, 3 * d :]], 0)
                    dq_t = attention_block(
                        c * heads + z, count, q, g, own_ref, prev_ref, own_kt_ref, prev_kt_ref,
                        own_grad_ref, prev_grad_ref, bias,
                    )
                    dq_ref[n, rows, :d] = dq_t[:, :BLOCK].T.astype(jnp.bfloat16)
                    dq_ref[n, rows, d:] = dq_t[:, BLOCK:].T.astype(jnp.bfloat16)

    def finish(ref, grad_ref, rows):
        ref[low_rows, :d] = (grad_ref[rows, :d] * score_scale).astype(ref.dtype)
        ref[low_rows, d:] = grad_ref[rows, d:].astype(ref.dtype)

    if phase == 0:
        for n, ref in enumerate(dq_refs):
            ref[...] = dq_ref[n]
    elif phase == 1:
        finish(back_ref, prev_grad_ref, low_rows)
        prev_high_ref[...] = prev_grad_ref[high_rows]
        dq_out_ref[...] = dq_ref[:, :BLOCK]
    else:
        finish(back_ref, prev_grad_ref, high_rows)
        finish(own_a_ref, own_grad_ref, low_rows)
        finish(own_b_ref, own_grad_ref, high_rows)
        for ref, early_ref in zip(dq_refs, dq_early_refs):
            ref[...] = early_ref[...]
        for n, ref in enumerate(dq_refs[len(dq_early_refs) :]):
            ref[...] = dq_ref[n]


def attention_backward(heads, place, own, near, far, blocks):
    half, d = heads * BLOCK, HEAD_SIZE
    whole = 2 * half
    low, wide = jnp.bfloat16, jnp.float32
    sums, half_sums, part = shape_of(wide, whole, 2 * d), shape_of(wide, half, 2 * d), shape_of(low, half, 2 * d)
    block = shape_of(low, 2 * BLOCK, 2 * d)
    early, late = tuple(range(heads // 2)), tuple(range(heads // 2, heads))

    def run(steps, cores, phase, outs, operands, scratch):
        scratch = (
            pltpu.VMEM((len(steps), 2 * BLOCK, 4 * d), low),
            pltpu.VMEM((len(steps), 2 * BLOCK, 2 * d), low),
        ) + (pltpu.VMEM((whole, 2 * d), wide),) * scratch
        kernel = functools.partial(attention_kernel, heads, steps, cores, phase)
        return call(kernel, outs, (place,) + tuple(own) + tuple(operands), scratch, 1, 1, 32)

    outs = (shape_of(low, whole, 2 * d), shape_of(low, d, whole), sums, sums) + (block,) * len(early)
    outs = run(early, (0, 1), 0, outs, [near, far] + [blocks[k] for k in early], 0)
    prev, (own_sums, prev_sums), dq_early = outs[:2], outs[2:4], outs[4:]
    late_blocks = tuple(blocks[k] for k in late)
    wide_part = shape_of(low, half + 32, 2 * d)
    outs = (half_sums, half_sums, wide_part, shape_of(low, len(late), BLOCK, 2 * d))
    own_low, prev_high, back_a, dq_so_far = run(
        late, (0,), 1, outs, prev + late_blocks + (own_sums, prev_sums), 1
    )
    outs = run(
        late,
        (1,),
        2,
        (half_sums, half_sums, part) + (block,) * heads,
        prev + late_blocks + (own_low, own_sums, prev_high, dq_so_far) + dq_early,
        2,
    )
    return outs[:2], (back_a, outs[2]), outs[3:]


def moved(value, chips, heads, chip_step, flip, head_step):
    index = lambda chip, core, head: (chip * 2 + core) * heads + head
    pairs = [
        (index(chip, core, head), index(chip + chip_step, core ^ flip, (head + head_step) % heads))
        for chip in range(chips)
        for core in range(2)
        for head in range(heads)
        if 0 <= chip + chip_step < chips
    ]
    return lax.ppermute(value, ("chip", "core", "head"), pairs)


def on_device(query_rows, key_rows, saved_value_rows, out_grad):
    chips, heads = lax.axis_size("chip"), lax.axis_size("head")
    send = functools.partial(moved, chips=chips, heads=heads)
    rows, d, low = key_rows.shape[0], HEAD_SIZE, jnp.bfloat16
    bind = lambda kernel: functools.partial(kernel, heads)
    place = jnp.stack(
        [(lax.axis_index("chip") == 0).astype(jnp.int32), lax.axis_index("core"), lax.axis_index("head")]
    ).astype(jnp.int32)

    def spread(parts):
        order = sorted(range(1, heads), key=lambda k: -min(k, heads - k))
        out = {k: send(parts[k], chip_step=0, flip=0, head_step=k) for k in order}
        return (parts[0],) + tuple(out[k] for k in range(1, heads))

    across = functools.partial(send, head_step=0)
    slab = shape_of(low, rows, 4 * d)
    kvs = copy_call(bind(pack_kv_kernel), 4 * heads, (slab,) * heads, (place, key_rows, saved_value_rows))
    qd_mine, qd_other = copy_call(
        bind(pack_qd_kernel),
        4 * heads,
        (shape_of(low, heads, rows, 4 * d),) * 2,
        (place, query_rows, out_grad),
    )
    kvs = spread(kvs)
    qd_other = across(qd_other, chip_step=0, flip=1)
    mine, other = call(bind(gather_kv_kernel), (shape_of(low, heads * rows, 2 * d),) * 2, (place,) + kvs)
    near = across(mine, chip_step=1, flip=0)
    far = across(other, chip_step=1, flip=1)
    blocks = call(
        bind(merge_rows_kernel),
        (shape_of(low, 2 * rows + 16, 4 * d),) * heads,
        (place, qd_mine, qd_other, mine[:8]),
    )
    blocks = spread(blocks)
    sibling = across(other, chip_step=0, flip=1)
    own = call(
        join_kernel,
        (shape_of(low, 2 * heads * rows, 2 * d), shape_of(low, d, 2 * heads * rows)),
        (place, mine, sibling),
    )
    own_sums, partial, dqs = attention_backward(heads, place, own, near, far, blocks)
    back = [across(part, chip_step=-1, flip=0) for part in partial]
    dqs = (dqs[0],) + tuple(send(dqs[heads - k], chip_step=0, flip=0, head_step=k) for k in range(1, heads))
    piece = shape_of(low, rows, 2 * d)
    total_a = call(bind(add_kernel), (piece,) * heads, (place, own_sums[0], back[0], mine[:8]))
    total_b = call(bind(add_kernel), (piece,) * heads, (place, own_sums[1], back[1], total_a[0]))
    totals = [spread(total_a), spread(total_b)]
    kv_mine, kv_other = call(
        bind(sort_kv_kernel), (shape_of(low, heads * rows, 2 * d),) * 2, (place,) + totals[0] + totals[1]
    )
    kv_sibling = across(kv_other, chip_step=0, flip=1)
    dq_mine, dq_other = call(
        bind(sort_dq_kernel), (shape_of(low, heads * rows, 2 * d),) * 2, (place,) + tuple(dqs)
    )
    dq_sibling = across(dq_other, chip_step=0, flip=1)
    query_grad = copy_call(
        bind(unpack_dq_kernel), 2 * heads, shape_of(low, *query_rows.shape), (place, dq_mine, dq_sibling)
    )
    key_grad, value_grad = call(
        bind(unpack_kv_kernel), (shape_of(low, *key_rows.shape),) * 2, (place, kv_mine, kv_sibling)
    )
    return query_grad, key_grad, value_grad


def solution(mesh):
    heads = mesh.shape["head"]
    devices = mesh.devices.reshape(-1, 2, heads)
    fine_mesh = Mesh(devices, ("chip", "core", "head"))
    rows = P(("chip", "core", "head"), None)
    return jax.shard_map(
        on_device,
        mesh=fine_mesh,
        in_specs=(rows,) * 4,
        out_specs=(rows,) * 3,
        check_vma=False,
    )
```

```python
import functools

import jax
import jax.numpy as jnp
from jax import lax
from jax.experimental import pallas as pl
from jax.experimental.pallas import tpu as pltpu
from jax.sharding import Mesh
from jax.sharding import PartitionSpec as P

HEAD_SIZE = 128
BLOCK = 128
LOG2_E = 1.4426950408889634

score_scale = 168.0 ** (-0.5)
masked_value = -1e30
contract_last = (((1,), (1,)), ((), ()))
VMEM_SPEC = pl.BlockSpec(memory_space=pltpu.VMEM)
ANY_SPEC = pl.BlockSpec(memory_space=pl.ANY)
SMEM_SPEC = pl.BlockSpec(memory_space=pltpu.SMEM)


def call(kernel, out_shape, operands, scratch=(), flops=0, transcendentals=0, vmem=16, spec=VMEM_SPEC, out_spec=VMEM_SPEC):
    outs = out_shape if isinstance(out_shape, tuple) else (out_shape,)
    moved = sum(a.size * a.dtype.itemsize for a in operands + outs)
    return pl.pallas_call(
        kernel,
        out_shape=out_shape,
        in_specs=[SMEM_SPEC] + [spec] * (len(operands) - 1),
        out_specs=jax.tree.map(lambda _: out_spec, out_shape),
        scratch_shapes=list(scratch),
        compiler_params=pltpu.CompilerParams(vmem_limit_bytes=vmem * 2**20),
        cost_estimate=pl.CostEstimate(flops=flops, bytes_accessed=moved, transcendentals=transcendentals),
    )(*operands)


def copy_call(kernel, copies, out_shape, operands):
    return call(kernel, out_shape, operands, (pltpu.SemaphoreType.DMA((copies,)),), spec=ANY_SPEC, out_spec=ANY_SPEC)


def shape_of(dtype, *shape):
    return jax.ShapeDtypeStruct(shape, dtype)


def at(start, size):
    return pl.ds(pl.multiple_of(start, size), size)


def copied(sems, pairs):
    copies = [pltpu.make_async_copy(src, dst, sems.at[n]) for n, (src, dst) in enumerate(pairs)]
    for copy in copies:
        copy.start()
    for copy in copies:
        copy.wait()


def steps_of(heads):
    return (0,) + tuple(sorted(range(1, heads), key=lambda k: -min(k, heads - k)))


def onward(place_ref, heads, n):
    return lax.rem(place_ref[2] + steps_of(heads)[n], heads)


def source(place_ref, heads, n):
    return lax.rem(place_ref[2] + heads - steps_of(heads)[n], heads)


def pack_kernel(heads, place_ref, k_ref, v_ref, q_ref, g_ref, *refs):
    kv_refs, (mine_ref, other_ref, sems) = refs[:heads], refs[heads:]
    core = place_ref[1]
    d, width = HEAD_SIZE, 2 * HEAD_SIZE
    pairs = []
    for k, out_ref in enumerate(kv_refs):
        z = onward(place_ref, heads, k)
        for n, g in enumerate((2 * z + core, 2 * z + 1 - core)):
            columns = at(g * d, d)
            pairs.append((k_ref.at[:, columns], out_ref.at[:, pl.ds(2 * n * d, d)]))
            pairs.append((v_ref.at[:, columns], out_ref.at[:, pl.ds((2 * n + 1) * d, d)]))
    for ref, c in ((other_ref, 1 - core), (mine_ref, core)):
        for k in range(heads):
            columns = at((2 * onward(place_ref, heads, k) + c) * width, width)
            pairs.append((q_ref.at[:, columns], ref.at[k, :, pl.ds(0, width)]))
            pairs.append((g_ref.at[:, columns], ref.at[k, :, pl.ds(width, width)]))
    copied(sems, pairs)


def gather_kv_kernel(heads, place_ref, *refs):
    in_refs, (mine_ref, other_ref) = refs[:heads], refs[heads:]
    width = 2 * HEAD_SIZE
    for k, in_ref in enumerate(in_refs):
        rows = at(source(place_ref, heads, k) * BLOCK, BLOCK)
        mine_ref[rows] = in_ref[:, :width]
        other_ref[rows] = in_ref[:, width:]


def join_kernel(place_ref, mine_ref, sibling_ref, out_ref, kt_ref):
    core = place_ref[1]
    half = mine_ref.shape[0]
    out_ref[at(core * half, half)] = mine_ref[...]
    out_ref[at((1 - core) * half, half)] = sibling_ref[...]
    kt_ref[...] = out_ref[:, :HEAD_SIZE].T


def merge_rows_kernel(heads, place_ref, mine_ref, other_ref, after_ref, *out_refs):
    core = place_ref[1]
    for k, out_ref in enumerate(out_refs):
        out_ref[at(core * BLOCK, BLOCK)] = mine_ref[k]
        out_ref[at((1 - core) * BLOCK, BLOCK)] = other_ref[k]


def sort_kernel(heads, place_ref, *refs):
    in_refs, (mine_ref, other_ref) = refs[:heads], refs[heads:]
    core = place_ref[1]
    for k, in_ref in enumerate(in_refs):
        mine_ref[k * BLOCK : (k + 1) * BLOCK] = in_ref[at(core * BLOCK, BLOCK)]
        other_ref[k * BLOCK : (k + 1) * BLOCK] = in_ref[at((1 - core) * BLOCK, BLOCK)]


def unpack_dq_kernel(heads, place_ref, mine_ref, sibling_ref, out_ref, sems):
    core = place_ref[1]
    width = 2 * HEAD_SIZE
    pairs = []
    for k in range(heads):
        z = onward(place_ref, heads, k)
        for ref, c in ((mine_ref, core), (sibling_ref, 1 - core)):
            rows = pl.ds(k * BLOCK, BLOCK)
            pairs.append((ref.at[rows], out_ref.at[:, at((2 * z + c) * width, width)]))
    copied(sems, pairs)


def unpack_kv_kernel(heads, place_ref, mine_ref, sibling_ref, k_ref, v_ref):
    core = place_ref[1]
    d = HEAD_SIZE
    for k in range(heads):
        z = source(place_ref, heads, k)
        rows = slice(k * BLOCK, (k + 1) * BLOCK)
        for ref, c in ((mine_ref, core), (sibling_ref, 1 - core)):
            columns = at((2 * z + c) * d, d)
            k_ref[:, columns] = ref[rows, :d]
            v_ref[:, columns] = ref[rows, d:]


def add_kernel(heads, place_ref, own_a_ref, own_b_ref, back_a_ref, back_b_ref, *out_refs):
    for k, out_ref in enumerate(out_refs):
        rows = at(onward(place_ref, heads, k) * BLOCK, BLOCK)
        for c, (own_ref, back_ref) in enumerate(((own_a_ref, back_a_ref), (own_b_ref, back_b_ref))):
            total = own_ref[rows] + back_ref[rows].astype(jnp.float32)
            out_ref[c * BLOCK : (c + 1) * BLOCK] = total.astype(jnp.bfloat16)


def attention_block(i, count, q, g, own_ref, prev_ref, own_kt_ref, prev_kt_ref, own_grad_ref, prev_grad_ref, bias):
    d = HEAD_SIZE
    low, high = i * BLOCK, (i + 1) * BLOCK
    below, above = i > 0, i < count - 1
    key_row = lax.broadcasted_iota(jnp.int32, (BLOCK, 2 * BLOCK), 0)
    query_row = lax.broadcasted_iota(jnp.int32, (BLOCK, 2 * BLOCK), 1) % BLOCK
    own_seen = key_row <= query_row
    zero = jnp.zeros((BLOCK, 2 * BLOCK), jnp.bfloat16)
    dot_t = lambda a, b: lax.dot_general(a, b, contract_last, preferred_element_type=jnp.float32)
    dot = lambda a, b: jnp.dot(a, b, preferred_element_type=jnp.float32)
    s_own = dot_t(own_ref[:high, :d], q)
    s_prev = dot_t(prev_ref[low:, :d], q) + bias
    p_own = dot_t(own_ref[:high, d:], g)
    p_prev = dot_t(prev_ref[low:, d:], g)
    s_diag = jnp.where(own_seen, s_own[low:], s_prev[:BLOCK])
    p_diag = jnp.where(own_seen, p_own[low:], p_prev[:BLOCK])
    s = jnp.concatenate([s_own[:low]] * below + [s_diag] + [s_prev[BLOCK:]] * above, 0)
    dp = jnp.concatenate([p_own[:low]] * below + [p_diag] + [p_prev[BLOCK:]] * above, 0)
    top = jnp.max(s, axis=0, keepdims=True)
    w = jnp.exp2((s - top) * (score_scale * LOG2_E))
    inverse = 1.0 / jnp.sum(w, axis=0, keepdims=True)
    delta = jnp.sum(w * dp, axis=0, keepdims=True) * inverse
    attention = w * inverse
    ds = (attention * (dp - delta)).astype(jnp.bfloat16)
    low_attention = attention.astype(jnp.bfloat16)
    split = lambda x: (
        jnp.concatenate([x[:low]] * below + [jnp.where(own_seen, x[low:high], zero)], 0),
        jnp.concatenate([jnp.where(own_seen, zero, x[low:high])] + [x[high:]] * above, 0),
    )
    ds_own, ds_prev = split(ds)
    at_own, at_prev = split(low_attention)
    own_grad_ref[:high, d:] += dot(at_own, g)
    prev_grad_ref[low:, d:] += dot(at_prev, g)
    own_grad_ref[:high, :d] += dot(ds_own, q)
    prev_grad_ref[low:, :d] += dot(ds_prev, q)
    dq_t = dot(own_kt_ref[:, :high], ds_own) + dot(prev_kt_ref[:, low:], ds_prev)
    return dq_t * score_scale


def attention_kernel(heads, steps, cores, phase, place_ref, own_ref, own_kt_ref, a_ref, b_ref, *refs):
    d = HEAD_SIZE
    count = 2 * heads
    half = heads * BLOCK
    first, core, head = place_ref[0], place_ref[1], place_ref[2]
    low_rows, high_rows = slice(0, half), slice(half, 2 * half)
    block_refs, refs = refs[: len(steps)], refs[len(steps) :]
    prev_ref, prev_kt_ref = a_ref, b_ref
    if phase == 0:
        prev_ref, prev_kt_ref, own_grad_ref, prev_grad_ref = refs[:4]
        dq_refs, (qd_ref, dq_ref) = refs[4:-2], refs[-2:]
        own_grad_ref[...] = jnp.zeros_like(own_grad_ref)
        prev_grad_ref[...] = jnp.zeros_like(prev_grad_ref)
        prev_ref[at(core * half, half)] = a_ref[...]
        prev_ref[at((1 - core) * half, half)] = b_ref[...]
        prev_kt_ref[...] = prev_ref[:, :d].T
    elif phase == 1:
        own_sums_ref, prev_sums_ref, own_grad_ref, prev_high_ref, back_ref, dq_out_ref = refs[:6]
        qd_ref, dq_ref, prev_grad_ref = refs[6:]
        own_grad_ref[...] = own_sums_ref[low_rows]
        prev_grad_ref[...] = prev_sums_ref[...]
    else:
        own_low_ref, own_sums_ref, prev_high_ref, dq_so_far_ref = refs[:4]
        dq_early_refs, refs = refs[4 : 4 + heads - len(steps)], refs[4 + heads - len(steps) :]
        own_a_ref, own_b_ref, back_ref = refs[:3]
        dq_refs, (qd_ref, dq_ref, own_grad_ref, prev_grad_ref) = refs[3:-4], refs[-4:]
        own_grad_ref[low_rows] = own_low_ref[...]
        own_grad_ref[high_rows] = own_sums_ref[high_rows]
        prev_grad_ref[high_rows] = prev_high_ref[...]
        dq_ref[:, :BLOCK] = dq_so_far_ref[...]
    for n, block_ref in enumerate(block_refs):
        qd_ref[n] = block_ref[: 2 * BLOCK]
    bias = jnp.where(first == 1, masked_value, 0.0).astype(jnp.float32)

    @pl.loop(0, len(steps))
    def _(n):
        step = steps[0] + n * (steps[-1] - steps[0]) // max(len(steps) - 1, 1)
        z_here = lax.rem(head + heads - step, heads)
        for z in range(heads):

            @pl.when(z_here == z)
            def _():
                for c in cores:
                    rows = slice(c * BLOCK, (c + 1) * BLOCK)
                    q = jnp.concatenate([qd_ref[n, rows, :d], qd_ref[n, rows, d : 2 * d]], 0)
                    g = jnp.concatenate([qd_ref[n, rows, 2 * d : 3 * d], qd_ref[n, rows, 3 * d :]], 0)
                    dq_t = attention_block(
                        c * heads + z, count, q, g, own_ref, prev_ref, own_kt_ref, prev_kt_ref,
                        own_grad_ref, prev_grad_ref, bias,
                    )
                    dq_ref[n, rows, :d] = dq_t[:, :BLOCK].T.astype(jnp.bfloat16)
                    dq_ref[n, rows, d:] = dq_t[:, BLOCK:].T.astype(jnp.bfloat16)

    def finish(ref, grad_ref, rows):
        ref[low_rows, :d] = (grad_ref[rows, :d] * score_scale).astype(ref.dtype)
        ref[low_rows, d:] = grad_ref[rows, d:].astype(ref.dtype)

    if phase == 0:
        for n, ref in enumerate(dq_refs):
            ref[...] = dq_ref[n]
    elif phase == 1:
        finish(back_ref, prev_grad_ref, low_rows)
        prev_high_ref[...] = prev_grad_ref[high_rows]
        dq_out_ref[...] = dq_ref[:, :BLOCK]
    else:
        finish(back_ref, prev_grad_ref, high_rows)
        finish(own_a_ref, own_grad_ref, low_rows)
        finish(own_b_ref, own_grad_ref, high_rows)
        for ref, early_ref in zip(dq_refs, dq_early_refs):
            ref[...] = early_ref[...]
        for n, ref in enumerate(dq_refs[len(dq_early_refs) :]):
            ref[...] = dq_ref[n]


def attention_backward(heads, place, own, near, far, blocks):
    half, d = heads * BLOCK, HEAD_SIZE
    whole = 2 * half
    low, wide = jnp.bfloat16, jnp.float32
    sums, half_sums, part = shape_of(wide, whole, 2 * d), shape_of(wide, half, 2 * d), shape_of(low, half, 2 * d)
    block = shape_of(low, 2 * BLOCK, 2 * d)
    early, late = steps_of(heads)[: heads // 2], steps_of(heads)[heads // 2 :]

    def run(steps, cores, phase, outs, operands, scratch):
        scratch = (
            pltpu.VMEM((len(steps), 2 * BLOCK, 4 * d), low),
            pltpu.VMEM((len(steps), 2 * BLOCK, 2 * d), low),
        ) + (pltpu.VMEM((whole, 2 * d), wide),) * scratch
        kernel = functools.partial(attention_kernel, heads, steps, cores, phase)
        return call(kernel, outs, (place,) + tuple(own) + tuple(operands), scratch, 1, 1, 32)

    outs = (shape_of(low, whole, 2 * d), shape_of(low, d, whole), sums, sums) + (block,) * len(early)
    outs = run(early, (0, 1), 0, outs, [near, far] + list(blocks[: len(early)]), 0)
    prev, (own_sums, prev_sums), dq_early = outs[:2], outs[2:4], outs[4:]
    late_blocks = tuple(blocks[len(early) :])
    wide_part = shape_of(low, half + 32, 2 * d)
    outs = (half_sums, half_sums, wide_part, shape_of(low, len(late), BLOCK, 2 * d))
    own_low, prev_high, back_a, dq_so_far = run(
        late, (0,), 1, outs, prev + late_blocks + (own_sums, prev_sums), 1
    )
    outs = run(
        late,
        (1,),
        2,
        (half_sums, half_sums, part) + (block,) * heads,
        prev + late_blocks + (own_low, own_sums, prev_high, dq_so_far) + dq_early,
        2,
    )
    return outs[:2], (back_a, outs[2]), outs[3:]


def moved(value, chips, heads, chip_step, flip, head_step):
    index = lambda chip, core, head: (chip * 2 + core) * heads + head
    pairs = [
        (index(chip, core, head), index(chip + chip_step, core ^ flip, (head + head_step) % heads))
        for chip in range(chips)
        for core in range(2)
        for head in range(heads)
        if 0 <= chip + chip_step < chips
    ]
    return lax.ppermute(value, ("chip", "core", "head"), pairs)


def on_device(query_rows, key_rows, saved_value_rows, out_grad):
    chips, heads = lax.axis_size("chip"), lax.axis_size("head")
    send = functools.partial(moved, chips=chips, heads=heads)
    rows, d, low = key_rows.shape[0], HEAD_SIZE, jnp.bfloat16
    bind = lambda kernel: functools.partial(kernel, heads)
    place = jnp.stack(
        [(lax.axis_index("chip") == 0).astype(jnp.int32), lax.axis_index("core"), lax.axis_index("head")]
    ).astype(jnp.int32)

    def spread(parts, way=1):
        steps = steps_of(heads)
        return (parts[0],) + tuple(
            send(parts[n], chip_step=0, flip=0, head_step=way * steps[n]) for n in range(1, heads)
        )

    across = functools.partial(send, head_step=0)
    slab = shape_of(low, rows, 4 * d)
    packed = copy_call(
        bind(pack_kernel),
        8 * heads,
        (slab,) * heads + (shape_of(low, heads, rows, 4 * d),) * 2,
        (place, key_rows, saved_value_rows, query_rows, out_grad),
    )
    kvs, (qd_mine, qd_other) = spread(packed[:heads]), packed[heads:]
    qd_other = across(qd_other, chip_step=0, flip=1)
    mine, other = call(bind(gather_kv_kernel), (shape_of(low, heads * rows, 2 * d),) * 2, (place,) + kvs)
    near = across(mine, chip_step=1, flip=0)
    far = across(other, chip_step=1, flip=1)
    blocks = call(
        bind(merge_rows_kernel),
        (shape_of(low, 2 * rows + 16, 4 * d),) * heads,
        (place, qd_mine, qd_other, mine[:8]),
    )
    blocks = spread(blocks)
    sibling = across(other, chip_step=0, flip=1)
    own = call(
        join_kernel,
        (shape_of(low, 2 * heads * rows, 2 * d), shape_of(low, d, 2 * heads * rows)),
        (place, mine, sibling),
    )
    own_sums, partial, dqs = attention_backward(heads, place, own, near, far, blocks)
    back = [across(part, chip_step=-1, flip=0) for part in partial]
    dqs = spread(dqs, -1)
    halves = shape_of(low, heads * rows, 2 * d)
    totals = spread(call(bind(add_kernel), (shape_of(low, 2 * rows, 2 * d),) * heads, (place, *own_sums, *back)))
    kv_mine, kv_other = call(bind(sort_kernel), (halves, halves), (place,) + totals)
    kv_sibling = across(kv_other, chip_step=0, flip=1)
    dq_mine, dq_other = call(
        bind(sort_kernel), (shape_of(low, heads * rows, 2 * d),) * 2, (place,) + tuple(dqs)
    )
    dq_sibling = across(dq_other, chip_step=0, flip=1)
    query_grad = copy_call(
        bind(unpack_dq_kernel), 2 * heads, shape_of(low, *query_rows.shape), (place, dq_mine, dq_sibling)
    )
    key_grad, value_grad = call(
        bind(unpack_kv_kernel), (shape_of(low, *key_rows.shape),) * 2, (place, kv_mine, kv_sibling)
    )
    return query_grad, key_grad, value_grad


def solution(mesh):
    heads = mesh.shape["head"]
    devices = mesh.devices.reshape(-1, 2, heads)
    fine_mesh = Mesh(devices, ("chip", "core", "head"))
    rows = P(("chip", "core", "head"), None)
    return jax.shard_map(
        on_device,
        mesh=fine_mesh,
        in_specs=(rows,) * 4,
        out_specs=(rows,) * 3,
        check_vma=False,
    )
```

```python
import functools

import jax
import jax.numpy as jnp
from jax import lax
from jax.experimental import pallas as pl
from jax.experimental.pallas import tpu as pltpu
from jax.sharding import Mesh
from jax.sharding import PartitionSpec as P

HEAD_SIZE = 128
BLOCK = 128
LOG2_E = 1.4426950408889634

score_scale = 168.0 ** (-0.5)
masked_value = -1e30
contract_last = (((1,), (1,)), ((), ()))
VMEM_SPEC = pl.BlockSpec(memory_space=pltpu.VMEM)
ANY_SPEC = pl.BlockSpec(memory_space=pl.ANY)
SMEM_SPEC = pl.BlockSpec(memory_space=pltpu.SMEM)


def call(kernel, out_shape, operands, scratch=(), flops=0, transcendentals=0, vmem=16, spec=VMEM_SPEC, out_spec=VMEM_SPEC):
    outs = out_shape if isinstance(out_shape, tuple) else (out_shape,)
    moved = sum(a.size * a.dtype.itemsize for a in operands + outs)
    return pl.pallas_call(
        kernel,
        out_shape=out_shape,
        in_specs=[SMEM_SPEC] + [spec] * (len(operands) - 1),
        out_specs=jax.tree.map(lambda _: out_spec, out_shape),
        scratch_shapes=list(scratch),
        compiler_params=pltpu.CompilerParams(vmem_limit_bytes=vmem * 2**20),
        cost_estimate=pl.CostEstimate(flops=flops, bytes_accessed=moved, transcendentals=transcendentals),
    )(*operands)


def copy_call(kernel, copies, out_shape, operands):
    return call(kernel, out_shape, operands, (pltpu.SemaphoreType.DMA((copies,)),), spec=ANY_SPEC, out_spec=ANY_SPEC)


def shape_of(dtype, *shape):
    return jax.ShapeDtypeStruct(shape, dtype)


def at(start, size):
    return pl.ds(pl.multiple_of(start, size), size)


def copied(sems, pairs):
    copies = [pltpu.make_async_copy(src, dst, sems.at[n]) for n, (src, dst) in enumerate(pairs)]
    for copy in copies:
        copy.start()
    for copy in copies:
        copy.wait()


def steps_of(heads):
    return (0,) + tuple(sorted(range(1, heads), key=lambda k: -min(k, heads - k)))


def onward(place_ref, heads, n):
    return lax.rem(place_ref[2] + steps_of(heads)[n], heads)


def source(place_ref, heads, n):
    return lax.rem(place_ref[2] + heads - steps_of(heads)[n], heads)


def pack_kv_kernel(heads, place_ref, k_ref, v_ref, *refs):
    out_refs, sems = refs[:-1], refs[-1]
    core = place_ref[1]
    d = HEAD_SIZE
    pairs = []
    for k, out_ref in enumerate(out_refs):
        z = onward(place_ref, heads, k)
        for n, g in enumerate((2 * z + core, 2 * z + 1 - core)):
            columns = at(g * d, d)
            pairs.append((k_ref.at[:, columns], out_ref.at[:, pl.ds(2 * n * d, d)]))
            pairs.append((v_ref.at[:, columns], out_ref.at[:, pl.ds((2 * n + 1) * d, d)]))
    copied(sems, pairs)


def pack_qd_kernel(heads, place_ref, q_ref, g_ref, mine_ref, other_ref, sems):
    core = place_ref[1]
    width = 2 * HEAD_SIZE
    pairs = []
    for ref, c in ((other_ref, 1 - core), (mine_ref, core)):
        for k in range(heads):
            columns = at((2 * onward(place_ref, heads, k) + c) * width, width)
            pairs.append((q_ref.at[:, columns], ref.at[k, :, pl.ds(0, width)]))
            pairs.append((g_ref.at[:, columns], ref.at[k, :, pl.ds(width, width)]))
    copied(sems, pairs)


def gather_kv_kernel(heads, place_ref, *refs):
    in_refs, (mine_ref, other_ref) = refs[:heads], refs[heads:]
    width = 2 * HEAD_SIZE
    for k, in_ref in enumerate(in_refs):
        rows = at(source(place_ref, heads, k) * BLOCK, BLOCK)
        mine_ref[rows] = in_ref[:, :width]
        other_ref[rows] = in_ref[:, width:]


def join_kernel(place_ref, mine_ref, sibling_ref, out_ref, kt_ref):
    core = place_ref[1]
    half = mine_ref.shape[0]
    out_ref[at(core * half, half)] = mine_ref[...]
    out_ref[at((1 - core) * half, half)] = sibling_ref[...]
    kt_ref[...] = out_ref[:, :HEAD_SIZE].T


def merge_rows_kernel(heads, place_ref, mine_ref, other_ref, after_ref, *out_refs):
    core = place_ref[1]
    for k, out_ref in enumerate(out_refs):
        out_ref[at(core * BLOCK, BLOCK)] = mine_ref[k]
        out_ref[at((1 - core) * BLOCK, BLOCK)] = other_ref[k]


def sort_kernel(heads, place_ref, *refs):
    in_refs, (mine_ref, other_ref) = refs[:heads], refs[heads:]
    core = place_ref[1]
    for k, in_ref in enumerate(in_refs):
        mine_ref[k * BLOCK : (k + 1) * BLOCK] = in_ref[at(core * BLOCK, BLOCK)]
        other_ref[k * BLOCK : (k + 1) * BLOCK] = in_ref[at((1 - core) * BLOCK, BLOCK)]


def unpack_dq_kernel(heads, place_ref, mine_ref, sibling_ref, out_ref, sems):
    core = place_ref[1]
    width = 2 * HEAD_SIZE
    pairs = []
    for k in range(heads):
        z = onward(place_ref, heads, k)
        for ref, c in ((mine_ref, core), (sibling_ref, 1 - core)):
            rows = pl.ds(k * BLOCK, BLOCK)
            pairs.append((ref.at[rows], out_ref.at[:, at((2 * z + c) * width, width)]))
    copied(sems, pairs)


def unpack_kv_kernel(heads, place_ref, mine_ref, sibling_ref, k_ref, v_ref):
    core = place_ref[1]
    d = HEAD_SIZE
    for k in range(heads):
        z = source(place_ref, heads, k)
        rows = slice(k * BLOCK, (k + 1) * BLOCK)
        for ref, c in ((mine_ref, core), (sibling_ref, 1 - core)):
            columns = at((2 * z + c) * d, d)
            k_ref[:, columns] = ref[rows, :d]
            v_ref[:, columns] = ref[rows, d:]


def add_kernel(heads, place_ref, own_a_ref, own_b_ref, back_a_ref, back_b_ref, *out_refs):
    for k, out_ref in enumerate(out_refs):
        rows = at(onward(place_ref, heads, k) * BLOCK, BLOCK)
        for c, (own_ref, back_ref) in enumerate(((own_a_ref, back_a_ref), (own_b_ref, back_b_ref))):
            total = own_ref[rows] + back_ref[rows].astype(jnp.float32)
            out_ref[c * BLOCK : (c + 1) * BLOCK] = total.astype(jnp.bfloat16)


def attention_block(i, count, q, g, own_ref, prev_ref, own_kt_ref, prev_kt_ref, own_grad_ref, prev_grad_ref, bias):
    d = HEAD_SIZE
    low, high = i * BLOCK, (i + 1) * BLOCK
    below, above = i > 0, i < count - 1
    key_row = lax.broadcasted_iota(jnp.int32, (BLOCK, 2 * BLOCK), 0)
    query_row = lax.broadcasted_iota(jnp.int32, (BLOCK, 2 * BLOCK), 1) % BLOCK
    own_seen = key_row <= query_row
    zero = jnp.zeros((BLOCK, 2 * BLOCK), jnp.bfloat16)
    dot_t = lambda a, b: lax.dot_general(a, b, contract_last, preferred_element_type=jnp.float32)
    dot = lambda a, b: jnp.dot(a, b, preferred_element_type=jnp.float32)
    s_own = dot_t(own_ref[:high, :d], q)
    s_prev = dot_t(prev_ref[low:, :d], q) + bias
    p_own = dot_t(own_ref[:high, d:], g)
    p_prev = dot_t(prev_ref[low:, d:], g)
    s_diag = jnp.where(own_seen, s_own[low:], s_prev[:BLOCK])
    p_diag = jnp.where(own_seen, p_own[low:], p_prev[:BLOCK])
    s = jnp.concatenate([s_own[:low]] * below + [s_diag] + [s_prev[BLOCK:]] * above, 0)
    dp = jnp.concatenate([p_own[:low]] * below + [p_diag] + [p_prev[BLOCK:]] * above, 0)
    top = jnp.max(s, axis=0, keepdims=True)
    w = jnp.exp2((s - top) * (score_scale * LOG2_E))
    inverse = 1.0 / jnp.sum(w, axis=0, keepdims=True)
    delta = jnp.sum(w * dp, axis=0, keepdims=True) * inverse
    attention = w * inverse
    ds = (attention * (dp - delta)).astype(jnp.bfloat16)
    low_attention = attention.astype(jnp.bfloat16)
    split = lambda x: (
        jnp.concatenate([x[:low]] * below + [jnp.where(own_seen, x[low:high], zero)], 0),
        jnp.concatenate([jnp.where(own_seen, zero, x[low:high])] + [x[high:]] * above, 0),
    )
    ds_own, ds_prev = split(ds)
    at_own, at_prev = split(low_attention)
    own_grad_ref[:high, d:] += dot(at_own, g)
    prev_grad_ref[low:, d:] += dot(at_prev, g)
    own_grad_ref[:high, :d] += dot(ds_own, q)
    prev_grad_ref[low:, :d] += dot(ds_prev, q)
    dq_t = dot(own_kt_ref[:, :high], ds_own) + dot(prev_kt_ref[:, low:], ds_prev)
    return dq_t * score_scale


def attention_kernel(heads, steps, cores, phase, place_ref, own_ref, own_kt_ref, a_ref, b_ref, *refs):
    d = HEAD_SIZE
    count = 2 * heads
    half = heads * BLOCK
    first, core, head = place_ref[0], place_ref[1], place_ref[2]
    low_rows, high_rows = slice(0, half), slice(half, 2 * half)
    block_refs, refs = refs[: len(steps)], refs[len(steps) :]
    prev_ref, prev_kt_ref = a_ref, b_ref
    if phase == 0:
        prev_ref, prev_kt_ref, own_grad_ref, prev_grad_ref = refs[:4]
        dq_refs, (qd_ref, dq_ref) = refs[4:-2], refs[-2:]
        own_grad_ref[...] = jnp.zeros_like(own_grad_ref)
        prev_grad_ref[...] = jnp.zeros_like(prev_grad_ref)
        prev_ref[at(core * half, half)] = a_ref[...]
        prev_ref[at((1 - core) * half, half)] = b_ref[...]
        prev_kt_ref[...] = prev_ref[:, :d].T
    elif phase == 1:
        own_sums_ref, prev_sums_ref, own_grad_ref, prev_high_ref, back_ref, dq_out_ref = refs[:6]
        qd_ref, dq_ref, prev_grad_ref = refs[6:]
        own_grad_ref[...] = own_sums_ref[low_rows]
        prev_grad_ref[...] = prev_sums_ref[...]
    else:
        own_low_ref, own_sums_ref, prev_high_ref, dq_so_far_ref, after_ref = refs[:5]
        own_a_ref, own_b_ref, back_ref = refs[5:8]
        dq_refs, (qd_ref, dq_ref, own_grad_ref, prev_grad_ref) = refs[8:-4], refs[-4:]
        own_grad_ref[low_rows] = own_low_ref[...]
        own_grad_ref[high_rows] = own_sums_ref[high_rows]
        prev_grad_ref[high_rows] = prev_high_ref[...]
        dq_ref[:, :BLOCK] = dq_so_far_ref[...]
    for n, block_ref in enumerate(block_refs):
        qd_ref[n] = block_ref[: 2 * BLOCK]
    bias = jnp.where(first == 1, masked_value, 0.0).astype(jnp.float32)

    @pl.loop(0, len(steps))
    def _(n):
        step = steps[0] + n * (steps[-1] - steps[0]) // max(len(steps) - 1, 1)
        z_here = lax.rem(head + heads - step, heads)
        for z in range(heads):

            @pl.when(z_here == z)
            def _():
                for c in cores:
                    rows = slice(c * BLOCK, (c + 1) * BLOCK)
                    q = jnp.concatenate([qd_ref[n, rows, :d], qd_ref[n, rows, d : 2 * d]], 0)
                    g = jnp.concatenate([qd_ref[n, rows, 2 * d : 3 * d], qd_ref[n, rows, 3 * d :]], 0)
                    dq_t = attention_block(
                        c * heads + z, count, q, g, own_ref, prev_ref, own_kt_ref, prev_kt_ref,
                        own_grad_ref, prev_grad_ref, bias,
                    )
                    dq_ref[n, rows, :d] = dq_t[:, :BLOCK].T.astype(jnp.bfloat16)
                    dq_ref[n, rows, d:] = dq_t[:, BLOCK:].T.astype(jnp.bfloat16)

    def finish(ref, grad_ref, rows):
        ref[low_rows, :d] = (grad_ref[rows, :d] * score_scale).astype(ref.dtype)
        ref[low_rows, d:] = grad_ref[rows, d:].astype(ref.dtype)

    if phase == 0:
        for n, ref in enumerate(dq_refs):
            ref[...] = dq_ref[n]
    elif phase == 1:
        finish(back_ref, prev_grad_ref, low_rows)
        prev_high_ref[...] = prev_grad_ref[high_rows]
        dq_out_ref[...] = dq_ref[:, :BLOCK]
    else:
        finish(back_ref, prev_grad_ref, high_rows)
        finish(own_a_ref, own_grad_ref, low_rows)
        finish(own_b_ref, own_grad_ref, high_rows)
        for n, ref in enumerate(dq_refs):
            ref[...] = dq_ref[n]


def attention_backward(heads, place, own, near, far, blocks, home):
    half, d = heads * BLOCK, HEAD_SIZE
    whole = 2 * half
    low, wide = jnp.bfloat16, jnp.float32
    sums, half_sums, part = shape_of(wide, whole, 2 * d), shape_of(wide, half, 2 * d), shape_of(low, half, 2 * d)
    block = shape_of(low, 2 * BLOCK, 2 * d)
    early, late = steps_of(heads)[: heads // 2], steps_of(heads)[heads // 2 :]

    def run(steps, cores, phase, outs, operands, scratch):
        scratch = (
            pltpu.VMEM((len(steps), 2 * BLOCK, 4 * d), low),
            pltpu.VMEM((len(steps), 2 * BLOCK, 2 * d), low),
        ) + (pltpu.VMEM((whole, 2 * d), wide),) * scratch
        kernel = functools.partial(attention_kernel, heads, steps, cores, phase)
        return call(kernel, outs, (place,) + tuple(own) + tuple(operands), scratch, 1, 1, 32)

    outs = (shape_of(low, whole, 2 * d), shape_of(low, d, whole), sums, sums) + (block,) * len(early)
    outs = run(early, (0, 1), 0, outs, [near, far] + list(blocks[: len(early)]), 0)
    prev, (own_sums, prev_sums), dq_early = outs[:2], outs[2:4], outs[4:]
    dq_early = (dq_early[0],) + tuple(home(dq_early[n], early[n]) for n in range(1, len(early)))
    late_blocks = tuple(blocks[len(early) :])
    wide_part = shape_of(low, half + 32, 2 * d)
    outs = (half_sums, half_sums, wide_part, shape_of(low, len(late), BLOCK, 2 * d))
    own_low, prev_high, back_a, dq_so_far = run(
        late, (0,), 1, outs, prev + late_blocks + (own_sums, prev_sums), 1
    )
    outs = run(
        late,
        (1,),
        2,
        (half_sums, half_sums, part) + (block,) * len(late),
        prev + late_blocks + (own_low, own_sums, prev_high, dq_so_far, dq_early[-1][:16]),
        2,
    )
    dq_late = tuple(home(dq, step) for dq, step in zip(outs[3:], late))
    return outs[:2], (back_a, outs[2]), dq_early + dq_late


def moved(value, chips, heads, chip_step, flip, head_step):
    index = lambda chip, core, head: (chip * 2 + core) * heads + head
    pairs = [
        (index(chip, core, head), index(chip + chip_step, core ^ flip, (head + head_step) % heads))
        for chip in range(chips)
        for core in range(2)
        for head in range(heads)
        if 0 <= chip + chip_step < chips
    ]
    return lax.ppermute(value, ("chip", "core", "head"), pairs)


def on_device(query_rows, key_rows, saved_value_rows, out_grad):
    chips, heads = lax.axis_size("chip"), lax.axis_size("head")
    send = functools.partial(moved, chips=chips, heads=heads)
    rows, d, low = key_rows.shape[0], HEAD_SIZE, jnp.bfloat16
    bind = lambda kernel: functools.partial(kernel, heads)
    place = jnp.stack(
        [(lax.axis_index("chip") == 0).astype(jnp.int32), lax.axis_index("core"), lax.axis_index("head")]
    ).astype(jnp.int32)

    def ship(value, head_step):
        return send(value, chip_step=0, flip=0, head_step=head_step)

    def spread(parts):
        return (parts[0],) + tuple(ship(parts[n], steps_of(heads)[n]) for n in range(1, heads))

    across = functools.partial(send, head_step=0)
    slab = shape_of(low, rows, 4 * d)
    kvs = spread(
        copy_call(bind(pack_kv_kernel), 4 * heads, (slab,) * heads, (place, key_rows, saved_value_rows))
    )
    qd_mine, qd_other = copy_call(
        bind(pack_qd_kernel),
        4 * heads,
        (shape_of(low, heads, rows, 4 * d),) * 2,
        (place, query_rows, out_grad),
    )
    qd_other = across(qd_other, chip_step=0, flip=1)
    mine, other = call(bind(gather_kv_kernel), (shape_of(low, heads * rows, 2 * d),) * 2, (place,) + kvs)
    near = across(mine, chip_step=1, flip=0)
    far = across(other, chip_step=1, flip=1)
    blocks = call(
        bind(merge_rows_kernel),
        (shape_of(low, 2 * rows + 16, 4 * d),) * heads,
        (place, qd_mine, qd_other, mine[:8]),
    )
    blocks = spread(blocks)
    sibling = across(other, chip_step=0, flip=1)
    own = call(
        join_kernel,
        (shape_of(low, 2 * heads * rows, 2 * d), shape_of(low, d, 2 * heads * rows)),
        (place, mine, sibling),
    )
    own_sums, partial, dqs = attention_backward(
        heads, place, own, near, far, blocks, lambda dq, step: ship(dq, -step)
    )
    back = [across(part, chip_step=-1, flip=0) for part in partial]
    halves = shape_of(low, heads * rows, 2 * d)
    totals = spread(call(bind(add_kernel), (shape_of(low, 2 * rows, 2 * d),) * heads, (place, *own_sums, *back)))
    kv_mine, kv_other = call(bind(sort_kernel), (halves, halves), (place,) + totals)
    kv_sibling = across(kv_other, chip_step=0, flip=1)
    dq_mine, dq_other = call(
        bind(sort_kernel), (shape_of(low, heads * rows, 2 * d),) * 2, (place,) + tuple(dqs)
    )
    dq_sibling = across(dq_other, chip_step=0, flip=1)
    query_grad = copy_call(
        bind(unpack_dq_kernel), 2 * heads, shape_of(low, *query_rows.shape), (place, dq_mine, dq_sibling)
    )
    key_grad, value_grad = call(
        bind(unpack_kv_kernel), (shape_of(low, *key_rows.shape),) * 2, (place, kv_mine, kv_sibling)
    )
    return query_grad, key_grad, value_grad


def solution(mesh):
    heads = mesh.shape["head"]
    devices = mesh.devices.reshape(-1, 2, heads)
    fine_mesh = Mesh(devices, ("chip", "core", "head"))
    rows = P(("chip", "core", "head"), None)
    return jax.shard_map(
        on_device,
        mesh=fine_mesh,
        in_specs=(rows,) * 4,
        out_specs=(rows,) * 3,
        check_vma=False,
    )
```

```python
import functools

import jax
import jax.numpy as jnp
from jax import lax
from jax.experimental import pallas as pl
from jax.experimental.pallas import tpu as pltpu
from jax.sharding import Mesh
from jax.sharding import PartitionSpec as P

HEAD_SIZE = 128
BLOCK = 128
LOG2_E = 1.4426950408889634

score_scale = 168.0 ** (-0.5)
masked_value = -1e30
contract_last = (((1,), (1,)), ((), ()))
VMEM_SPEC = pl.BlockSpec(memory_space=pltpu.VMEM)
ANY_SPEC = pl.BlockSpec(memory_space=pl.ANY)
SMEM_SPEC = pl.BlockSpec(memory_space=pltpu.SMEM)


def call(kernel, out_shape, operands, scratch=(), flops=0, transcendentals=0, vmem=16, spec=VMEM_SPEC, out_spec=VMEM_SPEC):
    outs = out_shape if isinstance(out_shape, tuple) else (out_shape,)
    moved = sum(a.size * a.dtype.itemsize for a in operands + outs)
    return pl.pallas_call(
        kernel,
        out_shape=out_shape,
        in_specs=[SMEM_SPEC] + [spec] * (len(operands) - 1),
        out_specs=jax.tree.map(lambda _: out_spec, out_shape),
        scratch_shapes=list(scratch),
        compiler_params=pltpu.CompilerParams(vmem_limit_bytes=vmem * 2**20),
        cost_estimate=pl.CostEstimate(flops=flops, bytes_accessed=moved, transcendentals=transcendentals),
    )(*operands)


def copy_call(kernel, copies, out_shape, operands):
    return call(kernel, out_shape, operands, (pltpu.SemaphoreType.DMA((copies,)),), spec=ANY_SPEC, out_spec=ANY_SPEC)


def shape_of(dtype, *shape):
    return jax.ShapeDtypeStruct(shape, dtype)


def at(start, size):
    return pl.ds(pl.multiple_of(start, size), size)


def copied(sems, pairs):
    copies = [pltpu.make_async_copy(src, dst, sems.at[n]) for n, (src, dst) in enumerate(pairs)]
    for copy in copies:
        copy.start()
    for copy in copies:
        copy.wait()


def steps_of(heads):
    return (0,) + tuple(sorted(range(1, heads), key=lambda k: -min(k, heads - k)))


def onward(place_ref, heads, n):
    return lax.rem(place_ref[2] + steps_of(heads)[n], heads)


def source(place_ref, heads, n):
    return lax.rem(place_ref[2] + heads - steps_of(heads)[n], heads)


def pack_kv_kernel(heads, place_ref, k_ref, v_ref, *refs):
    out_refs, sems = refs[:-1], refs[-1]
    core = place_ref[1]
    d = HEAD_SIZE
    pairs = []
    for k, out_ref in enumerate(out_refs):
        z = onward(place_ref, heads, k)
        for n, g in enumerate((2 * z + core, 2 * z + 1 - core)):
            columns = at(g * d, d)
            pairs.append((k_ref.at[:, columns], out_ref.at[:, pl.ds(2 * n * d, d)]))
            pairs.append((v_ref.at[:, columns], out_ref.at[:, pl.ds((2 * n + 1) * d, d)]))
    copied(sems, pairs)


def pack_qd_kernel(heads, place_ref, q_ref, g_ref, mine_ref, *refs):
    other_refs, sems = refs[:heads], refs[heads]
    core = place_ref[1]
    width = 2 * HEAD_SIZE
    pairs = []
    for k in range(heads):
        for ref, c in ((other_refs[k], 1 - core), (mine_ref.at[k], core)):
            columns = at((2 * onward(place_ref, heads, k) + c) * width, width)
            pairs.append((q_ref.at[:, columns], ref.at[:, pl.ds(0, width)]))
            pairs.append((g_ref.at[:, columns], ref.at[:, pl.ds(width, width)]))
    copied(sems, pairs)


def gather_kv_kernel(heads, place_ref, *refs):
    in_refs, (mine_ref, other_ref) = refs[:heads], refs[heads:]
    width = 2 * HEAD_SIZE
    for k, in_ref in enumerate(in_refs):
        rows = at(source(place_ref, heads, k) * BLOCK, BLOCK)
        mine_ref[rows] = in_ref[:, :width]
        other_ref[rows] = in_ref[:, width:]


def join_kernel(place_ref, mine_ref, sibling_ref, out_ref, kt_ref):
    core = place_ref[1]
    half = mine_ref.shape[0]
    out_ref[at(core * half, half)] = mine_ref[...]
    out_ref[at((1 - core) * half, half)] = sibling_ref[...]
    kt_ref[...] = out_ref[:, :HEAD_SIZE].T


def merge_rows_kernel(heads, place_ref, mine_ref, *refs):
    other_refs, out_refs = refs[:heads], refs[heads + 1 :]
    core = place_ref[1]
    for k, out_ref in enumerate(out_refs):
        out_ref[at(core * BLOCK, BLOCK)] = mine_ref[k]
        out_ref[at((1 - core) * BLOCK, BLOCK)] = other_refs[k][...]


def sort_kernel(heads, place_ref, *refs):
    in_refs, (mine_ref, other_ref) = refs[:heads], refs[heads:]
    core = place_ref[1]
    for k, in_ref in enumerate(in_refs):
        mine_ref[k * BLOCK : (k + 1) * BLOCK] = in_ref[at(core * BLOCK, BLOCK)]
        other_ref[k * BLOCK : (k + 1) * BLOCK] = in_ref[at((1 - core) * BLOCK, BLOCK)]


def unpack_dq_kernel(heads, place_ref, mine_ref, sibling_ref, out_ref, sems):
    core = place_ref[1]
    width = 2 * HEAD_SIZE
    pairs = []
    for k in range(heads):
        z = onward(place_ref, heads, k)
        for ref, c in ((mine_ref, core), (sibling_ref, 1 - core)):
            rows = pl.ds(k * BLOCK, BLOCK)
            pairs.append((ref.at[rows], out_ref.at[:, at((2 * z + c) * width, width)]))
    copied(sems, pairs)


def unpack_kv_kernel(heads, place_ref, mine_ref, sibling_ref, k_ref, v_ref):
    core = place_ref[1]
    d = HEAD_SIZE
    for k in range(heads):
        z = source(place_ref, heads, k)
        rows = slice(k * BLOCK, (k + 1) * BLOCK)
        for ref, c in ((mine_ref, core), (sibling_ref, 1 - core)):
            columns = at((2 * z + c) * d, d)
            k_ref[:, columns] = ref[rows, :d]
            v_ref[:, columns] = ref[rows, d:]


def add_kernel(heads, place_ref, own_a_ref, own_b_ref, back_a_ref, back_b_ref, *out_refs):
    for k, out_ref in enumerate(out_refs):
        rows = at(onward(place_ref, heads, k) * BLOCK, BLOCK)
        for c, (own_ref, back_ref) in enumerate(((own_a_ref, back_a_ref), (own_b_ref, back_b_ref))):
            total = own_ref[rows] + back_ref[rows].astype(jnp.float32)
            out_ref[c * BLOCK : (c + 1) * BLOCK] = total.astype(jnp.bfloat16)


def attention_block(i, count, q, g, own_ref, prev_ref, own_kt_ref, prev_kt_ref, own_grad_ref, prev_grad_ref, bias):
    d = HEAD_SIZE
    low, high = i * BLOCK, (i + 1) * BLOCK
    below, above = i > 0, i < count - 1
    key_row = lax.broadcasted_iota(jnp.int32, (BLOCK, 2 * BLOCK), 0)
    query_row = lax.broadcasted_iota(jnp.int32, (BLOCK, 2 * BLOCK), 1) % BLOCK
    own_seen = key_row <= query_row
    zero = jnp.zeros((BLOCK, 2 * BLOCK), jnp.bfloat16)
    dot_t = lambda a, b: lax.dot_general(a, b, contract_last, preferred_element_type=jnp.float32)
    dot = lambda a, b: jnp.dot(a, b, preferred_element_type=jnp.float32)
    s_own = dot_t(own_ref[:high, :d], q)
    s_prev = dot_t(prev_ref[low:, :d], q) + bias
    p_own = dot_t(own_ref[:high, d:], g)
    p_prev = dot_t(prev_ref[low:, d:], g)
    s_diag = jnp.where(own_seen, s_own[low:], s_prev[:BLOCK])
    p_diag = jnp.where(own_seen, p_own[low:], p_prev[:BLOCK])
    s = jnp.concatenate([s_own[:low]] * below + [s_diag] + [s_prev[BLOCK:]] * above, 0)
    dp = jnp.concatenate([p_own[:low]] * below + [p_diag] + [p_prev[BLOCK:]] * above, 0)
    top = jnp.max(s, axis=0, keepdims=True)
    w = jnp.exp2((s - top) * (score_scale * LOG2_E))
    inverse = 1.0 / jnp.sum(w, axis=0, keepdims=True)
    delta = jnp.sum(w * dp, axis=0, keepdims=True) * inverse
    attention = w * inverse
    ds = (attention * (dp - delta)).astype(jnp.bfloat16)
    low_attention = attention.astype(jnp.bfloat16)
    split = lambda x: (
        jnp.concatenate([x[:low]] * below + [jnp.where(own_seen, x[low:high], zero)], 0),
        jnp.concatenate([jnp.where(own_seen, zero, x[low:high])] + [x[high:]] * above, 0),
    )
    ds_own, ds_prev = split(ds)
    at_own, at_prev = split(low_attention)
    own_grad_ref[:high, d:] += dot(at_own, g)
    prev_grad_ref[low:, d:] += dot(at_prev, g)
    own_grad_ref[:high, :d] += dot(ds_own, q)
    prev_grad_ref[low:, :d] += dot(ds_prev, q)
    dq_t = dot(own_kt_ref[:, :high], ds_own) + dot(prev_kt_ref[:, low:], ds_prev)
    return dq_t * score_scale


def attention_kernel(heads, steps, cores, phase, place_ref, own_ref, own_kt_ref, a_ref, b_ref, *refs):
    d = HEAD_SIZE
    count = 2 * heads
    half = heads * BLOCK
    first, core, head = place_ref[0], place_ref[1], place_ref[2]
    low_rows, high_rows = slice(0, half), slice(half, 2 * half)
    block_refs, refs = refs[: len(steps)], refs[len(steps) :]
    prev_ref, prev_kt_ref = a_ref, b_ref
    if phase == 0:
        prev_ref, prev_kt_ref, own_grad_ref, prev_grad_ref = refs[:4]
        dq_refs, (qd_ref, dq_ref) = refs[4:-2], refs[-2:]
        own_grad_ref[...] = jnp.zeros_like(own_grad_ref)
        prev_grad_ref[...] = jnp.zeros_like(prev_grad_ref)
        prev_ref[at(core * half, half)] = a_ref[...]
        prev_ref[at((1 - core) * half, half)] = b_ref[...]
        prev_kt_ref[...] = prev_ref[:, :d].T
    elif phase == 1:
        own_sums_ref, prev_sums_ref, own_grad_ref, prev_high_ref, back_ref, dq_out_ref = refs[:6]
        qd_ref, dq_ref, prev_grad_ref = refs[6:]
        own_grad_ref[...] = own_sums_ref[low_rows]
        prev_grad_ref[...] = prev_sums_ref[...]
    else:
        own_low_ref, own_sums_ref, prev_high_ref, dq_so_far_ref, after_ref = refs[:5]
        own_a_ref, own_b_ref, back_ref = refs[5:8]
        dq_refs, (qd_ref, dq_ref, own_grad_ref, prev_grad_ref) = refs[8:-4], refs[-4:]
        own_grad_ref[low_rows] = own_low_ref[...]
        own_grad_ref[high_rows] = own_sums_ref[high_rows]
        prev_grad_ref[high_rows] = prev_high_ref[...]
        dq_ref[:, :BLOCK] = dq_so_far_ref[...]
    for n, block_ref in enumerate(block_refs):
        qd_ref[n] = block_ref[: 2 * BLOCK]
    bias = jnp.where(first == 1, masked_value, 0.0).astype(jnp.float32)

    @pl.loop(0, len(steps))
    def _(n):
        step = steps[0] + n * (steps[-1] - steps[0]) // max(len(steps) - 1, 1)
        z_here = lax.rem(head + heads - step, heads)
        for z in range(heads):

            @pl.when(z_here == z)
            def _():
                for c in cores:
                    rows = slice(c * BLOCK, (c + 1) * BLOCK)
                    q = jnp.concatenate([qd_ref[n, rows, :d], qd_ref[n, rows, d : 2 * d]], 0)
                    g = jnp.concatenate([qd_ref[n, rows, 2 * d : 3 * d], qd_ref[n, rows, 3 * d :]], 0)
                    dq_t = attention_block(
                        c * heads + z, count, q, g, own_ref, prev_ref, own_kt_ref, prev_kt_ref,
                        own_grad_ref, prev_grad_ref, bias,
                    )
                    dq_ref[n, rows, :d] = dq_t[:, :BLOCK].T.astype(jnp.bfloat16)
                    dq_ref[n, rows, d:] = dq_t[:, BLOCK:].T.astype(jnp.bfloat16)

    def finish(ref, grad_ref, rows):
        ref[low_rows, :d] = (grad_ref[rows, :d] * score_scale).astype(ref.dtype)
        ref[low_rows, d:] = grad_ref[rows, d:].astype(ref.dtype)

    if phase == 0:
        for n, ref in enumerate(dq_refs):
            ref[...] = dq_ref[n]
    elif phase == 1:
        finish(back_ref, prev_grad_ref, low_rows)
        prev_high_ref[...] = prev_grad_ref[high_rows]
        dq_out_ref[...] = dq_ref[:, :BLOCK]
    else:
        finish(back_ref, prev_grad_ref, high_rows)
        finish(own_a_ref, own_grad_ref, low_rows)
        finish(own_b_ref, own_grad_ref, high_rows)
        for n, ref in enumerate(dq_refs):
            ref[...] = dq_ref[n]


def attention_backward(heads, place, own, near, far, blocks, home):
    half, d = heads * BLOCK, HEAD_SIZE
    whole = 2 * half
    low, wide = jnp.bfloat16, jnp.float32
    sums, half_sums, part = shape_of(wide, whole, 2 * d), shape_of(wide, half, 2 * d), shape_of(low, half, 2 * d)
    block = shape_of(low, 2 * BLOCK, 2 * d)
    early, late = steps_of(heads)[: heads // 2], steps_of(heads)[heads // 2 :]

    def run(steps, cores, phase, outs, operands, scratch):
        scratch = (
            pltpu.VMEM((len(steps), 2 * BLOCK, 4 * d), low),
            pltpu.VMEM((len(steps), 2 * BLOCK, 2 * d), low),
        ) + (pltpu.VMEM((whole, 2 * d), wide),) * scratch
        kernel = functools.partial(attention_kernel, heads, steps, cores, phase)
        return call(kernel, outs, (place,) + tuple(own) + tuple(operands), scratch, 1, 1, 32)

    outs = (shape_of(low, whole, 2 * d), shape_of(low, d, whole), sums, sums) + (block,) * len(early)
    outs = run(early, (0, 1), 0, outs, [near, far] + list(blocks[: len(early)]), 0)
    prev, (own_sums, prev_sums), dq_early = outs[:2], outs[2:4], outs[4:]
    dq_early = (dq_early[0],) + tuple(home(dq_early[n], early[n]) for n in range(1, len(early)))
    late_blocks = tuple(blocks[len(early) :])
    wide_part = shape_of(low, half + 16, 2 * d)
    outs = (half_sums, half_sums, wide_part, shape_of(low, len(late), BLOCK, 2 * d))
    own_low, prev_high, back_a, dq_so_far = run(
        late, (0,), 1, outs, prev + late_blocks + (own_sums, prev_sums), 1
    )
    outs = run(
        late,
        (1,),
        2,
        (half_sums, half_sums, part) + (block,) * len(late),
        prev + late_blocks + (own_low, own_sums, prev_high, dq_so_far, dq_early[-1][:16]),
        2,
    )
    dq_late = tuple(home(dq, step) for dq, step in zip(outs[3:], late))
    return outs[:2], (back_a, outs[2]), dq_early + dq_late


def moved(value, chips, heads, chip_step, flip, head_step):
    index = lambda chip, core, head: (chip * 2 + core) * heads + head
    pairs = [
        (index(chip, core, head), index(chip + chip_step, core ^ flip, (head + head_step) % heads))
        for chip in range(chips)
        for core in range(2)
        for head in range(heads)
        if 0 <= chip + chip_step < chips
    ]
    return lax.ppermute(value, ("chip", "core", "head"), pairs)


def on_device(query_rows, key_rows, saved_value_rows, out_grad):
    chips, heads = lax.axis_size("chip"), lax.axis_size("head")
    send = functools.partial(moved, chips=chips, heads=heads)
    rows, d, low = key_rows.shape[0], HEAD_SIZE, jnp.bfloat16
    bind = lambda kernel: functools.partial(kernel, heads)
    place = jnp.stack(
        [(lax.axis_index("chip") == 0).astype(jnp.int32), lax.axis_index("core"), lax.axis_index("head")]
    ).astype(jnp.int32)

    def ship(value, head_step):
        return send(value, chip_step=0, flip=0, head_step=head_step)

    def spread(parts):
        return (parts[0],) + tuple(ship(parts[n], steps_of(heads)[n]) for n in range(1, heads))

    across = functools.partial(send, head_step=0)
    slab = shape_of(low, rows, 4 * d)
    kvs = spread(
        copy_call(bind(pack_kv_kernel), 4 * heads, (slab,) * heads, (place, key_rows, saved_value_rows))
    )
    qd_mine, *qd_other = copy_call(
        bind(pack_qd_kernel),
        4 * heads,
        (shape_of(low, heads, rows, 4 * d),) + (slab,) * heads,
        (place, query_rows, out_grad),
    )
    qd_other = [across(part, chip_step=0, flip=1) for part in qd_other]
    mine, other = call(bind(gather_kv_kernel), (shape_of(low, heads * rows, 2 * d),) * 2, (place,) + kvs)
    near = across(mine, chip_step=1, flip=0)
    far = across(other, chip_step=1, flip=1)
    blocks = call(
        bind(merge_rows_kernel),
        tuple(shape_of(low, 2 * rows + 16 * (n == 1), 4 * d) for n in range(heads)),
        (place, qd_mine, *qd_other, mine[:8]),
    )
    blocks = spread(blocks)
    sibling = across(other, chip_step=0, flip=1)
    own = call(
        join_kernel,
        (shape_of(low, 2 * heads * rows, 2 * d), shape_of(low, d, 2 * heads * rows)),
        (place, mine, sibling),
    )
    own_sums, partial, dqs = attention_backward(
        heads, place, own, near, far, blocks, lambda dq, step: ship(dq, -step)
    )
    back = [across(part, chip_step=-1, flip=0) for part in partial]
    halves = shape_of(low, heads * rows, 2 * d)
    totals = spread(call(bind(add_kernel), (shape_of(low, 2 * rows, 2 * d),) * heads, (place, *own_sums, *back)))
    kv_mine, kv_other = call(bind(sort_kernel), (halves, halves), (place,) + totals)
    kv_sibling = across(kv_other, chip_step=0, flip=1)
    dq_mine, dq_other = call(
        bind(sort_kernel), (shape_of(low, heads * rows, 2 * d),) * 2, (place,) + tuple(dqs)
    )
    dq_sibling = across(dq_other, chip_step=0, flip=1)
    query_grad = copy_call(
        bind(unpack_dq_kernel), 2 * heads, shape_of(low, *query_rows.shape), (place, dq_mine, dq_sibling)
    )
    key_grad, value_grad = call(
        bind(unpack_kv_kernel), (shape_of(low, *key_rows.shape),) * 2, (place, kv_mine, kv_sibling)
    )
    return query_grad, key_grad, value_grad


def solution(mesh):
    heads = mesh.shape["head"]
    devices = mesh.devices.reshape(-1, 2, heads)
    fine_mesh = Mesh(devices, ("chip", "core", "head"))
    rows = P(("chip", "core", "head"), None)
    return jax.shard_map(
        on_device,
        mesh=fine_mesh,
        in_specs=(rows,) * 4,
        out_specs=(rows,) * 3,
        check_vma=False,
    )
```

```python
import functools

import jax
import jax.numpy as jnp
from jax import lax
from jax.experimental import pallas as pl
from jax.experimental.pallas import tpu as pltpu
from jax.sharding import Mesh
from jax.sharding import PartitionSpec as P

HEAD_SIZE = 128
BLOCK = 128
LOG2_E = 1.4426950408889634

score_scale = 168.0 ** (-0.5)
masked_value = -1e30
contract_last = (((1,), (1,)), ((), ()))
VMEM_SPEC = pl.BlockSpec(memory_space=pltpu.VMEM)
ANY_SPEC = pl.BlockSpec(memory_space=pl.ANY)
SMEM_SPEC = pl.BlockSpec(memory_space=pltpu.SMEM)


def call(kernel, out_shape, operands, scratch=(), flops=0, transcendentals=0, vmem=16, spec=VMEM_SPEC, out_spec=VMEM_SPEC):
    outs = out_shape if isinstance(out_shape, tuple) else (out_shape,)
    moved = sum(a.size * a.dtype.itemsize for a in operands + outs)
    return pl.pallas_call(
        kernel,
        out_shape=out_shape,
        in_specs=[SMEM_SPEC] + [spec] * (len(operands) - 1),
        out_specs=jax.tree.map(lambda _: out_spec, out_shape),
        scratch_shapes=list(scratch),
        compiler_params=pltpu.CompilerParams(vmem_limit_bytes=vmem * 2**20),
        cost_estimate=pl.CostEstimate(flops=flops, bytes_accessed=moved, transcendentals=transcendentals),
    )(*operands)


def copy_call(kernel, copies, out_shape, operands):
    return call(kernel, out_shape, operands, (pltpu.SemaphoreType.DMA((copies,)),), spec=ANY_SPEC, out_spec=ANY_SPEC)


def shape_of(dtype, *shape):
    return jax.ShapeDtypeStruct(shape, dtype)


def at(start, size):
    return pl.ds(pl.multiple_of(start, size), size)


def copied(sems, pairs):
    copies = [pltpu.make_async_copy(src, dst, sems.at[n]) for n, (src, dst) in enumerate(pairs)]
    for copy in copies:
        copy.start()
    for copy in copies:
        copy.wait()


def steps_of(heads):
    return (0,) + tuple(sorted(range(1, heads), key=lambda k: -min(k, heads - k)))


def onward(place_ref, heads, n):
    return lax.rem(place_ref[2] + steps_of(heads)[n], heads)


def source(place_ref, heads, n):
    return lax.rem(place_ref[2] + heads - steps_of(heads)[n], heads)


def pack_kv_kernel(heads, place_ref, k_ref, v_ref, *refs):
    out_refs, sems = refs[:-1], refs[-1]
    core = place_ref[1]
    d = HEAD_SIZE
    pairs = []
    for k, out_ref in enumerate(out_refs):
        z = onward(place_ref, heads, k)
        for n, g in enumerate((2 * z + core, 2 * z + 1 - core)):
            columns = at(g * d, d)
            pairs.append((k_ref.at[:, columns], out_ref.at[:, pl.ds(2 * n * d, d)]))
            pairs.append((v_ref.at[:, columns], out_ref.at[:, pl.ds((2 * n + 1) * d, d)]))
    copied(sems, pairs)


def pack_qd_kernel(heads, place_ref, q_ref, g_ref, mine_ref, *refs):
    other_refs, sems = refs[:heads], refs[heads]
    core = place_ref[1]
    width = 2 * HEAD_SIZE
    pairs = []
    for k in range(heads):
        for ref, c in ((other_refs[k], 1 - core), (mine_ref.at[k], core)):
            columns = at((2 * onward(place_ref, heads, k) + c) * width, width)
            pairs.append((q_ref.at[:, columns], ref.at[:, pl.ds(0, width)]))
            pairs.append((g_ref.at[:, columns], ref.at[:, pl.ds(width, width)]))
    copied(sems, pairs)


def gather_kv_kernel(heads, place_ref, *refs):
    in_refs, (mine_ref, other_ref) = refs[:heads], refs[heads:]
    width = 2 * HEAD_SIZE
    for k, in_ref in enumerate(in_refs):
        rows = at(source(place_ref, heads, k) * BLOCK, BLOCK)
        mine_ref[rows] = in_ref[:, :width]
        other_ref[rows] = in_ref[:, width:]


def join_kernel(place_ref, mine_ref, sibling_ref, out_ref, kt_ref):
    core = place_ref[1]
    half = mine_ref.shape[0]
    out_ref[at(core * half, half)] = mine_ref[...]
    out_ref[at((1 - core) * half, half)] = sibling_ref[...]
    kt_ref[...] = out_ref[:, :HEAD_SIZE].T


def merge_rows_kernel(heads, place_ref, mine_ref, *refs):
    other_refs, out_refs = refs[:heads], refs[heads + 1 :]
    core = place_ref[1]
    for k, out_ref in enumerate(out_refs):
        out_ref[at(core * BLOCK, BLOCK)] = mine_ref[k]
        out_ref[at((1 - core) * BLOCK, BLOCK)] = other_refs[k][...]


def sort_kernel(heads, place_ref, *refs):
    in_refs, (mine_ref, other_ref) = refs[:heads], refs[heads:]
    core = place_ref[1]
    for k, in_ref in enumerate(in_refs):
        mine_ref[k * BLOCK : (k + 1) * BLOCK] = in_ref[at(core * BLOCK, BLOCK)]
        other_ref[k * BLOCK : (k + 1) * BLOCK] = in_ref[at((1 - core) * BLOCK, BLOCK)]


def unpack_dq_kernel(heads, place_ref, mine_ref, sibling_ref, out_ref, sems):
    core = place_ref[1]
    width = 2 * HEAD_SIZE
    pairs = []
    for k in range(heads):
        z = onward(place_ref, heads, k)
        for ref, c in ((mine_ref, core), (sibling_ref, 1 - core)):
            rows = pl.ds(k * BLOCK, BLOCK)
            pairs.append((ref.at[rows], out_ref.at[:, at((2 * z + c) * width, width)]))
    copied(sems, pairs)


def unpack_kv_kernel(heads, place_ref, mine_ref, sibling_ref, k_ref, v_ref):
    core = place_ref[1]
    d = HEAD_SIZE
    for k in range(heads):
        z = source(place_ref, heads, k)
        rows = slice(k * BLOCK, (k + 1) * BLOCK)
        for ref, c in ((mine_ref, core), (sibling_ref, 1 - core)):
            columns = at((2 * z + c) * d, d)
            k_ref[:, columns] = ref[rows, :d]
            v_ref[:, columns] = ref[rows, d:]


def add_kernel(heads, place_ref, own_a_ref, own_b_ref, back_a_ref, back_b_ref, *out_refs):
    for k, out_ref in enumerate(out_refs):
        rows = at(onward(place_ref, heads, k) * BLOCK, BLOCK)
        for c, (own_ref, back_ref) in enumerate(((own_a_ref, back_a_ref), (own_b_ref, back_b_ref))):
            total = own_ref[rows] + back_ref[rows].astype(jnp.float32)
            out_ref[c * BLOCK : (c + 1) * BLOCK] = total.astype(jnp.bfloat16)


def attention_block(i, count, q, g, own_ref, prev_ref, own_kt_ref, prev_kt_ref, own_grad_ref, prev_grad_ref, bias):
    d = HEAD_SIZE
    low, high = i * BLOCK, (i + 1) * BLOCK
    below, above = i > 0, i < count - 1
    key_row = lax.broadcasted_iota(jnp.int32, (BLOCK, 2 * BLOCK), 0)
    query_row = lax.broadcasted_iota(jnp.int32, (BLOCK, 2 * BLOCK), 1) % BLOCK
    own_seen = key_row <= query_row
    zero = jnp.zeros((BLOCK, 2 * BLOCK), jnp.bfloat16)
    dot_t = lambda a, b: lax.dot_general(a, b, contract_last, preferred_element_type=jnp.float32)
    dot = lambda a, b: jnp.dot(a, b, preferred_element_type=jnp.float32)
    s_own = dot_t(own_ref[:high, :d], q)
    s_prev = dot_t(prev_ref[low:, :d], q) + bias
    p_own = dot_t(own_ref[:high, d:], g)
    p_prev = dot_t(prev_ref[low:, d:], g)
    s_diag = jnp.where(own_seen, s_own[low:], s_prev[:BLOCK])
    p_diag = jnp.where(own_seen, p_own[low:], p_prev[:BLOCK])
    s = jnp.concatenate([s_own[:low]] * below + [s_diag] + [s_prev[BLOCK:]] * above, 0)
    dp = jnp.concatenate([p_own[:low]] * below + [p_diag] + [p_prev[BLOCK:]] * above, 0)
    top = jnp.max(s, axis=0, keepdims=True)
    w = jnp.exp2((s - top) * (score_scale * LOG2_E))
    inverse = 1.0 / jnp.sum(w, axis=0, keepdims=True)
    delta = jnp.sum(w * dp, axis=0, keepdims=True) * inverse
    attention = w * inverse
    ds = (attention * (dp - delta)).astype(jnp.bfloat16)
    low_attention = attention.astype(jnp.bfloat16)
    split = lambda x: (
        jnp.concatenate([x[:low]] * below + [jnp.where(own_seen, x[low:high], zero)], 0),
        jnp.concatenate([jnp.where(own_seen, zero, x[low:high])] + [x[high:]] * above, 0),
    )
    ds_own, ds_prev = split(ds)
    at_own, at_prev = split(low_attention)
    own_grad_ref[:high, d:] += dot(at_own, g)
    prev_grad_ref[low:, d:] += dot(at_prev, g)
    own_grad_ref[:high, :d] += dot(ds_own, q)
    prev_grad_ref[low:, :d] += dot(ds_prev, q)
    dq_t = dot(own_kt_ref[:, :high], ds_own) + dot(prev_kt_ref[:, low:], ds_prev)
    return dq_t * score_scale


def attention_kernel(heads, steps, cores, phase, place_ref, own_ref, own_kt_ref, a_ref, b_ref, *refs):
    d = HEAD_SIZE
    count = 2 * heads
    half = heads * BLOCK
    first, core, head = place_ref[0], place_ref[1], place_ref[2]
    low_rows, high_rows = slice(0, half), slice(half, 2 * half)
    block_refs, refs = refs[: len(steps)], refs[len(steps) :]
    prev_ref, prev_kt_ref = a_ref, b_ref
    if phase == 0:
        prev_ref, prev_kt_ref, own_grad_ref, prev_grad_ref = refs[:4]
        dq_refs, (qd_ref, dq_ref) = refs[4:-2], refs[-2:]
        own_grad_ref[...] = jnp.zeros_like(own_grad_ref)
        prev_grad_ref[...] = jnp.zeros_like(prev_grad_ref)
        prev_ref[at(core * half, half)] = a_ref[...]
        prev_ref[at((1 - core) * half, half)] = b_ref[...]
        prev_kt_ref[...] = prev_ref[:, :d].T
    elif phase == 1:
        own_sums_ref, prev_sums_ref, own_grad_ref, prev_high_ref, back_ref, dq_out_ref = refs[:6]
        qd_ref, dq_ref, prev_grad_ref = refs[6:]
        own_grad_ref[...] = own_sums_ref[low_rows]
        prev_grad_ref[...] = prev_sums_ref[...]
    else:
        own_low_ref, own_sums_ref, prev_high_ref, dq_so_far_ref, after_ref = refs[:5]
        own_a_ref, own_b_ref, back_ref = refs[5:8]
        dq_refs, (qd_ref, dq_ref, own_grad_ref, prev_grad_ref) = refs[8:-4], refs[-4:]
        own_grad_ref[low_rows] = own_low_ref[...]
        own_grad_ref[high_rows] = own_sums_ref[high_rows]
        prev_grad_ref[high_rows] = prev_high_ref[...]
        dq_ref[:, :BLOCK] = dq_so_far_ref[...]
    for n, block_ref in enumerate(block_refs):
        qd_ref[n] = block_ref[: 2 * BLOCK]
    bias = jnp.where(first == 1, masked_value, 0.0).astype(jnp.float32)

    @pl.loop(0, len(steps))
    def _(n):
        step = steps[0] + n * (steps[-1] - steps[0]) // max(len(steps) - 1, 1)
        z_here = lax.rem(head + heads - step, heads)
        for z in range(heads):

            @pl.when(z_here == z)
            def _():
                for c in cores:
                    rows = slice(c * BLOCK, (c + 1) * BLOCK)
                    q = jnp.concatenate([qd_ref[n, rows, :d], qd_ref[n, rows, d : 2 * d]], 0)
                    g = jnp.concatenate([qd_ref[n, rows, 2 * d : 3 * d], qd_ref[n, rows, 3 * d :]], 0)
                    dq_t = attention_block(
                        c * heads + z, count, q, g, own_ref, prev_ref, own_kt_ref, prev_kt_ref,
                        own_grad_ref, prev_grad_ref, bias,
                    )
                    dq_ref[n, rows, :d] = dq_t[:, :BLOCK].T.astype(jnp.bfloat16)
                    dq_ref[n, rows, d:] = dq_t[:, BLOCK:].T.astype(jnp.bfloat16)

    def finish(ref, grad_ref, rows):
        ref[low_rows, :d] = (grad_ref[rows, :d] * score_scale).astype(ref.dtype)
        ref[low_rows, d:] = grad_ref[rows, d:].astype(ref.dtype)

    if phase == 0:
        for n, ref in enumerate(dq_refs):
            ref[...] = dq_ref[n]
    elif phase == 1:
        finish(back_ref, prev_grad_ref, low_rows)
        prev_high_ref[...] = prev_grad_ref[high_rows]
        dq_out_ref[...] = dq_ref[:, :BLOCK]
    else:
        finish(back_ref, prev_grad_ref, high_rows)
        finish(own_a_ref, own_grad_ref, low_rows)
        finish(own_b_ref, own_grad_ref, high_rows)
        for n, ref in enumerate(dq_refs):
            ref[...] = dq_ref[n]


def attention_backward(heads, place, own, near, far, blocks, home):
    half, d = heads * BLOCK, HEAD_SIZE
    whole = 2 * half
    low, wide = jnp.bfloat16, jnp.float32
    sums, half_sums, part = shape_of(wide, whole, 2 * d), shape_of(wide, half, 2 * d), shape_of(low, half, 2 * d)
    block = shape_of(low, 2 * BLOCK, 2 * d)
    early, late = steps_of(heads)[: heads // 2], steps_of(heads)[heads // 2 :]

    def run(steps, cores, phase, outs, operands, scratch):
        scratch = (
            pltpu.VMEM((len(steps), 2 * BLOCK, 4 * d), low),
            pltpu.VMEM((len(steps), 2 * BLOCK, 2 * d), low),
        ) + (pltpu.VMEM((whole, 2 * d), wide),) * scratch
        kernel = functools.partial(attention_kernel, heads, steps, cores, phase)
        return call(kernel, outs, (place,) + tuple(own) + tuple(operands), scratch, 1, 1, 32)

    outs = (shape_of(low, whole, 2 * d), shape_of(low, d, whole), sums, sums) + (block,) * len(early)
    outs = run(early, (0, 1), 0, outs, [near, far] + list(blocks[: len(early)]), 0)
    prev, (own_sums, prev_sums), dq_early = outs[:2], outs[2:4], outs[4:]
    dq_early = (dq_early[0],) + tuple(home(dq_early[n], early[n]) for n in range(1, len(early)))
    late_blocks = tuple(blocks[len(early) :])
    wide_part = shape_of(low, half + 16, 2 * d)
    outs = (half_sums, half_sums, wide_part, shape_of(low, len(late), BLOCK, 2 * d))
    own_low, prev_high, back_a, dq_so_far = run(
        late, (0,), 1, outs, prev + late_blocks + (own_sums, prev_sums), 1
    )
    outs = run(
        late,
        (1,),
        2,
        (half_sums, half_sums, part) + (block,) * len(late),
        prev + late_blocks + (own_low, own_sums, prev_high, dq_so_far, dq_early[-1][:16]),
        2,
    )
    dq_late = tuple(home(dq, step) for dq, step in zip(outs[3:], late))
    return outs[:2], (back_a, outs[2]), dq_early + dq_late


def moved(value, chips, heads, chip_step, flip, head_step):
    index = lambda chip, core, head: (chip * 2 + core) * heads + head
    pairs = [
        (index(chip, core, head), index(chip + chip_step, core ^ flip, (head + head_step) % heads))
        for chip in range(chips)
        for core in range(2)
        for head in range(heads)
        if 0 <= chip + chip_step < chips
    ]
    return lax.ppermute(value, ("chip", "core", "head"), pairs)


def on_device(query_rows, key_rows, saved_value_rows, out_grad):
    chips, heads = lax.axis_size("chip"), lax.axis_size("head")
    send = functools.partial(moved, chips=chips, heads=heads)
    rows, d, low = key_rows.shape[0], HEAD_SIZE, jnp.bfloat16
    bind = lambda kernel: functools.partial(kernel, heads)
    place = jnp.stack(
        [(lax.axis_index("chip") == 0).astype(jnp.int32), lax.axis_index("core"), lax.axis_index("head")]
    ).astype(jnp.int32)

    def ship(value, head_step):
        return send(value, chip_step=0, flip=0, head_step=head_step)

    def spread(parts):
        return (parts[0],) + tuple(ship(parts[n], steps_of(heads)[n]) for n in range(1, heads))

    across = functools.partial(send, head_step=0)
    slab = shape_of(low, rows, 4 * d)
    kvs = spread(
        copy_call(bind(pack_kv_kernel), 4 * heads, (slab,) * heads, (place, key_rows, saved_value_rows))
    )
    qd_mine, *qd_other = copy_call(
        bind(pack_qd_kernel),
        4 * heads,
        (shape_of(low, heads, rows, 4 * d),) + (slab,) * heads,
        (place, query_rows, out_grad),
    )
    qd_other = [across(part, chip_step=0, flip=1) for part in qd_other]
    mine, other = call(bind(gather_kv_kernel), (shape_of(low, heads * rows, 2 * d),) * 2, (place,) + kvs)
    near = across(mine, chip_step=1, flip=0)
    far = across(other, chip_step=1, flip=1)
    blocks = call(
        bind(merge_rows_kernel),
        tuple(shape_of(low, 2 * rows + 16 * (n > 0), 4 * d) for n in range(heads)),
        (place, qd_mine, *qd_other, mine[:8]),
    )
    blocks = spread(blocks)
    sibling = across(other, chip_step=0, flip=1)
    own = call(
        join_kernel,
        (shape_of(low, 2 * heads * rows, 2 * d), shape_of(low, d, 2 * heads * rows)),
        (place, mine, sibling),
    )
    own_sums, partial, dqs = attention_backward(
        heads, place, own, near, far, blocks, lambda dq, step: ship(dq, -step)
    )
    back = [across(part, chip_step=-1, flip=0) for part in partial]
    halves = shape_of(low, heads * rows, 2 * d)
    totals = spread(call(bind(add_kernel), (shape_of(low, 2 * rows, 2 * d),) * heads, (place, *own_sums, *back)))
    kv_mine, kv_other = call(bind(sort_kernel), (halves, halves), (place,) + totals)
    kv_sibling = across(kv_other, chip_step=0, flip=1)
    dq_mine, dq_other = call(
        bind(sort_kernel), (shape_of(low, heads * rows, 2 * d),) * 2, (place,) + tuple(dqs)
    )
    dq_sibling = across(dq_other, chip_step=0, flip=1)
    query_grad = copy_call(
        bind(unpack_dq_kernel), 2 * heads, shape_of(low, *query_rows.shape), (place, dq_mine, dq_sibling)
    )
    key_grad, value_grad = call(
        bind(unpack_kv_kernel), (shape_of(low, *key_rows.shape),) * 2, (place, kv_mine, kv_sibling)
    )
    return query_grad, key_grad, value_grad


def solution(mesh):
    heads = mesh.shape["head"]
    devices = mesh.devices.reshape(-1, 2, heads)
    fine_mesh = Mesh(devices, ("chip", "core", "head"))
    rows = P(("chip", "core", "head"), None)
    return jax.shard_map(
        on_device,
        mesh=fine_mesh,
        in_specs=(rows,) * 4,
        out_specs=(rows,) * 3,
        check_vma=False,
    )
```

```python
import functools

import jax
import jax.numpy as jnp
from jax import lax
from jax.experimental import pallas as pl
from jax.experimental.pallas import tpu as pltpu
from jax.sharding import Mesh
from jax.sharding import PartitionSpec as P

HEAD_SIZE = 128
BLOCK = 128
LOG2_E = 1.4426950408889634

score_scale = 168.0 ** (-0.5)
masked_value = -1e30
contract_last = (((1,), (1,)), ((), ()))
VMEM_SPEC = pl.BlockSpec(memory_space=pltpu.VMEM)
ANY_SPEC = pl.BlockSpec(memory_space=pl.ANY)
SMEM_SPEC = pl.BlockSpec(memory_space=pltpu.SMEM)


def call(kernel, out_shape, operands, scratch=(), flops=0, transcendentals=0, vmem=16, spec=VMEM_SPEC, out_spec=VMEM_SPEC):
    outs = out_shape if isinstance(out_shape, tuple) else (out_shape,)
    moved = sum(a.size * a.dtype.itemsize for a in operands + outs)
    return pl.pallas_call(
        kernel,
        out_shape=out_shape,
        in_specs=[SMEM_SPEC] + [spec] * (len(operands) - 1),
        out_specs=jax.tree.map(lambda _: out_spec, out_shape),
        scratch_shapes=list(scratch),
        compiler_params=pltpu.CompilerParams(vmem_limit_bytes=vmem * 2**20),
        cost_estimate=pl.CostEstimate(flops=flops, bytes_accessed=moved, transcendentals=transcendentals),
    )(*operands)


def copy_call(kernel, copies, out_shape, operands):
    return call(kernel, out_shape, operands, (pltpu.SemaphoreType.DMA((copies,)),), spec=ANY_SPEC, out_spec=ANY_SPEC)


def shape_of(dtype, *shape):
    return jax.ShapeDtypeStruct(shape, dtype)


def at(start, size):
    return pl.ds(pl.multiple_of(start, size), size)


def copied(sems, pairs):
    copies = [pltpu.make_async_copy(src, dst, sems.at[n]) for n, (src, dst) in enumerate(pairs)]
    for copy in copies:
        copy.start()
    for copy in copies:
        copy.wait()


def steps_of(heads):
    return (0,) + tuple(sorted(range(1, heads), key=lambda k: -min(k, heads - k)))


def onward(place_ref, heads, n):
    return lax.rem(place_ref[2] + steps_of(heads)[n], heads)


def source(place_ref, heads, n):
    return lax.rem(place_ref[2] + heads - steps_of(heads)[n], heads)


def pack_kv_kernel(heads, place_ref, k_ref, v_ref, *refs):
    out_refs, sems = refs[:-1], refs[-1]
    core = place_ref[1]
    d = HEAD_SIZE
    pairs = []
    for k, out_ref in enumerate(out_refs):
        z = onward(place_ref, heads, k)
        for n, g in enumerate((2 * z + core, 2 * z + 1 - core)):
            columns = at(g * d, d)
            pairs.append((k_ref.at[:, columns], out_ref.at[:, pl.ds(2 * n * d, d)]))
            pairs.append((v_ref.at[:, columns], out_ref.at[:, pl.ds((2 * n + 1) * d, d)]))
    copied(sems, pairs)


def pack_qd_kernel(heads, place_ref, q_ref, g_ref, mine_ref, *refs):
    other_refs, sems = refs[:heads], refs[heads]
    core = place_ref[1]
    width = 2 * HEAD_SIZE
    pairs = []
    for k in range(heads):
        for ref, c in ((other_refs[k], 1 - core), (mine_ref.at[k], core)):
            columns = at((2 * onward(place_ref, heads, k) + c) * width, width)
            pairs.append((q_ref.at[:, columns], ref.at[:, pl.ds(0, width)]))
            pairs.append((g_ref.at[:, columns], ref.at[:, pl.ds(width, width)]))
    copied(sems, pairs)


def gather_kv_kernel(heads, place_ref, *refs):
    in_refs, (mine_ref, other_ref) = refs[:heads], refs[heads:]
    width = 2 * HEAD_SIZE
    for k, in_ref in enumerate(in_refs):
        rows = at(source(place_ref, heads, k) * BLOCK, BLOCK)
        mine_ref[rows] = in_ref[:, :width]
        other_ref[rows] = in_ref[:, width:]


def join_kernel(place_ref, mine_ref, sibling_ref, out_ref, kt_ref):
    core = place_ref[1]
    half = mine_ref.shape[0]
    out_ref[at(core * half, half)] = mine_ref[...]
    out_ref[at((1 - core) * half, half)] = sibling_ref[...]
    kt_ref[...] = out_ref[:, :HEAD_SIZE].T


def merge_rows_kernel(heads, place_ref, mine_ref, *refs):
    other_refs, out_refs = refs[:heads], refs[heads + 1 :]
    core = place_ref[1]
    for k, out_ref in enumerate(out_refs):
        out_ref[at(core * BLOCK, BLOCK)] = mine_ref[k]
        out_ref[at((1 - core) * BLOCK, BLOCK)] = other_refs[k][...]


def sort_kernel(heads, place_ref, *refs):
    in_refs, (mine_ref, other_ref) = refs[:heads], refs[heads:]
    core = place_ref[1]
    for k, in_ref in enumerate(in_refs):
        mine_ref[k * BLOCK : (k + 1) * BLOCK] = in_ref[at(core * BLOCK, BLOCK)]
        other_ref[k * BLOCK : (k + 1) * BLOCK] = in_ref[at((1 - core) * BLOCK, BLOCK)]


def unpack_dq_kernel(heads, place_ref, mine_ref, sibling_ref, out_ref, sems):
    core = place_ref[1]
    width = 2 * HEAD_SIZE
    pairs = []
    for k in range(heads):
        z = onward(place_ref, heads, k)
        for ref, c in ((mine_ref, core), (sibling_ref, 1 - core)):
            rows = pl.ds(k * BLOCK, BLOCK)
            pairs.append((ref.at[rows], out_ref.at[:, at((2 * z + c) * width, width)]))
    copied(sems, pairs)


def unpack_kv_kernel(heads, place_ref, mine_ref, sibling_ref, k_ref, v_ref):
    core = place_ref[1]
    d = HEAD_SIZE
    for k in range(heads):
        z = source(place_ref, heads, k)
        rows = slice(k * BLOCK, (k + 1) * BLOCK)
        for ref, c in ((mine_ref, core), (sibling_ref, 1 - core)):
            columns = at((2 * z + c) * d, d)
            k_ref[:, columns] = ref[rows, :d]
            v_ref[:, columns] = ref[rows, d:]


def add_kernel(heads, place_ref, own_a_ref, own_b_ref, back_a_ref, back_b_ref, *out_refs):
    for k, out_ref in enumerate(out_refs):
        rows = at(onward(place_ref, heads, k) * BLOCK, BLOCK)
        for c, (own_ref, back_ref) in enumerate(((own_a_ref, back_a_ref), (own_b_ref, back_b_ref))):
            total = own_ref[rows] + back_ref[rows].astype(jnp.float32)
            out_ref[c * BLOCK : (c + 1) * BLOCK] = total.astype(jnp.bfloat16)


def attention_block(i, count, q, g, own_ref, prev_ref, own_kt_ref, prev_kt_ref, own_grad_ref, prev_grad_ref, bias):
    d = HEAD_SIZE
    low, high = i * BLOCK, (i + 1) * BLOCK
    below, above = i > 0, i < count - 1
    key_row = lax.broadcasted_iota(jnp.int32, (BLOCK, 2 * BLOCK), 0)
    query_row = lax.broadcasted_iota(jnp.int32, (BLOCK, 2 * BLOCK), 1) % BLOCK
    own_seen = key_row <= query_row
    zero = jnp.zeros((BLOCK, 2 * BLOCK), jnp.bfloat16)
    dot_t = lambda a, b: lax.dot_general(a, b, contract_last, preferred_element_type=jnp.float32)
    dot = lambda a, b: jnp.dot(a, b, preferred_element_type=jnp.float32)
    s_own = dot_t(own_ref[:high, :d], q)
    s_prev = dot_t(prev_ref[low:, :d], q) + bias
    p_own = dot_t(own_ref[:high, d:], g)
    p_prev = dot_t(prev_ref[low:, d:], g)
    s_diag = jnp.where(own_seen, s_own[low:], s_prev[:BLOCK])
    p_diag = jnp.where(own_seen, p_own[low:], p_prev[:BLOCK])
    s = jnp.concatenate([s_own[:low]] * below + [s_diag] + [s_prev[BLOCK:]] * above, 0)
    dp = jnp.concatenate([p_own[:low]] * below + [p_diag] + [p_prev[BLOCK:]] * above, 0)
    top = jnp.max(s, axis=0, keepdims=True)
    w = jnp.exp2((s - top) * (score_scale * LOG2_E))
    inverse = 1.0 / jnp.sum(w, axis=0, keepdims=True)
    delta = jnp.sum(w * dp, axis=0, keepdims=True) * inverse
    attention = w * inverse
    ds = (attention * (dp - delta)).astype(jnp.bfloat16)
    low_attention = attention.astype(jnp.bfloat16)
    split = lambda x: (
        jnp.concatenate([x[:low]] * below + [jnp.where(own_seen, x[low:high], zero)], 0),
        jnp.concatenate([jnp.where(own_seen, zero, x[low:high])] + [x[high:]] * above, 0),
    )
    ds_own, ds_prev = split(ds)
    at_own, at_prev = split(low_attention)
    own_grad_ref[:high, d:] += dot(at_own, g)
    prev_grad_ref[low:, d:] += dot(at_prev, g)
    own_grad_ref[:high, :d] += dot(ds_own, q)
    prev_grad_ref[low:, :d] += dot(ds_prev, q)
    dq_t = dot(own_kt_ref[:, :high], ds_own) + dot(prev_kt_ref[:, low:], ds_prev)
    return dq_t * score_scale


def attention_kernel(heads, steps, cores, phase, place_ref, own_ref, own_kt_ref, a_ref, b_ref, *refs):
    d = HEAD_SIZE
    count = 2 * heads
    half = heads * BLOCK
    first, core, head = place_ref[0], place_ref[1], place_ref[2]
    low_rows, high_rows = slice(0, half), slice(half, 2 * half)
    block_refs, refs = refs[: len(steps)], refs[len(steps) :]
    prev_ref, prev_kt_ref = a_ref, b_ref
    if phase == 0:
        prev_ref, prev_kt_ref, own_grad_ref, prev_grad_ref = refs[:4]
        dq_refs, (qd_ref, dq_ref) = refs[4:-2], refs[-2:]
        own_grad_ref[...] = jnp.zeros_like(own_grad_ref)
        prev_grad_ref[...] = jnp.zeros_like(prev_grad_ref)
        prev_ref[at(core * half, half)] = a_ref[...]
        prev_ref[at((1 - core) * half, half)] = b_ref[...]
        prev_kt_ref[...] = prev_ref[:, :d].T
    elif phase == 1:
        own_sums_ref, prev_sums_ref, own_grad_ref, prev_high_ref, back_ref, dq_out_ref = refs[:6]
        qd_ref, dq_ref, prev_grad_ref = refs[6:]
        own_grad_ref[...] = own_sums_ref[low_rows]
        prev_grad_ref[...] = prev_sums_ref[...]
    else:
        own_low_ref, own_sums_ref, prev_high_ref, dq_so_far_ref, after_ref = refs[:5]
        own_a_ref, own_b_ref, back_ref = refs[5:8]
        dq_refs, (qd_ref, dq_ref, own_grad_ref, prev_grad_ref) = refs[8:-4], refs[-4:]
        own_grad_ref[low_rows] = own_low_ref[...]
        own_grad_ref[high_rows] = own_sums_ref[high_rows]
        prev_grad_ref[high_rows] = prev_high_ref[...]
        dq_ref[:, :BLOCK] = dq_so_far_ref[...]
    for n, block_ref in enumerate(block_refs):
        qd_ref[n] = block_ref[: 2 * BLOCK]
    bias = jnp.where(first == 1, masked_value, 0.0).astype(jnp.float32)

    @pl.loop(0, len(steps))
    def _(n):
        step = steps[0] + n * (steps[-1] - steps[0]) // max(len(steps) - 1, 1)
        z_here = lax.rem(head + heads - step, heads)
        for z in range(heads):

            @pl.when(z_here == z)
            def _():
                for c in cores:
                    rows = slice(c * BLOCK, (c + 1) * BLOCK)
                    q = jnp.concatenate([qd_ref[n, rows, :d], qd_ref[n, rows, d : 2 * d]], 0)
                    g = jnp.concatenate([qd_ref[n, rows, 2 * d : 3 * d], qd_ref[n, rows, 3 * d :]], 0)
                    dq_t = attention_block(
                        c * heads + z, count, q, g, own_ref, prev_ref, own_kt_ref, prev_kt_ref,
                        own_grad_ref, prev_grad_ref, bias,
                    )
                    dq_ref[n, rows, :d] = dq_t[:, :BLOCK].T.astype(jnp.bfloat16)
                    dq_ref[n, rows, d:] = dq_t[:, BLOCK:].T.astype(jnp.bfloat16)

    def finish(ref, grad_ref, rows):
        ref[low_rows, :d] = (grad_ref[rows, :d] * score_scale).astype(ref.dtype)
        ref[low_rows, d:] = grad_ref[rows, d:].astype(ref.dtype)

    if phase == 0:
        for n, ref in enumerate(dq_refs):
            ref[...] = dq_ref[n]
    elif phase == 1:
        finish(back_ref, prev_grad_ref, low_rows)
        prev_high_ref[...] = prev_grad_ref[high_rows]
        dq_out_ref[...] = dq_ref[:, :BLOCK]
    else:
        finish(back_ref, prev_grad_ref, high_rows)
        finish(own_a_ref, own_grad_ref, low_rows)
        finish(own_b_ref, own_grad_ref, high_rows)
        for n, ref in enumerate(dq_refs):
            ref[...] = dq_ref[n]


def attention_backward(heads, place, own, near, far, blocks, home):
    half, d = heads * BLOCK, HEAD_SIZE
    whole = 2 * half
    low, wide = jnp.bfloat16, jnp.float32
    sums, half_sums, part = shape_of(wide, whole, 2 * d), shape_of(wide, half, 2 * d), shape_of(low, half, 2 * d)
    block = shape_of(low, 2 * BLOCK, 2 * d)
    early, late = steps_of(heads)[: heads // 2], steps_of(heads)[heads // 2 :]

    def run(steps, cores, phase, outs, operands, scratch):
        scratch = (
            pltpu.VMEM((len(steps), 2 * BLOCK, 4 * d), low),
            pltpu.VMEM((len(steps), 2 * BLOCK, 2 * d), low),
        ) + (pltpu.VMEM((whole, 2 * d), wide),) * scratch
        kernel = functools.partial(attention_kernel, heads, steps, cores, phase)
        return call(kernel, outs, (place,) + tuple(own) + tuple(operands), scratch, 1, 1, 32)

    outs = (shape_of(low, whole, 2 * d), shape_of(low, d, whole), sums, sums) + (block,) * len(early)
    outs = run(early, (0, 1), 0, outs, [near, far] + list(blocks[: len(early)]), 0)
    prev, (own_sums, prev_sums), dq_early = outs[:2], outs[2:4], outs[4:]
    dq_early = (dq_early[0],) + tuple(home(dq_early[n], early[n]) for n in range(1, len(early)))
    late_blocks = tuple(blocks[len(early) :])
    wide_part = shape_of(low, half + 16, 2 * d)
    outs = (half_sums, half_sums, wide_part, shape_of(low, len(late), BLOCK, 2 * d))
    own_low, prev_high, back_a, dq_so_far = run(
        late, (0,), 1, outs, prev + late_blocks + (own_sums, prev_sums), 1
    )
    outs = run(
        late,
        (1,),
        2,
        (half_sums, half_sums, part) + (block,) * len(late),
        prev + late_blocks + (own_low, own_sums, prev_high, dq_so_far, dq_early[-1][:16]),
        2,
    )
    dq_late = tuple(home(dq, step) for dq, step in zip(outs[3:], late))
    return outs[:2], (back_a, outs[2]), dq_early + dq_late


def moved(value, chips, heads, chip_step, flip, head_step):
    index = lambda chip, core, head: (chip * 2 + core) * heads + head
    pairs = [
        (index(chip, core, head), index((chip + chip_step) % chips, core ^ flip, (head + head_step) % heads))
        for chip in range(chips)
        for core in range(2)
        for head in range(heads)
    ]
    return lax.ppermute(value, ("chip", "core", "head"), pairs)


def on_device(query_rows, key_rows, saved_value_rows, out_grad):
    chips, heads = lax.axis_size("chip"), lax.axis_size("head")
    send = functools.partial(moved, chips=chips, heads=heads)
    rows, d, low = key_rows.shape[0], HEAD_SIZE, jnp.bfloat16
    bind = lambda kernel: functools.partial(kernel, heads)
    place = jnp.stack(
        [(lax.axis_index("chip") == 0).astype(jnp.int32), lax.axis_index("core"), lax.axis_index("head")]
    ).astype(jnp.int32)

    def ship(value, head_step):
        return send(value, chip_step=0, flip=0, head_step=head_step)

    def spread(parts):
        return (parts[0],) + tuple(ship(parts[n], steps_of(heads)[n]) for n in range(1, heads))

    across = functools.partial(send, head_step=0)
    slab = shape_of(low, rows, 4 * d)
    kvs = spread(
        copy_call(bind(pack_kv_kernel), 4 * heads, (slab,) * heads, (place, key_rows, saved_value_rows))
    )
    qd_mine, *qd_other = copy_call(
        bind(pack_qd_kernel),
        4 * heads,
        (shape_of(low, heads, rows, 4 * d),) + (slab,) * heads,
        (place, query_rows, out_grad),
    )
    qd_other = [across(part, chip_step=0, flip=1) for part in qd_other]
    mine, other = call(bind(gather_kv_kernel), (shape_of(low, heads * rows, 2 * d),) * 2, (place,) + kvs)
    near = across(mine, chip_step=1, flip=0)
    far = across(other, chip_step=1, flip=1)
    blocks = call(
        bind(merge_rows_kernel),
        tuple(shape_of(low, 2 * rows + 16 * (n == 1), 4 * d) for n in range(heads)),
        (place, qd_mine, *qd_other, mine[:8]),
    )
    blocks = spread(blocks)
    sibling = across(other, chip_step=0, flip=1)
    own = call(
        join_kernel,
        (shape_of(low, 2 * heads * rows, 2 * d), shape_of(low, d, 2 * heads * rows)),
        (place, mine, sibling),
    )
    own_sums, partial, dqs = attention_backward(
        heads, place, own, near, far, blocks, lambda dq, step: ship(dq, -step)
    )
    back = [across(part, chip_step=-1, flip=0) for part in partial]
    halves = shape_of(low, heads * rows, 2 * d)
    totals = spread(call(bind(add_kernel), (shape_of(low, 2 * rows, 2 * d),) * heads, (place, *own_sums, *back)))
    kv_mine, kv_other = call(bind(sort_kernel), (halves, halves), (place,) + totals)
    kv_sibling = across(kv_other, chip_step=0, flip=1)
    dq_mine, dq_other = call(
        bind(sort_kernel), (shape_of(low, heads * rows, 2 * d),) * 2, (place,) + tuple(dqs)
    )
    dq_sibling = across(dq_other, chip_step=0, flip=1)
    query_grad = copy_call(
        bind(unpack_dq_kernel), 2 * heads, shape_of(low, *query_rows.shape), (place, dq_mine, dq_sibling)
    )
    key_grad, value_grad = call(
        bind(unpack_kv_kernel), (shape_of(low, *key_rows.shape),) * 2, (place, kv_mine, kv_sibling)
    )
    return query_grad, key_grad, value_grad


def solution(mesh):
    heads = mesh.shape["head"]
    devices = mesh.devices.reshape(-1, 2, heads)
    fine_mesh = Mesh(devices, ("chip", "core", "head"))
    rows = P(("chip", "core", "head"), None)
    return jax.shard_map(
        on_device,
        mesh=fine_mesh,
        in_specs=(rows,) * 4,
        out_specs=(rows,) * 3,
        check_vma=False,
    )
```

```python
import functools

import jax
import jax.numpy as jnp
from jax import lax
from jax.experimental import pallas as pl
from jax.experimental.pallas import tpu as pltpu
from jax.sharding import Mesh
from jax.sharding import PartitionSpec as P

HEAD_SIZE = 128
BLOCK = 128
LOG2_E = 1.4426950408889634

score_scale = 168.0 ** (-0.5)
masked_value = -1e30
contract_last = (((1,), (1,)), ((), ()))
VMEM_SPEC = pl.BlockSpec(memory_space=pltpu.VMEM)
ANY_SPEC = pl.BlockSpec(memory_space=pl.ANY)
SMEM_SPEC = pl.BlockSpec(memory_space=pltpu.SMEM)


def call(kernel, out_shape, operands, scratch=(), flops=0, transcendentals=0, vmem=16, spec=VMEM_SPEC, out_spec=VMEM_SPEC):
    outs = out_shape if isinstance(out_shape, tuple) else (out_shape,)
    moved = sum(a.size * a.dtype.itemsize for a in operands + outs)
    return pl.pallas_call(
        kernel,
        out_shape=out_shape,
        in_specs=[SMEM_SPEC] + [spec] * (len(operands) - 1),
        out_specs=jax.tree.map(lambda _: out_spec, out_shape),
        scratch_shapes=list(scratch),
        compiler_params=pltpu.CompilerParams(vmem_limit_bytes=vmem * 2**20),
        cost_estimate=pl.CostEstimate(flops=flops, bytes_accessed=moved, transcendentals=transcendentals),
    )(*operands)


def copy_call(kernel, copies, out_shape, operands):
    return call(kernel, out_shape, operands, (pltpu.SemaphoreType.DMA((copies,)),), spec=ANY_SPEC, out_spec=ANY_SPEC)


def shape_of(dtype, *shape):
    return jax.ShapeDtypeStruct(shape, dtype)


def at(start, size):
    return pl.ds(pl.multiple_of(start, size), size)


def copied(sems, pairs):
    copies = [pltpu.make_async_copy(src, dst, sems.at[n]) for n, (src, dst) in enumerate(pairs)]
    for copy in copies:
        copy.start()
    for copy in copies:
        copy.wait()


def steps_of(heads):
    return (0,) + tuple(sorted(range(1, heads), key=lambda k: -min(k, heads - k)))


def onward(place_ref, heads, n):
    return lax.rem(place_ref[2] + steps_of(heads)[n], heads)


def source(place_ref, heads, n):
    return lax.rem(place_ref[2] + heads - steps_of(heads)[n], heads)


def pack_kv_kernel(heads, place_ref, k_ref, v_ref, *refs):
    out_refs, sems = refs[:-1], refs[-1]
    core = place_ref[1]
    d = HEAD_SIZE
    pairs = []
    for k, out_ref in enumerate(out_refs):
        z = onward(place_ref, heads, k)
        for n, g in enumerate((2 * z + core, 2 * z + 1 - core)):
            columns = at(g * d, d)
            pairs.append((k_ref.at[:, columns], out_ref.at[:, pl.ds(2 * n * d, d)]))
            pairs.append((v_ref.at[:, columns], out_ref.at[:, pl.ds((2 * n + 1) * d, d)]))
    copied(sems, pairs)


def pack_qd_kernel(heads, place_ref, q_ref, g_ref, mine_ref, *refs):
    other_refs, sems = refs[:heads], refs[heads]
    core = place_ref[1]
    width = 2 * HEAD_SIZE
    pairs = []
    for k in range(heads):
        for ref, c in ((other_refs[k], 1 - core), (mine_ref.at[k], core)):
            columns = at((2 * onward(place_ref, heads, k) + c) * width, width)
            pairs.append((q_ref.at[:, columns], ref.at[:, pl.ds(0, width)]))
            pairs.append((g_ref.at[:, columns], ref.at[:, pl.ds(width, width)]))
    copied(sems, pairs)


def gather_kv_kernel(heads, place_ref, *refs):
    in_refs, (mine_ref, other_ref) = refs[:heads], refs[heads:]
    width = 2 * HEAD_SIZE
    for k, in_ref in enumerate(in_refs):
        rows = at(source(place_ref, heads, k) * BLOCK, BLOCK)
        mine_ref[rows] = in_ref[:, :width]
        other_ref[rows] = in_ref[:, width:]


def join_kernel(place_ref, mine_ref, sibling_ref, out_ref, kt_ref):
    core = place_ref[1]
    half = mine_ref.shape[0]
    out_ref[at(core * half, half)] = mine_ref[...]
    out_ref[at((1 - core) * half, half)] = sibling_ref[...]
    kt_ref[...] = out_ref[:, :HEAD_SIZE].T


def merge_rows_kernel(heads, place_ref, mine_ref, *refs):
    other_refs, out_refs = refs[:heads], refs[heads + 1 :]
    core = place_ref[1]
    for k, out_ref in enumerate(out_refs):
        out_ref[at(core * BLOCK, BLOCK)] = mine_ref[k]
        out_ref[at((1 - core) * BLOCK, BLOCK)] = other_refs[k][...]


def sort_kernel(heads, place_ref, *refs):
    in_refs, (mine_ref, other_ref) = refs[:heads], refs[heads:]
    core = place_ref[1]
    for k, in_ref in enumerate(in_refs):
        mine_ref[k * BLOCK : (k + 1) * BLOCK] = in_ref[at(core * BLOCK, BLOCK)]
        other_ref[k * BLOCK : (k + 1) * BLOCK] = in_ref[at((1 - core) * BLOCK, BLOCK)]


def unpack_dq_kernel(heads, place_ref, mine_ref, sibling_ref, out_ref, sems):
    core = place_ref[1]
    width = 2 * HEAD_SIZE
    pairs = []
    for k in range(heads):
        z = onward(place_ref, heads, k)
        for ref, c in ((mine_ref, core), (sibling_ref, 1 - core)):
            rows = pl.ds(k * BLOCK, BLOCK)
            pairs.append((ref.at[rows], out_ref.at[:, at((2 * z + c) * width, width)]))
    copied(sems, pairs)


def unpack_kv_kernel(heads, place_ref, mine_ref, sibling_ref, k_ref, v_ref):
    core = place_ref[1]
    d = HEAD_SIZE
    for k in range(heads):
        z = source(place_ref, heads, k)
        rows = slice(k * BLOCK, (k + 1) * BLOCK)
        for ref, c in ((mine_ref, core), (sibling_ref, 1 - core)):
            columns = at((2 * z + c) * d, d)
            k_ref[:, columns] = ref[rows, :d]
            v_ref[:, columns] = ref[rows, d:]


def add_kernel(heads, place_ref, own_a_ref, own_b_ref, back_a_ref, back_b_ref, *out_refs):
    for k, out_ref in enumerate(out_refs):
        rows = at(onward(place_ref, heads, k) * BLOCK, BLOCK)
        for c, (own_ref, back_ref) in enumerate(((own_a_ref, back_a_ref), (own_b_ref, back_b_ref))):
            total = own_ref[rows] + back_ref[rows].astype(jnp.float32)
            out_ref[c * BLOCK : (c + 1) * BLOCK] = total.astype(jnp.bfloat16)


def attention_block(i, count, q, g, own_ref, prev_ref, own_kt_ref, prev_kt_ref, own_grad_ref, prev_grad_ref, bias):
    d = HEAD_SIZE
    low, high = i * BLOCK, (i + 1) * BLOCK
    below, above = i > 0, i < count - 1
    key_row = lax.broadcasted_iota(jnp.int32, (BLOCK, 2 * BLOCK), 0)
    query_row = lax.broadcasted_iota(jnp.int32, (BLOCK, 2 * BLOCK), 1) % BLOCK
    own_seen = key_row <= query_row
    zero = jnp.zeros((BLOCK, 2 * BLOCK), jnp.bfloat16)
    dot_t = lambda a, b: lax.dot_general(a, b, contract_last, preferred_element_type=jnp.float32)
    dot = lambda a, b: jnp.dot(a, b, preferred_element_type=jnp.float32)
    s_own = dot_t(own_ref[:high, :d], q)
    s_prev = dot_t(prev_ref[low:, :d], q) + bias
    p_own = dot_t(own_ref[:high, d:], g)
    p_prev = dot_t(prev_ref[low:, d:], g)
    s_diag = jnp.where(own_seen, s_own[low:], s_prev[:BLOCK])
    p_diag = jnp.where(own_seen, p_own[low:], p_prev[:BLOCK])
    s = jnp.concatenate([s_own[:low]] * below + [s_diag] + [s_prev[BLOCK:]] * above, 0)
    dp = jnp.concatenate([p_own[:low]] * below + [p_diag] + [p_prev[BLOCK:]] * above, 0)
    top = jnp.max(s, axis=0, keepdims=True)
    w = jnp.exp2((s - top) * (score_scale * LOG2_E))
    inverse = 1.0 / jnp.sum(w, axis=0, keepdims=True)
    delta = jnp.sum(w * dp, axis=0, keepdims=True) * inverse
    attention = w * inverse
    ds = (attention * (dp - delta)).astype(jnp.bfloat16)
    low_attention = attention.astype(jnp.bfloat16)
    split = lambda x: (
        jnp.concatenate([x[:low]] * below + [jnp.where(own_seen, x[low:high], zero)], 0),
        jnp.concatenate([jnp.where(own_seen, zero, x[low:high])] + [x[high:]] * above, 0),
    )
    ds_own, ds_prev = split(ds)
    at_own, at_prev = split(low_attention)
    own_grad_ref[:high, d:] += dot(at_own, g)
    prev_grad_ref[low:, d:] += dot(at_prev, g)
    own_grad_ref[:high, :d] += dot(ds_own, q)
    prev_grad_ref[low:, :d] += dot(ds_prev, q)
    dq_t = dot(own_kt_ref[:, :high], ds_own) + dot(prev_kt_ref[:, low:], ds_prev)
    return dq_t * score_scale


def attention_kernel(heads, steps, cores, phase, place_ref, own_ref, own_kt_ref, a_ref, b_ref, *refs):
    d = HEAD_SIZE
    count = 2 * heads
    half = heads * BLOCK
    first, core, head = place_ref[0], place_ref[1], place_ref[2]
    low_rows, high_rows = slice(0, half), slice(half, 2 * half)
    block_refs, refs = refs[: len(steps)], refs[len(steps) :]
    prev_ref, prev_kt_ref = a_ref, b_ref
    if phase == 0:
        prev_ref, prev_kt_ref, own_grad_ref, prev_grad_ref = refs[:4]
        dq_refs, (qd_ref, dq_ref) = refs[4:-2], refs[-2:]
        own_grad_ref[...] = jnp.zeros_like(own_grad_ref)
        prev_grad_ref[...] = jnp.zeros_like(prev_grad_ref)
        prev_ref[at(core * half, half)] = a_ref[...]
        prev_ref[at((1 - core) * half, half)] = b_ref[...]
        prev_kt_ref[...] = prev_ref[:, :d].T
    elif phase == 1:
        own_sums_ref, prev_sums_ref, own_grad_ref, prev_high_ref, back_ref, dq_out_ref = refs[:6]
        qd_ref, dq_ref, prev_grad_ref = refs[6:]
        own_grad_ref[...] = own_sums_ref[low_rows]
        prev_grad_ref[...] = prev_sums_ref[...]
    else:
        own_low_ref, own_sums_ref, prev_high_ref, dq_so_far_ref, after_ref = refs[:5]
        own_a_ref, own_b_ref, back_ref = refs[5:8]
        dq_refs, (qd_ref, dq_ref, own_grad_ref, prev_grad_ref) = refs[8:-4], refs[-4:]
        own_grad_ref[low_rows] = own_low_ref[...]
        own_grad_ref[high_rows] = own_sums_ref[high_rows]
        prev_grad_ref[high_rows] = prev_high_ref[...]
        dq_ref[:, :BLOCK] = dq_so_far_ref[...]
    for n, block_ref in enumerate(block_refs):
        qd_ref[n] = block_ref[: 2 * BLOCK]
    bias = jnp.where(first == 1, masked_value, 0.0).astype(jnp.float32)

    @pl.loop(0, len(steps))
    def _(n):
        step = steps[0] + n * (steps[-1] - steps[0]) // max(len(steps) - 1, 1)
        z_here = lax.rem(head + heads - step, heads)
        for z in range(heads):

            @pl.when(z_here == z)
            def _():
                for c in cores:
                    rows = slice(c * BLOCK, (c + 1) * BLOCK)
                    q = jnp.concatenate([qd_ref[n, rows, :d], qd_ref[n, rows, d : 2 * d]], 0)
                    g = jnp.concatenate([qd_ref[n, rows, 2 * d : 3 * d], qd_ref[n, rows, 3 * d :]], 0)
                    dq_t = attention_block(
                        c * heads + z, count, q, g, own_ref, prev_ref, own_kt_ref, prev_kt_ref,
                        own_grad_ref, prev_grad_ref, bias,
                    )
                    dq_ref[n, rows, :d] = dq_t[:, :BLOCK].T.astype(jnp.bfloat16)
                    dq_ref[n, rows, d:] = dq_t[:, BLOCK:].T.astype(jnp.bfloat16)

    def finish(ref, grad_ref, rows):
        ref[low_rows, :d] = (grad_ref[rows, :d] * score_scale).astype(ref.dtype)
        ref[low_rows, d:] = grad_ref[rows, d:].astype(ref.dtype)

    if phase == 0:
        for n, ref in enumerate(dq_refs):
            ref[...] = dq_ref[n]
    elif phase == 1:
        finish(back_ref, prev_grad_ref, low_rows)
        prev_high_ref[...] = prev_grad_ref[high_rows]
        dq_out_ref[...] = dq_ref[:, :BLOCK]
    else:
        finish(back_ref, prev_grad_ref, high_rows)
        finish(own_a_ref, own_grad_ref, low_rows)
        finish(own_b_ref, own_grad_ref, high_rows)
        for n, ref in enumerate(dq_refs):
            ref[...] = dq_ref[n]


def attention_backward(heads, place, own, near, far, blocks, home):
    half, d = heads * BLOCK, HEAD_SIZE
    whole = 2 * half
    low, wide = jnp.bfloat16, jnp.float32
    sums, half_sums, part = shape_of(wide, whole, 2 * d), shape_of(wide, half, 2 * d), shape_of(low, half, 2 * d)
    block = shape_of(low, 2 * BLOCK, 2 * d)
    early, late = steps_of(heads)[: heads // 2], steps_of(heads)[heads // 2 :]

    def run(steps, cores, phase, outs, operands, scratch):
        scratch = (
            pltpu.VMEM((len(steps), 2 * BLOCK, 4 * d), low),
            pltpu.VMEM((len(steps), 2 * BLOCK, 2 * d), low),
        ) + (pltpu.VMEM((whole, 2 * d), wide),) * scratch
        kernel = functools.partial(attention_kernel, heads, steps, cores, phase)
        return call(kernel, outs, (place,) + tuple(own) + tuple(operands), scratch, 1, 1, 32)

    outs = (shape_of(low, whole, 2 * d), shape_of(low, d, whole), sums, sums) + (block,) * len(early)
    outs = run(early, (0, 1), 0, outs, [near, far] + list(blocks[: len(early)]), 0)
    prev, (own_sums, prev_sums), dq_early = outs[:2], outs[2:4], outs[4:]
    late_blocks = tuple(blocks[len(early) :])
    tied, late_blocks = lax.optimization_barrier((dq_early[1:], late_blocks))
    dq_early = (dq_early[0],) + tuple(home(dq, step) for dq, step in zip(tied, early[1:]))
    wide_part = shape_of(low, half + 16, 2 * d)
    outs = (half_sums, half_sums, wide_part, shape_of(low, len(late), BLOCK, 2 * d))
    own_low, prev_high, back_a, dq_so_far = run(
        late, (0,), 1, outs, prev + late_blocks + (own_sums, prev_sums), 1
    )
    outs = run(
        late,
        (1,),
        2,
        (half_sums, half_sums, part) + (block,) * len(late),
        prev + late_blocks + (own_low, own_sums, prev_high, dq_so_far, dq_early[-1][:16]),
        2,
    )
    dq_late = tuple(home(dq, step) for dq, step in zip(outs[3:], late))
    return outs[:2], (back_a, outs[2]), dq_early + dq_late


def moved(value, chips, heads, chip_step, flip, head_step):
    index = lambda chip, core, head: (chip * 2 + core) * heads + head
    pairs = [
        (index(chip, core, head), index((chip + chip_step) % chips, core ^ flip, (head + head_step) % heads))
        for chip in range(chips)
        for core in range(2)
        for head in range(heads)
    ]
    return lax.ppermute(value, ("chip", "core", "head"), pairs)


def on_device(query_rows, key_rows, saved_value_rows, out_grad):
    chips, heads = lax.axis_size("chip"), lax.axis_size("head")
    send = functools.partial(moved, chips=chips, heads=heads)
    rows, d, low = key_rows.shape[0], HEAD_SIZE, jnp.bfloat16
    bind = lambda kernel: functools.partial(kernel, heads)
    place = jnp.stack(
        [(lax.axis_index("chip") == 0).astype(jnp.int32), lax.axis_index("core"), lax.axis_index("head")]
    ).astype(jnp.int32)

    def ship(value, head_step):
        return send(value, chip_step=0, flip=0, head_step=head_step)

    def spread(parts):
        return (parts[0],) + tuple(ship(parts[n], steps_of(heads)[n]) for n in range(1, heads))

    across = functools.partial(send, head_step=0)
    slab = shape_of(low, rows, 4 * d)
    kvs = spread(
        copy_call(bind(pack_kv_kernel), 4 * heads, (slab,) * heads, (place, key_rows, saved_value_rows))
    )
    qd_mine, *qd_other = copy_call(
        bind(pack_qd_kernel),
        4 * heads,
        (shape_of(low, heads, rows, 4 * d),) + (slab,) * heads,
        (place, query_rows, out_grad),
    )
    qd_other = [across(part, chip_step=0, flip=1) for part in qd_other]
    mine, other = call(bind(gather_kv_kernel), (shape_of(low, heads * rows, 2 * d),) * 2, (place,) + kvs)
    near = across(mine, chip_step=1, flip=0)
    far = across(other, chip_step=1, flip=1)
    blocks = call(
        bind(merge_rows_kernel),
        tuple(shape_of(low, 2 * rows + 16 * (n == 1), 4 * d) for n in range(heads)),
        (place, qd_mine, *qd_other, mine[:8]),
    )
    blocks = spread(blocks)
    sibling = across(other, chip_step=0, flip=1)
    own = call(
        join_kernel,
        (shape_of(low, 2 * heads * rows, 2 * d), shape_of(low, d, 2 * heads * rows)),
        (place, mine, sibling),
    )
    own_sums, partial, dqs = attention_backward(
        heads, place, own, near, far, blocks, lambda dq, step: ship(dq, -step)
    )
    back = [across(part, chip_step=-1, flip=0) for part in partial]
    halves = shape_of(low, heads * rows, 2 * d)
    totals = spread(call(bind(add_kernel), (shape_of(low, 2 * rows, 2 * d),) * heads, (place, *own_sums, *back)))
    kv_mine, kv_other = call(bind(sort_kernel), (halves, halves), (place,) + totals)
    kv_sibling = across(kv_other, chip_step=0, flip=1)
    dq_mine, dq_other = call(
        bind(sort_kernel), (shape_of(low, heads * rows, 2 * d),) * 2, (place,) + tuple(dqs)
    )
    dq_sibling = across(dq_other, chip_step=0, flip=1)
    query_grad = copy_call(
        bind(unpack_dq_kernel), 2 * heads, shape_of(low, *query_rows.shape), (place, dq_mine, dq_sibling)
    )
    key_grad, value_grad = call(
        bind(unpack_kv_kernel), (shape_of(low, *key_rows.shape),) * 2, (place, kv_mine, kv_sibling)
    )
    return query_grad, key_grad, value_grad


def solution(mesh):
    heads = mesh.shape["head"]
    devices = mesh.devices.reshape(-1, 2, heads)
    fine_mesh = Mesh(devices, ("chip", "core", "head"))
    rows = P(("chip", "core", "head"), None)
    return jax.shard_map(
        on_device,
        mesh=fine_mesh,
        in_specs=(rows,) * 4,
        out_specs=(rows,) * 3,
        check_vma=False,
    )
```

```python
import functools

import jax
import jax.numpy as jnp
from jax import lax
from jax.experimental import pallas as pl
from jax.experimental.pallas import tpu as pltpu
from jax.sharding import Mesh
from jax.sharding import PartitionSpec as P

HEAD_SIZE = 128
BLOCK = 128
LOG2_E = 1.4426950408889634

score_scale = 168.0 ** (-0.5)
masked_value = -1e30
contract_last = (((1,), (1,)), ((), ()))
VMEM_SPEC = pl.BlockSpec(memory_space=pltpu.VMEM)
ANY_SPEC = pl.BlockSpec(memory_space=pl.ANY)
SMEM_SPEC = pl.BlockSpec(memory_space=pltpu.SMEM)


def call(kernel, out_shape, operands, scratch=(), flops=0, transcendentals=0, vmem=16, spec=VMEM_SPEC, out_spec=VMEM_SPEC):
    outs = out_shape if isinstance(out_shape, tuple) else (out_shape,)
    moved = sum(a.size * a.dtype.itemsize for a in operands + outs)
    return pl.pallas_call(
        kernel,
        out_shape=out_shape,
        in_specs=[SMEM_SPEC] + [spec] * (len(operands) - 1),
        out_specs=jax.tree.map(lambda _: out_spec, out_shape),
        scratch_shapes=list(scratch),
        compiler_params=pltpu.CompilerParams(vmem_limit_bytes=vmem * 2**20),
        cost_estimate=pl.CostEstimate(flops=flops, bytes_accessed=moved, transcendentals=transcendentals),
    )(*operands)


def copy_call(kernel, copies, out_shape, operands):
    return call(kernel, out_shape, operands, (pltpu.SemaphoreType.DMA((copies,)),), spec=ANY_SPEC, out_spec=ANY_SPEC)


def shape_of(dtype, *shape):
    return jax.ShapeDtypeStruct(shape, dtype)


def at(start, size):
    return pl.ds(pl.multiple_of(start, size), size)


def copied(sems, pairs):
    copies = [pltpu.make_async_copy(src, dst, sems.at[n]) for n, (src, dst) in enumerate(pairs)]
    for copy in copies:
        copy.start()
    for copy in copies:
        copy.wait()


def steps_of(heads):
    return (0,) + tuple(sorted(range(1, heads), key=lambda k: -min(k, heads - k)))


def onward(place_ref, heads, n):
    return lax.rem(place_ref[2] + steps_of(heads)[n], heads)


def source(place_ref, heads, n):
    return lax.rem(place_ref[2] + heads - steps_of(heads)[n], heads)


def pack_kv_kernel(heads, place_ref, k_ref, v_ref, *refs):
    out_refs, sems = refs[:-1], refs[-1]
    core = place_ref[1]
    d = HEAD_SIZE
    pairs = []
    for k, out_ref in enumerate(out_refs):
        z = onward(place_ref, heads, k)
        for n, g in enumerate((2 * z + core, 2 * z + 1 - core)):
            columns = at(g * d, d)
            pairs.append((k_ref.at[:, columns], out_ref.at[:, pl.ds(2 * n * d, d)]))
            pairs.append((v_ref.at[:, columns], out_ref.at[:, pl.ds((2 * n + 1) * d, d)]))
    copied(sems, pairs)


def pack_qd_kernel(heads, place_ref, q_ref, g_ref, mine_ref, *refs):
    other_refs, sems = refs[:heads], refs[heads]
    core = place_ref[1]
    width = 2 * HEAD_SIZE
    pairs = []
    for k in range(heads):
        for ref, c in ((other_refs[k], 1 - core), (mine_ref.at[k], core)):
            columns = at((2 * onward(place_ref, heads, k) + c) * width, width)
            pairs.append((q_ref.at[:, columns], ref.at[:, pl.ds(0, width)]))
            pairs.append((g_ref.at[:, columns], ref.at[:, pl.ds(width, width)]))
    copied(sems, pairs)


def gather_kv_kernel(heads, place_ref, *refs):
    in_refs, (mine_ref, other_ref) = refs[:heads], refs[heads:]
    width = 2 * HEAD_SIZE
    for k, in_ref in enumerate(in_refs):
        rows = at(source(place_ref, heads, k) * BLOCK, BLOCK)
        mine_ref[rows] = in_ref[:, :width]
        other_ref[rows] = in_ref[:, width:]


def join_kernel(place_ref, mine_ref, sibling_ref, out_ref, kt_ref):
    core = place_ref[1]
    half = mine_ref.shape[0]
    out_ref[at(core * half, half)] = mine_ref[...]
    out_ref[at((1 - core) * half, half)] = sibling_ref[...]
    kt_ref[...] = out_ref[:, :HEAD_SIZE].T


def merge_rows_kernel(heads, place_ref, mine_ref, *refs):
    other_refs, out_refs = refs[:heads], refs[heads + 1 :]
    core = place_ref[1]
    for k, out_ref in enumerate(out_refs):
        out_ref[at(core * BLOCK, BLOCK)] = mine_ref[k]
        out_ref[at((1 - core) * BLOCK, BLOCK)] = other_refs[k][...]


def sort_kernel(heads, place_ref, *refs):
    in_refs, (after_ref, mine_ref, other_ref) = refs[:heads], refs[heads:]
    core = place_ref[1]
    for k, in_ref in enumerate(in_refs):
        mine_ref[k * BLOCK : (k + 1) * BLOCK] = in_ref[at(core * BLOCK, BLOCK)]
        other_ref[k * BLOCK : (k + 1) * BLOCK] = in_ref[at((1 - core) * BLOCK, BLOCK)]


def unpack_dq_kernel(heads, place_ref, mine_ref, sibling_ref, out_ref, sems):
    core = place_ref[1]
    width = 2 * HEAD_SIZE
    pairs = []
    for k in range(heads):
        z = onward(place_ref, heads, k)
        for ref, c in ((mine_ref, core), (sibling_ref, 1 - core)):
            rows = pl.ds(k * BLOCK, BLOCK)
            pairs.append((ref.at[rows], out_ref.at[:, at((2 * z + c) * width, width)]))
    copied(sems, pairs)


def unpack_kv_kernel(heads, place_ref, mine_ref, sibling_ref, k_ref, v_ref):
    core = place_ref[1]
    d = HEAD_SIZE
    for k in range(heads):
        z = source(place_ref, heads, k)
        rows = slice(k * BLOCK, (k + 1) * BLOCK)
        for ref, c in ((mine_ref, core), (sibling_ref, 1 - core)):
            columns = at((2 * z + c) * d, d)
            k_ref[:, columns] = ref[rows, :d]
            v_ref[:, columns] = ref[rows, d:]


def add_kernel(heads, place_ref, own_a_ref, own_b_ref, back_a_ref, back_b_ref, *out_refs):
    for k, out_ref in enumerate(out_refs):
        rows = at(onward(place_ref, heads, k) * BLOCK, BLOCK)
        for c, (own_ref, back_ref) in enumerate(((own_a_ref, back_a_ref), (own_b_ref, back_b_ref))):
            total = own_ref[rows] + back_ref[rows].astype(jnp.float32)
            out_ref[c * BLOCK : (c + 1) * BLOCK] = total.astype(jnp.bfloat16)


def attention_block(i, count, q, g, own_ref, prev_ref, own_kt_ref, prev_kt_ref, own_grad_ref, prev_grad_ref, bias):
    d = HEAD_SIZE
    low, high = i * BLOCK, (i + 1) * BLOCK
    below, above = i > 0, i < count - 1
    key_row = lax.broadcasted_iota(jnp.int32, (BLOCK, 2 * BLOCK), 0)
    query_row = lax.broadcasted_iota(jnp.int32, (BLOCK, 2 * BLOCK), 1) % BLOCK
    own_seen = key_row <= query_row
    zero = jnp.zeros((BLOCK, 2 * BLOCK), jnp.bfloat16)
    dot_t = lambda a, b: lax.dot_general(a, b, contract_last, preferred_element_type=jnp.float32)
    dot = lambda a, b: jnp.dot(a, b, preferred_element_type=jnp.float32)
    s_own = dot_t(own_ref[:high, :d], q)
    s_prev = dot_t(prev_ref[low:, :d], q) + bias
    p_own = dot_t(own_ref[:high, d:], g)
    p_prev = dot_t(prev_ref[low:, d:], g)
    s_diag = jnp.where(own_seen, s_own[low:], s_prev[:BLOCK])
    p_diag = jnp.where(own_seen, p_own[low:], p_prev[:BLOCK])
    s = jnp.concatenate([s_own[:low]] * below + [s_diag] + [s_prev[BLOCK:]] * above, 0)
    dp = jnp.concatenate([p_own[:low]] * below + [p_diag] + [p_prev[BLOCK:]] * above, 0)
    top = jnp.max(s, axis=0, keepdims=True)
    w = jnp.exp2((s - top) * (score_scale * LOG2_E))
    inverse = 1.0 / jnp.sum(w, axis=0, keepdims=True)
    delta = jnp.sum(w * dp, axis=0, keepdims=True) * inverse
    attention = w * inverse
    ds = (attention * (dp - delta)).astype(jnp.bfloat16)
    low_attention = attention.astype(jnp.bfloat16)
    split = lambda x: (
        jnp.concatenate([x[:low]] * below + [jnp.where(own_seen, x[low:high], zero)], 0),
        jnp.concatenate([jnp.where(own_seen, zero, x[low:high])] + [x[high:]] * above, 0),
    )
    ds_own, ds_prev = split(ds)
    at_own, at_prev = split(low_attention)
    own_grad_ref[:high, d:] += dot(at_own, g)
    prev_grad_ref[low:, d:] += dot(at_prev, g)
    own_grad_ref[:high, :d] += dot(ds_own, q)
    prev_grad_ref[low:, :d] += dot(ds_prev, q)
    dq_t = dot(own_kt_ref[:, :high], ds_own) + dot(prev_kt_ref[:, low:], ds_prev)
    return dq_t * score_scale


def attention_kernel(heads, steps, cores, phase, place_ref, own_ref, own_kt_ref, a_ref, b_ref, *refs):
    d = HEAD_SIZE
    count = 2 * heads
    half = heads * BLOCK
    first, core, head = place_ref[0], place_ref[1], place_ref[2]
    low_rows, high_rows = slice(0, half), slice(half, 2 * half)
    block_refs, refs = refs[: len(steps)], refs[len(steps) :]
    prev_ref, prev_kt_ref = a_ref, b_ref
    if phase == 0:
        prev_ref, prev_kt_ref, own_grad_ref, prev_grad_ref = refs[:4]
        dq_refs, (qd_ref, dq_ref) = refs[4:-2], refs[-2:]
        own_grad_ref[...] = jnp.zeros_like(own_grad_ref)
        prev_grad_ref[...] = jnp.zeros_like(prev_grad_ref)
        prev_ref[at(core * half, half)] = a_ref[...]
        prev_ref[at((1 - core) * half, half)] = b_ref[...]
        prev_kt_ref[...] = prev_ref[:, :d].T
    elif phase == 1:
        own_sums_ref, prev_sums_ref, own_grad_ref, prev_high_ref, back_ref, dq_out_ref = refs[:6]
        qd_ref, dq_ref, prev_grad_ref = refs[6:]
        own_grad_ref[...] = own_sums_ref[low_rows]
        prev_grad_ref[...] = prev_sums_ref[...]
    else:
        own_low_ref, own_sums_ref, prev_high_ref, dq_so_far_ref, after_ref = refs[:5]
        own_a_ref, own_b_ref, back_ref = refs[5:8]
        dq_refs, (qd_ref, dq_ref, own_grad_ref, prev_grad_ref) = refs[8:-4], refs[-4:]
        own_grad_ref[low_rows] = own_low_ref[...]
        own_grad_ref[high_rows] = own_sums_ref[high_rows]
        prev_grad_ref[high_rows] = prev_high_ref[...]
        dq_ref[:, :BLOCK] = dq_so_far_ref[...]
    for n, block_ref in enumerate(block_refs):
        qd_ref[n] = block_ref[: 2 * BLOCK]
    bias = jnp.where(first == 1, masked_value, 0.0).astype(jnp.float32)

    @pl.loop(0, len(steps))
    def _(n):
        step = steps[0] + n * (steps[-1] - steps[0]) // max(len(steps) - 1, 1)
        z_here = lax.rem(head + heads - step, heads)
        for z in range(heads):

            @pl.when(z_here == z)
            def _():
                for c in cores:
                    rows = slice(c * BLOCK, (c + 1) * BLOCK)
                    q = jnp.concatenate([qd_ref[n, rows, :d], qd_ref[n, rows, d : 2 * d]], 0)
                    g = jnp.concatenate([qd_ref[n, rows, 2 * d : 3 * d], qd_ref[n, rows, 3 * d :]], 0)
                    dq_t = attention_block(
                        c * heads + z, count, q, g, own_ref, prev_ref, own_kt_ref, prev_kt_ref,
                        own_grad_ref, prev_grad_ref, bias,
                    )
                    dq_ref[n, rows, :d] = dq_t[:, :BLOCK].T.astype(jnp.bfloat16)
                    dq_ref[n, rows, d:] = dq_t[:, BLOCK:].T.astype(jnp.bfloat16)

    def finish(ref, grad_ref, rows):
        ref[low_rows, :d] = (grad_ref[rows, :d] * score_scale).astype(ref.dtype)
        ref[low_rows, d:] = grad_ref[rows, d:].astype(ref.dtype)

    if phase == 0:
        for n, ref in enumerate(dq_refs):
            ref[...] = dq_ref[n]
    elif phase == 1:
        finish(back_ref, prev_grad_ref, low_rows)
        prev_high_ref[...] = prev_grad_ref[high_rows]
        dq_out_ref[...] = dq_ref[:, :BLOCK]
    else:
        finish(back_ref, prev_grad_ref, high_rows)
        finish(own_a_ref, own_grad_ref, low_rows)
        finish(own_b_ref, own_grad_ref, high_rows)
        for n, ref in enumerate(dq_refs):
            ref[...] = dq_ref[n]


def attention_backward(heads, place, own, near, far, blocks, home):
    half, d = heads * BLOCK, HEAD_SIZE
    whole = 2 * half
    low, wide = jnp.bfloat16, jnp.float32
    sums, half_sums, part = shape_of(wide, whole, 2 * d), shape_of(wide, half, 2 * d), shape_of(low, half, 2 * d)
    block = shape_of(low, 2 * BLOCK, 2 * d)
    early, late = steps_of(heads)[: heads // 2], steps_of(heads)[heads // 2 :]

    def run(steps, cores, phase, outs, operands, scratch):
        scratch = (
            pltpu.VMEM((len(steps), 2 * BLOCK, 4 * d), low),
            pltpu.VMEM((len(steps), 2 * BLOCK, 2 * d), low),
        ) + (pltpu.VMEM((whole, 2 * d), wide),) * scratch
        kernel = functools.partial(attention_kernel, heads, steps, cores, phase)
        return call(kernel, outs, (place,) + tuple(own) + tuple(operands), scratch, 1, 1, 32)

    outs = (shape_of(low, whole, 2 * d), shape_of(low, d, whole), sums, sums) + (block,) * len(early)
    outs = run(early, (0, 1), 0, outs, [near, far] + list(blocks[: len(early)]), 0)
    prev, (own_sums, prev_sums), dq_early = outs[:2], outs[2:4], outs[4:]
    dq_early = (dq_early[0],) + tuple(home(dq_early[n], early[n]) for n in range(1, len(early)))
    late_blocks = tuple(blocks[len(early) :])
    wide_part = shape_of(low, half + 32, 2 * d)
    outs = (half_sums, half_sums, wide_part, shape_of(low, len(late), BLOCK, 2 * d))
    own_low, prev_high, back_a, dq_so_far = run(
        late, (0,), 1, outs, prev + late_blocks + (own_sums, prev_sums), 1
    )
    outs = run(
        late,
        (1,),
        2,
        (half_sums, half_sums, shape_of(low, half + 16, 2 * d)) + (block,) * len(late),
        prev + late_blocks + (own_low, own_sums, prev_high, dq_so_far, dq_early[-1][:16]),
        2,
    )
    dq_late = tuple(home(dq, step) for dq, step in zip(outs[3:], late))
    return outs[:2], (back_a, outs[2]), dq_early + dq_late


def moved(value, chips, heads, chip_step, flip, head_step):
    index = lambda chip, core, head: (chip * 2 + core) * heads + head
    pairs = [
        (index(chip, core, head), index((chip + chip_step) % chips, core ^ flip, (head + head_step) % heads))
        for chip in range(chips)
        for core in range(2)
        for head in range(heads)
    ]
    return lax.ppermute(value, ("chip", "core", "head"), pairs)


def on_device(query_rows, key_rows, saved_value_rows, out_grad):
    chips, heads = lax.axis_size("chip"), lax.axis_size("head")
    send = functools.partial(moved, chips=chips, heads=heads)
    rows, d, low = key_rows.shape[0], HEAD_SIZE, jnp.bfloat16
    bind = lambda kernel: functools.partial(kernel, heads)
    place = jnp.stack(
        [(lax.axis_index("chip") == 0).astype(jnp.int32), lax.axis_index("core"), lax.axis_index("head")]
    ).astype(jnp.int32)

    def ship(value, head_step):
        return send(value, chip_step=0, flip=0, head_step=head_step)

    def spread(parts):
        return (parts[0],) + tuple(ship(parts[n], steps_of(heads)[n]) for n in range(1, heads))

    across = functools.partial(send, head_step=0)
    slab = shape_of(low, rows, 4 * d)
    kvs = spread(
        copy_call(bind(pack_kv_kernel), 4 * heads, (slab,) * heads, (place, key_rows, saved_value_rows))
    )
    qd_mine, *qd_other = copy_call(
        bind(pack_qd_kernel),
        4 * heads,
        (shape_of(low, heads, rows, 4 * d),) + (slab,) * heads,
        (place, query_rows, out_grad),
    )
    qd_other = [across(part, chip_step=0, flip=1) for part in qd_other]
    mine, other = call(bind(gather_kv_kernel), (shape_of(low, heads * rows, 2 * d),) * 2, (place,) + kvs)
    near = across(mine, chip_step=1, flip=0)
    far = across(other, chip_step=1, flip=1)
    blocks = call(
        bind(merge_rows_kernel),
        tuple(shape_of(low, 2 * rows + 16 * (n == 1), 4 * d) for n in range(heads)),
        (place, qd_mine, *qd_other, mine[:8]),
    )
    blocks = spread(blocks)
    sibling = across(other, chip_step=0, flip=1)
    own = call(
        join_kernel,
        (shape_of(low, 2 * heads * rows, 2 * d), shape_of(low, d, 2 * heads * rows)),
        (place, mine, sibling),
    )
    own_sums, partial, dqs = attention_backward(
        heads, place, own, near, far, blocks, lambda dq, step: ship(dq, -step)
    )
    back = [across(part, chip_step=-1, flip=0) for part in partial]
    halves = shape_of(low, heads * rows, 2 * d)
    totals = spread(call(bind(add_kernel), (shape_of(low, 2 * rows, 2 * d),) * heads, (place, *own_sums, *back)))
    dq_mine, dq_other = call(
        bind(sort_kernel), (halves, halves), (place,) + tuple(dqs) + (near[:16, :d],)
    )
    dq_sibling = across(dq_other, chip_step=0, flip=1)
    query_grad = copy_call(
        bind(unpack_dq_kernel), 2 * heads, shape_of(low, *query_rows.shape), (place, dq_mine, dq_sibling)
    )
    kv_mine, kv_other = call(bind(sort_kernel), (halves, halves), (place,) + totals + (query_grad[:16, :d],))
    kv_sibling = across(kv_other, chip_step=0, flip=1)
    key_grad, value_grad = call(
        bind(unpack_kv_kernel), (shape_of(low, *key_rows.shape),) * 2, (place, kv_mine, kv_sibling)
    )
    return query_grad, key_grad, value_grad


def solution(mesh):
    heads = mesh.shape["head"]
    devices = mesh.devices.reshape(-1, 2, heads)
    fine_mesh = Mesh(devices, ("chip", "core", "head"))
    rows = P(("chip", "core", "head"), None)
    return jax.shard_map(
        on_device,
        mesh=fine_mesh,
        in_specs=(rows,) * 4,
        out_specs=(rows,) * 3,
        check_vma=False,
    )
```
